32 devices in a mesh: expert: 4 (over y, x), context: 4 (over z), dp: 2 (over core).
Axes of the slice: x: 2, y: 2, z: 4, core: 2. Of those that a mesh axis runs over, the one named last changes fastest.
Arguments:
- layer_input: bfloat16 [8, 1024, 1536], P(('expert', 'dp'), 'context'), may hold values from -6 to 6
- cotangent: bfloat16 [8, 1024, 1536], P(('expert', 'dp'), 'context'), may hold values from -6 to 6
- block_order: int32 [8, 8], P(('expert', 'dp')), may hold values from 0 to 7, each once within a row
- routes: int32 [8, 1024, 8], P(('expert', 'dp'), 'context'), may hold values from 0 to 19, all different within a row; in each aligned block of 256 rows (0 to 255, 256 to 511, ..., all dimensions but the last counted through in order) at most 200 rows name the same one
- route_gates: float32 [8, 1024, 8], P(('expert', 'dp'), 'context'), may hold values from 0.06 to 0.25
- joined_weight: float32 [1536, 2560], P(('expert', 'context', 'dp')), may hold values from -0.15625 to 0.15625
- joined_first: float32 [1536, 2560], P(('expert', 'context', 'dp')), may hold values from -128 to 128
- joined_second: float32 [1536, 2560], P(('expert', 'context', 'dp')), may hold values from 1720.32 to 6881.28
- output_weight: float32 [1536, 1536], P(None, ('expert', 'context', 'dp')), may hold values from -1.25 to 1.25
- output_first: float32 [1536, 1536], P(None, ('expert', 'context', 'dp')), may hold values from -16 to 16
- output_second: float32 [1536, 1536], P(None, ('expert', 'context', 'dp')), may hold values from 38.5024 to 155.648
- norm_gains: float32 [2, 1536], P(None, ('expert', 'context', 'dp')), may hold values from 0.5 to 1.5
- gains_first: float32 [2, 1536], P(None, ('expert', 'context', 'dp')), may hold values from -128 to 128
- gains_second: float32 [2, 1536], P(None, ('expert', 'context', 'dp')), may hold values from 1720.32 to 6881.28
- expand_weight: float32 [20, 1536, 1024], P('expert', ('context', 'dp')), may hold values from -0.15625 to 0.15625
- expand_first: float32 [20, 1536, 1024], P('expert', ('context', 'dp')), may hold values from -28 to 28
- expand_second: float32 [20, 1536, 1024], P('expert', ('context', 'dp')), may hold values from 84.5208 to 337.428
- contract_weight: float32 [20, 512, 1536], P('expert', None, ('context', 'dp')), may hold values from -1 to 1
- contract_first: float32 [20, 512, 1536], P('expert', None, ('context', 'dp')), may hold values from -6 to 6
- contract_second: float32 [20, 512, 1536], P('expert', None, ('context', 'dp')), may hold values from 1.104012 to 4.4226
Outputs:
- output: bfloat16 [8, 1024, 1536], P(('expert', 'dp'), 'context')
- grad_input: bfloat16 [8, 1024, 1536], P(('expert', 'dp'), 'context')
- joined_new: float32 [1536, 2560], P(('expert', 'context', 'dp'))
- joined_first_new: float32 [1536, 2560], P(('expert', 'context', 'dp'))
- joined_second_new: float32 [1536, 2560], P(('expert', 'context', 'dp'))
- output_new: float32 [1536, 1536], P(None, ('expert', 'context', 'dp'))
- output_first_new: float32 [1536, 1536], P(None, ('expert', 'context', 'dp'))
- output_second_new: float32 [1536, 1536], P(None, ('expert', 'context', 'dp'))
- gains_new: float32 [2, 1536], P(None, ('expert', 'context', 'dp'))
- gains_first_new: float32 [2, 1536], P(None, ('expert', 'context', 'dp'))
- gains_second_new: float32 [2, 1536], P(None, ('expert', 'context', 'dp'))
- expand_new: float32 [20, 1536, 1024], P('expert', ('context', 'dp'))
- expand_first_new: float32 [20, 1536, 1024], P('expert', ('context', 'dp'))
- expand_second_new: float32 [20, 1536, 1024], P('expert', ('context', 'dp'))
- contract_new: float32 [20, 512, 1536], P('expert', None, ('context', 'dp'))
- contract_first_new: float32 [20, 512, 1536], P('expert', None, ('context', 'dp'))
- contract_second_new: float32 [20, 512, 1536], P('expert', None, ('context', 'dp'))
The draws below stay inside these ranges and needn't reach their ends.
Inputs may be any that keep to these rules, and one draw needn't show every extreme that they name: `routes`: each row names 8 different experts. Within the rows of one device (aligned blocks of 256 tokens) no expert is named more than 200 times, and in every draw some expert is named exactly 200 times by the rows of some device. Each row is a permutation; stored block j of a sequence (its rows j * 128 to j * 128 + 127) holds positions block_order[s, j] * 128 onward in order.
All inputs are finite; a program needn't handle non-finite values.
Results may differ from the reference program's by a relative error of at most 0.024.
Values may be sent and summed in bfloat16 or wider, within the bound.
No kernel may reach another device: no remote copies, remote signals or barrier semaphores. Data moves between devices by JAX's collectives and lax.ppermute only.
A program may use at most 384 MiB of HBM per device.

```python
import math
import jax
import jax.numpy as jnp
import numpy as np
from jax import lax

D = 1536
HEADS = 24
KV_HEADS = 8
HEAD_DIM = 64
FF = 512
TOP = 8
TOK_DEV = 256
STEP = 10
EXPERTS = 20
CAP = 200
SEQS = 8
SEQ_LEN = 1024
TOKENS = 8192
HALF = 128
BLOCKS = 8
QDIM = 1536
KVDIM = 512
QKV = 2560
EXPERT_ROWS = 3276


def level_of(rng, dims, split, least, top_value):
    def one(axis_at, shards_of):
        heights = jax.random.uniform(jax.random.fold_in(jax.random.fold_in(rng, 6), axis_at), (shards_of,), jnp.float32, least / len(split), top_value / len(split))
        return jnp.repeat(jnp.exp(heights), dims[axis_at] // shards_of).reshape((-1,) + (1,) * (len(dims) - axis_at - 1))

    loudness = one(*split[0])
    for cut in split[1:]:
        loudness = loudness * one(*cut)
    return loudness


def routed_block(rng, own, number, rows, count, top, limit, skew):
    sequence = jax.random.permutation(rng, count)
    crowded, common = load_shares(count, rows * top, limit, skew, True), load_shares(count, rows * top, limit, skew, False)
    places = jnp.arange(count)

    def named(sizes, offset_by):
        used = int((sizes > 0).sum())
        fixed = max(1, used // 4)
        moved = fixed + (places - fixed + offset_by * (used - fixed)) % max(1, count - fixed)
        return jnp.zeros((count,), jnp.int32).at[sequence[jnp.where(places < fixed, places, moved)]].set(jnp.asarray(sizes, jnp.int32))

    sizes = jnp.where(number % 4 == 0, named(crowded, number // 4), named(common, number - number // 4 - 1))
    mixed = jax.random.permutation(jax.random.fold_in(own, 3), count)
    donor, taker = mixed[0:count // 2 * 2:2], mixed[1:count // 2 * 2:2]
    room = jnp.minimum(sizes[donor] - 1, limit - sizes[taker]) // 2
    room = jnp.where((donor == sequence[0]) | (taker == sequence[0]) | (sizes[taker] == 0), 0, jnp.maximum(room, 0))
    moved = jax.random.randint(jax.random.fold_in(own, 4), (count // 2,), 0, 1 << 20) % (room + 1)
    sizes = sizes.at[donor].add(-moved).at[taker].add(moved)
    members = jnp.searchsorted(jnp.cumsum(sizes), jnp.arange(rows * top), side="right").astype(jnp.int32)
    table = members.reshape(top, rows).T
    table = table[jax.random.permutation(jax.random.fold_in(own, 1), rows)]
    offset_by = jax.random.randint(jax.random.fold_in(own, 2), (rows, 1), 0, top)
    return jnp.take_along_axis(table, (jnp.arange(top)[None, :] + offset_by) % top, axis=1)


def load_shares(amount, total, reach, skew, full):
    weights = [(1 << 20) // math.isqrt(rank ** skew) + 1 for rank in range(1, amount + 1)]
    largest = reach if full else min(reach, max(-(-total // amount), total * weights[0] // sum(weights)))
    least = 1 if total - largest >= amount - 1 else 0
    holding, surplus = [largest] + [least] * (amount - 1), total - largest - least * (amount - 1)
    while surplus > 0:
        movable = [i for i in range(1, amount) if holding[i] < largest] or [i for i in range(1, amount) if holding[i] < reach]
        pool, remaining = sum([weights[i] for i in movable]), surplus
        for i in movable:
            extra = min(reach - holding[i], max(1, remaining * weights[i] // pool), surplus)
            holding[i] = holding[i] + extra
            surplus = surplus - extra
    return np.array(holding)


def normal_values(key, shape, deviation, limit, shards=(), held_as=jnp.bfloat16):
    values = jax.random.normal(key, shape, jnp.float32) * deviation
    if len(shards) > 0:
        values = level_of(key, shape, shards, -0.22, 0.18) * values
    return jnp.clip(values, min=-limit, max=limit).astype(held_as)


def setup_inputs(seed: int = 0) -> dict:
    streams_of = jax.random.split(jax.random.key(seed), 21)
    layer_input = normal_values(streams_of[0], (SEQS, SEQ_LEN, D), 1.0, 6.0, ((0, 8), (1, 4)))
    cotangent = normal_values(streams_of[1], (SEQS, SEQ_LEN, D), 1.0, 6.0, ((0, 8), (1, 4)))
    block_order = jax.vmap(lambda own: jax.random.permutation(own, BLOCKS))(jax.random.split(streams_of[2], SEQS)).reshape((SEQS, BLOCKS)).astype(jnp.int32)
    routes_keys = jax.random.split(jax.random.fold_in(streams_of[3], 1), SEQS * SEQ_LEN // TOK_DEV)
    routes_turns = jax.random.permutation(jax.random.fold_in(streams_of[3], 3), SEQS * SEQ_LEN // TOK_DEV)
    routes = jax.vmap(lambda own, number: routed_block(jax.random.fold_in(streams_of[3], 2), own, number, TOK_DEV, EXPERTS, TOP, CAP, 2))(routes_keys, routes_turns).reshape((SEQS, SEQ_LEN, TOP))
    route_gates = jnp.clip(jnp.exp(math.log(0.25) - 1.4271164 * jax.random.uniform(streams_of[4], (SEQS, SEQ_LEN, TOP), jnp.float32) ** level_of(streams_of[4], (SEQS, SEQ_LEN, TOP), ((0, 8), (1, 4)), -0.2, 0.2)), 0.06, 0.25)
    joined_weight = normal_values(streams_of[5], (D, QKV), D ** -0.5, 0.15625, ((0, 32),), jnp.float32)
    joined_first = normal_values(streams_of[6], (D, QKV), (0.22 * TOKENS ** 0.5), 128.0, ((0, 32),), jnp.float32)
    joined_second = jnp.clip(jnp.exp(math.log(6881.28) - 1.3862944 * jax.random.uniform(streams_of[7], (D, QKV), jnp.float32) ** level_of(streams_of[7], (D, QKV), ((0, 32),), -0.2, 0.2)), 1720.32, 6881.28)
    output_weight = normal_values(streams_of[8], (QDIM, D), (QDIM // 64) ** -0.5, 1.25, ((1, 32),), jnp.float32)
    output_first = normal_values(streams_of[9], (QDIM, D), (0.033 * TOKENS ** 0.5), 16.0, ((1, 32),), jnp.float32)
    output_second = jnp.clip(jnp.exp(math.log(155.648) - 1.3968765 * jax.random.uniform(streams_of[10], (QDIM, D), jnp.float32) ** level_of(streams_of[10], (QDIM, D), ((1, 32),), -0.2, 0.2)), 38.5024, 155.648)
    norm_gains = jnp.clip(1.0 + 0.1 * jax.random.normal(streams_of[11], (2, D), jnp.float32), 0.5, 1.5)
    gains_first = normal_values(streams_of[12], (2, D), (0.22 * TOKENS ** 0.5), 128.0, ((1, 32),), jnp.float32)
    gains_second = jnp.clip(jnp.exp(math.log(6881.28) - 1.3862944 * jax.random.uniform(streams_of[13], (2, D), jnp.float32) ** level_of(streams_of[13], (2, D), ((1, 32),), -0.2, 0.2)), 1720.32, 6881.28)
    expand_weight = normal_values(streams_of[14], (EXPERTS, D, 2 * FF), D ** -0.5, 0.15625, ((0, 4), (1, 8)), jnp.float32)
    expand_first = normal_values(streams_of[15], (EXPERTS, D, 2 * FF), (0.078 * EXPERT_ROWS ** 0.5), 28.0, ((0, 4), (1, 8)), jnp.float32)
    expand_second = jnp.clip(jnp.exp(math.log(337.428) - 1.38435455 * jax.random.uniform(streams_of[16], (EXPERTS, D, 2 * FF), jnp.float32) ** level_of(streams_of[16], (EXPERTS, D, 2 * FF), ((0, 4), (1, 8)), -0.2, 0.2)), 84.5208, 337.428)
    contract_weight = normal_values(streams_of[17], (EXPERTS, FF, D), (FF // 16) ** -0.5, 1.0, ((0, 4), (2, 8)), jnp.float32)
    contract_first = normal_values(streams_of[18], (EXPERTS, FF, D), (0.0089 * EXPERT_ROWS ** 0.5), 6.0, ((0, 4), (2, 8)), jnp.float32)
    contract_second = jnp.clip(jnp.exp(math.log(4.4226) - 1.3877769 * jax.random.uniform(streams_of[19], (EXPERTS, FF, D), jnp.float32) ** level_of(streams_of[19], (EXPERTS, FF, D), ((0, 4), (2, 8)), -0.2, 0.2)), 1.104012, 4.4226)
    return {"layer_input": layer_input, "cotangent": cotangent, "block_order": block_order, "routes": routes, "route_gates": route_gates, "joined_weight": joined_weight, "joined_first": joined_first, "joined_second": joined_second, "output_weight": output_weight, "output_first": output_first, "output_second": output_second, "norm_gains": norm_gains, "gains_first": gains_first, "gains_second": gains_second, "expand_weight": expand_weight, "expand_first": expand_first, "expand_second": expand_second, "contract_weight": contract_weight, "contract_first": contract_first, "contract_second": contract_second}


norm_eps = 1e-06
beta_one = 0.9
beta_two = 0.95
adam_eps = 1e-08
decay_rate = 0.1
rate_joined = 0.08
rate_output = 0.6
rate_gains = 0.6
rate_expand = 0.08
rate_contract = 0.5
masked_score = -1e+30
highest = lax.Precision.HIGHEST

@jax.custom_vjp
def low(v):
    return lax.optimization_barrier(v.astype(jnp.bfloat16)).astype(jnp.float32)

@jax.custom_vjp
def low_back(v):
    return v

def low_keep(v):
    return (low(v), None)

def low_pass(kept, grad):
    return (grad,)

def back_keep(v):
    return (v, None)

def back_low(kept, grad):
    return (low(grad),)
low.defvjp(low_keep, low_pass)
low_back.defvjp(back_keep, back_low)

def slot_tables(route_row, experts, capacity):
    count = route_row.shape[0]
    hits = (route_row[:, None] == jnp.arange(experts, dtype=jnp.int32)[None, :]).astype(jnp.int32)
    before = (jnp.cumsum(hits, axis=0) - hits).astype(jnp.int32)
    slot = lax.optimization_barrier(jnp.sum(before * hits, axis=1)).astype(jnp.int32)
    dest = (route_row * capacity + slot).astype(jnp.int32)
    slot_row = jnp.full((experts * capacity,), count, jnp.int32).at[dest].set(jnp.arange(count, dtype=jnp.int32))
    return (dest, slot_row)

def angles(places):
    half = HEAD_DIM // 2
    steps = jnp.arange(half, dtype=jnp.float32) * (2.0 / HEAD_DIM)
    freq = jnp.exp(steps * -math.log(10000.0))
    turn = places.astype(jnp.float32)[:, None] * freq[None, :]
    return (jnp.cos(turn)[:, None, :], jnp.sin(turn)[:, None, :])

def rotate(vals, places, heads):
    cosine, sine = angles(places)
    parts = vals.reshape(vals.shape[0], heads, HEAD_DIM)
    first = parts[..., :HEAD_DIM // 2]
    second = parts[..., HEAD_DIM // 2:]
    turned = jnp.concatenate([first * cosine - second * sine, second * cosine + first * sine], axis=-1)
    return turned.reshape(vals.shape)

def adamw(weight, first, second, grad, rate, decay):
    first_new = beta_one * first + (1.0 - beta_one) * grad
    second_new = beta_two * second + (1.0 - beta_two) * grad * grad
    first_hat = first_new / (1.0 - beta_one ** STEP)
    second_hat = second_new / (1.0 - beta_two ** STEP)
    weight_new = weight - rate * (first_hat / (jnp.sqrt(second_hat) + adam_eps) + decay * weight)
    return (weight_new, first_new, second_new)

def reference(layer_input, cotangent, block_order, routes, route_gates, joined_weight, joined_first, joined_second, output_weight, output_first, output_second, norm_gains, gains_first, gains_second, expand_weight, expand_first, expand_second, contract_weight, contract_first, contract_second):
    groups = HEADS // KV_HEADS
    attn_scale = HEAD_DIM ** (-0.5)
    query_block = math.gcd(SEQ_LEN, 512)
    offsets = jnp.arange(HALF, dtype=jnp.int32)
    places = (block_order[:, :, None] * HALF + offsets[None, None, :]).reshape(SEQS, SEQ_LEN).astype(jnp.int32)
    flat_places = places.reshape(-1)
    route_rows = routes.reshape(-1, TOK_DEV * TOP)
    gate_rows = route_gates.reshape(-1, TOK_DEV * TOP)

    def attention(queries, keys, values):

        def one_sequence(pack):
            seq_queries, seq_keys, seq_values, seq_places = pack
            key_heads = seq_keys.reshape(SEQ_LEN, KV_HEADS, HEAD_DIM)
            value_heads = seq_values.reshape(SEQ_LEN, KV_HEADS, HEAD_DIM)

            def one_block(inner):
                block_queries, block_places = inner
                scores = low_back(jnp.einsum('qhgd,khd->hgqk', block_queries, key_heads, precision=highest) * attn_scale)
                allowed = seq_places[None, :] <= block_places[:, None]
                scores = jnp.where(allowed[None, None], scores, masked_score)
                probs = low(jax.nn.softmax(scores, axis=-1))
                return jnp.einsum('hgqk,khd->qhgd', probs, value_heads, precision=highest)
            blocks = (seq_queries.reshape(-1, query_block, KV_HEADS, groups, HEAD_DIM), seq_places.reshape(-1, query_block))
            return lax.map(jax.checkpoint(one_block), blocks).reshape(SEQ_LEN, QDIM)
        packs = (queries.reshape(SEQS, SEQ_LEN, QDIM), keys.reshape(SEQS, SEQ_LEN, KVDIM), values.reshape(SEQS, SEQ_LEN, KVDIM), places)
        return lax.map(one_sequence, packs).reshape(-1, QDIM)

    def forward(inputs, weight_joined, weight_output, gain_pair, weight_expand, weight_contract):
        flat = inputs.reshape(-1, D)
        gain_low = low(gain_pair)
        expand_low = low(weight_expand)
        contract_low = low(weight_contract)
        scale_one = lax.rsqrt(lax.optimization_barrier(jnp.mean(flat * flat, axis=-1, keepdims=True)) + norm_eps)
        normed_one = low(flat * scale_one * gain_low[0])
        joined = low_back(jnp.dot(normed_one, low(weight_joined), precision=highest))
        queries = low(rotate(joined[:, :QDIM], flat_places, HEADS))
        keys = low(rotate(joined[:, QDIM:QDIM + KVDIM], flat_places, KV_HEADS))
        values = low(joined[:, QDIM + KVDIM:])
        attended = low_back(low(attention(queries, keys, values)))
        middle = flat + low_back(jnp.dot(attended, low(weight_output), precision=highest))
        scale_two = lax.rsqrt(lax.optimization_barrier(jnp.mean(middle * middle, axis=-1, keepdims=True)) + norm_eps)
        normed_two = low(middle * scale_two * gain_low[1])

        def block_moe(pack):
            block_rows, route_row, gate_row = pack
            dest, slot_row = slot_tables(route_row, EXPERTS, CAP)
            picked = jnp.take(block_rows, slot_row // TOP, axis=0, mode='fill', fill_value=0.0)
            rows = low_back(picked).reshape(EXPERTS, CAP, D)
            joined_in = low_back(jnp.einsum('xcd,xdf->xcf', rows, expand_low, precision=highest))
            gate_part = joined_in[..., :FF]
            up_part = joined_in[..., FF:]
            hidden = low(jax.nn.silu(gate_part) * up_part)
            expert_out = low_back(low(jnp.einsum('xcf,xfd->xcd', hidden, contract_low, precision=highest)))
            chosen = jnp.take(expert_out.reshape(-1, D), dest, axis=0).reshape(TOK_DEV, TOP, D)
            return lax.optimization_barrier(jnp.sum(chosen * gate_row.reshape(TOK_DEV, TOP, 1), axis=1))
        mixture = lax.map(jax.checkpoint(block_moe), (normed_two.reshape(-1, TOK_DEV, D), route_rows, gate_rows))
        return (middle + mixture.reshape(-1, D)).reshape(SEQS, SEQ_LEN, D)
    result, pullback = jax.vjp(forward, layer_input.astype(jnp.float32), joined_weight, output_weight, norm_gains, expand_weight, contract_weight)
    grad_x, grad_joined, grad_output, grad_gains, grad_expand, grad_contract = pullback(cotangent.astype(jnp.float32))
    joined_new = adamw(joined_weight, joined_first, joined_second, grad_joined, rate_joined, decay_rate)
    output_new = adamw(output_weight, output_first, output_second, grad_output, rate_output, decay_rate)
    gains_new = adamw(norm_gains, gains_first, gains_second, grad_gains, rate_gains, 0.0)
    expand_new = adamw(expand_weight, expand_first, expand_second, grad_expand, rate_expand, decay_rate)
    contract_new = adamw(contract_weight, contract_first, contract_second, grad_contract, rate_contract, decay_rate)
    return (result.astype(jnp.bfloat16), grad_x.astype(jnp.bfloat16), joined_new[0], joined_new[1], joined_new[2], output_new[0], output_new[1], output_new[2], gains_new[0], gains_new[1], gains_new[2], expand_new[0], expand_new[1], expand_new[2], contract_new[0], contract_new[1], contract_new[2])
```

```python
import functools
import math

import jax
import jax.numpy as jnp
import numpy as np
from jax import lax
from jax.experimental import pallas as pl
from jax.experimental.pallas import tpu as pltpu
from jax.sharding import PartitionSpec as P

HEADS = 24
KV_HEADS = 8
HEAD_DIM = 64
FF = 512
TOP = 8
STEP = 10
GROUPS = HEADS // KV_HEADS
PAIRS = KV_HEADS // 2
QUERY_WIDTH = HEADS * HEAD_DIM
KV_WIDTH = KV_HEADS * HEAD_DIM
PAIR_WIDTH = 2 * GROUPS * HEAD_DIM
LANES = 128
VMEM_BYTES = 60 * 1024 * 1024

norm_eps = 1e-06
beta_one = 0.9
beta_two = 0.95
adam_eps = 1e-08
decay_rate = 0.1
rate_joined = 0.08
rate_output = 0.6
rate_gains = 0.6
rate_expand = 0.08
rate_contract = 0.5
masked_score = -1e30

low = jnp.bfloat16
wide = jnp.float32


def adamw(weight, first, second, grad, rate, decay):
    first_new = beta_one * first + (1.0 - beta_one) * grad
    second_new = beta_two * second + (1.0 - beta_two) * grad * grad
    first_hat = first_new / (1.0 - beta_one**STEP)
    second_hat = second_new / (1.0 - beta_two**STEP)
    weight_new = weight - rate * (first_hat / (jnp.sqrt(second_hat) + adam_eps) + decay * weight)
    return (weight_new, first_new, second_new)


def dot_nn(left, right):
    return lax.dot_general(left, right, (((1,), (0,)), ((), ())), preferred_element_type=wide)


def dot_nt(left, right):
    return lax.dot_general(left, right, (((1,), (1,)), ((), ())), preferred_element_type=wide)


def pair_order(groups):
    half = HEAD_DIM // 2
    old = np.arange(2 * groups * HEAD_DIM).reshape(2, groups, 2, half)
    return old.transpose(1, 2, 0, 3).reshape(-1)


def order_matrix(groups):
    order = pair_order(groups)
    size = order.shape[0]
    return jnp.asarray(np.arange(size)[:, None] == order[None, :], dtype=low)


def reorder_columns(rows, back=False):
    count = rows.shape[0]
    query_mat = order_matrix(GROUPS)
    key_mat = order_matrix(1)
    if back:
        query_mat = query_mat.T
        key_mat = key_mat.T
    exact = lax.Precision.HIGHEST if rows.dtype == wide else None
    query = jnp.einsum(
        "rpo,on->rpn",
        rows[:, :QUERY_WIDTH].reshape(count, PAIRS, PAIR_WIDTH),
        query_mat.astype(rows.dtype),
        precision=exact,
        preferred_element_type=wide,
    ).reshape(count, QUERY_WIDTH)
    others = jnp.einsum(
        "rpo,on->rpn",
        rows[:, QUERY_WIDTH:].reshape(count, 2 * PAIRS, LANES),
        key_mat.astype(rows.dtype),
        precision=exact,
        preferred_element_type=wide,
    ).reshape(count, 2 * KV_WIDTH)
    return jnp.concatenate([query, others], axis=1)


def swap(block, axis, step):
    count = lax.axis_size(axis)
    return lax.ppermute(block, axis, [(i, i ^ step) for i in range(count)])


def spread(block, axis):
    return [block] + [swap(block, axis, k) for k in range(1, lax.axis_size(axis))]


def spread_weights(shard):
    line = jnp.concatenate(spread(shard, "context"), axis=0)
    mine = spread(line, "expert")
    other = [swap(part, "dp", 1) for part in mine]
    return mine + other


def sum_to_owners(parts):
    owners, contexts = parts.shape[1:3]
    both = (parts[0].astype(wide) + swap(parts[1], "dp", 1).astype(wide)).astype(low)
    total = both[0].astype(wide)
    for k in range(1, owners):
        total = total + swap(both[k], "expert", k).astype(wide)
    column = total.astype(low)
    total = column[0].astype(wide)
    for k in range(1, contexts):
        total = total + swap(column[k], "context", k).astype(wide)
    return total


def call(body, grid, in_specs, out_specs, out_shape, scratch=(), flops=0, moved=0, exps=0):
    return pl.pallas_call(
        body,
        grid=grid,
        in_specs=in_specs,
        out_specs=out_specs,
        out_shape=out_shape,
        scratch_shapes=list(scratch),
        compiler_params=pltpu.CompilerParams(vmem_limit_bytes=VMEM_BYTES),
        cost_estimate=pl.CostEstimate(flops=flops, bytes_accessed=moved, transcendentals=exps),
    )


def turn(vals, cosine, sine):
    return vals * cosine + pltpu.roll(vals, LANES // 2, 1) * sine


def project_body(count, rows_ref, scale_ref, cos_ref, sin_ref, *refs):
    weight_refs, (query_ref, kv_ref) = refs[:count], refs[count:]
    step = pl.program_id(0)
    total = None
    depth = weight_refs[0].shape[0]
    for k in range(count):
        part = dot_nn(rows_ref[:, k * depth : (k + 1) * depth], weight_refs[k][...])
        total = part if total is None else total + part
    total = total * scale_ref[...]
    block = total.shape[1]
    query_steps = QUERY_WIDTH // block
    cosine, sine = cos_ref[...], sin_ref[...]

    @pl.when(step < query_steps + KV_WIDTH // block)
    def _():
        turned = jnp.concatenate(
            [
                turn(total[:, i * LANES : (i + 1) * LANES], cosine, sine)
                for i in range(block // LANES)
            ],
            axis=1,
        )

        @pl.when(step < query_steps)
        def _():
            query_ref[...] = (turned * HEAD_DIM**-0.5).astype(low)

        @pl.when(step >= query_steps)
        def _():
            kv_ref[...] = turned.astype(low)

    @pl.when(step >= query_steps + KV_WIDTH // block)
    def _():
        kv_ref[...] = total.astype(low)


def project(rows, scale, cosine, sine, weights):
    tokens, width = rows.shape
    columns = QUERY_WIDTH + 2 * KV_WIDTH
    block = 256
    query_steps = QUERY_WIDTH // block
    depth = weights[0].shape[0]
    whole = lambda shape: pl.BlockSpec(shape, lambda j: (0, 0))
    return call(
        functools.partial(project_body, len(weights)),
        (columns // block,),
        [whole((tokens, width)), whole((tokens, 1)), whole((tokens, LANES)), whole((tokens, LANES))]
        + [pl.BlockSpec((depth, block), lambda j: (0, j))] * len(weights),
        [
            pl.BlockSpec((tokens, block), lambda j: (0, jnp.minimum(j, query_steps - 1))),
            pl.BlockSpec((tokens, block), lambda j: (0, jnp.maximum(j - query_steps, 0))),
        ],
        [
            jax.ShapeDtypeStruct((tokens, QUERY_WIDTH), low),
            jax.ShapeDtypeStruct((tokens, 2 * KV_WIDTH), low),
        ],
        flops=2 * tokens * width * columns,
        moved=2 * width * columns,
    )(rows, scale, cosine, sine, *weights)


def lane_of(shape, axis, which):
    place = lax.broadcasted_iota(jnp.int32, shape, axis)
    return ((place // (HEAD_DIM // 2)) % 2) == which


def stack_heads(block, which):
    keep = lane_of((block.shape[0], LANES), 1, which)
    return jnp.concatenate(
        [
            jnp.where(keep, block[:, g * LANES : (g + 1) * LANES], jnp.zeros((), block.dtype))
            for g in range(GROUPS)
        ],
        axis=0,
    )


def allowed_pairs(key_pos, query_pos):
    seen = key_pos <= query_pos
    return jnp.concatenate([seen] * GROUPS, axis=1)


def turned_block(block):
    return block.astype(wide).T.astype(low)


def attend_body(count, query_ref, key_pos_ref, query_pos_ref, *refs):
    key_refs, value_refs = refs[:count], refs[count : 2 * count]
    out_ref, out_low_ref, log_ref = refs[2 * count :]
    tokens = query_ref.shape[0]
    seen = [
        allowed_pairs(key_pos_ref[k * tokens : (k + 1) * tokens, :], query_pos_ref[...])
        for k in range(count)
    ]
    values = [turned_block(ref[...]) for ref in value_refs]
    outs = []
    for which in range(2):
        query = stack_heads(query_ref[...], which)
        scores = [
            jnp.where(seen[k], dot_nt(key_refs[k][...], query), masked_score) for k in range(count)
        ]
        peak = functools.reduce(jnp.maximum, [jnp.max(s, axis=0, keepdims=True) for s in scores])
        total = None
        accum = None
        for k in range(count):
            weight = jnp.exp(scores[k] - peak)
            part_sum = jnp.sum(weight, axis=0, keepdims=True)
            part = dot_nn(values[k], weight.astype(low))
            total = part_sum if total is None else total + part_sum
            accum = part if accum is None else accum + part
        outs.append(accum / total)
        log_ref[0, which : which + 1, :] = peak + jnp.log(total)
    first = lane_of(outs[0].shape, 0, 0)
    both = jnp.where(first, outs[0], outs[1]).T
    for g in range(GROUPS):
        piece = both[g * tokens : (g + 1) * tokens, :]
        out_ref[:, g * LANES : (g + 1) * LANES] = piece
        out_low_ref[:, g * LANES : (g + 1) * LANES] = piece.astype(low)


def pair_specs(tokens, count):
    return (
        [pl.BlockSpec((tokens, LANES), lambda p: (0, p))] * count
        + [pl.BlockSpec((tokens, LANES), lambda p: (0, PAIRS + p))] * count
    )


def attend(query, key_pos, query_pos, kv_parts):
    tokens = query.shape[0]
    count = len(kv_parts)
    seq_len = tokens * count
    pairs = pl.BlockSpec((tokens, PAIR_WIDTH), lambda p: (0, p))
    return call(
        functools.partial(attend_body, count),
        (PAIRS,),
        [
            pairs,
            pl.BlockSpec((seq_len, 1), lambda p: (0, 0)),
            pl.BlockSpec((1, tokens), lambda p: (0, 0)),
        ]
        + pair_specs(tokens, count),
        [pairs, pairs, pl.BlockSpec((1, 2, GROUPS * tokens), lambda p: (p, 0, 0))],
        [
            jax.ShapeDtypeStruct((tokens, QUERY_WIDTH), wide),
            jax.ShapeDtypeStruct((tokens, QUERY_WIDTH), low),
            jax.ShapeDtypeStruct((PAIRS, 2, GROUPS * tokens), wide),
        ],
        flops=16 * HEADS * tokens * seq_len * HEAD_DIM,
        moved=4 * seq_len * KV_WIDTH,
        exps=HEADS * tokens * seq_len,
    )(query, key_pos, query_pos, *kv_parts, *kv_parts)


def attend_back_body(count, query_ref, grad_ref, out_ref, log_ref, key_pos_ref, query_pos_ref,
                     scale_ref, cos_ref, sin_ref, *refs):
    key_refs, value_refs = refs[:count], refs[count : 2 * count]
    grad_query_ref = refs[2 * count]
    grad_key_refs = refs[2 * count + 1 : 3 * count + 1]
    grad_value_refs = refs[3 * count + 1 :]
    tokens = query_ref.shape[0]
    grads = grad_ref[...]
    product = jnp.concatenate(
        [
            (grads[:, g * LANES : (g + 1) * LANES].astype(wide)
             * out_ref[:, g * LANES : (g + 1) * LANES]).T
            for g in range(GROUPS)
        ],
        axis=1,
    )
    first = lane_of(product.shape, 0, 0)
    delta = [
        jnp.sum(jnp.where(first, product, 0.0), axis=0, keepdims=True),
        jnp.sum(jnp.where(first, 0.0, product), axis=0, keepdims=True),
    ]
    queries = [stack_heads(query_ref[...], which) for which in range(2)]
    heads = [stack_heads(grads, which) for which in range(2)]
    grad_query = [None, None]
    for k in range(count):
        seen = allowed_pairs(key_pos_ref[k * tokens : (k + 1) * tokens, :], query_pos_ref[...])
        keys, values = key_refs[k][...], value_refs[k][...]
        keys_turned = turned_block(keys)
        grad_key, grad_value = None, None
        for which in range(2):
            scores = jnp.where(seen, dot_nt(keys, queries[which]), masked_score)
            probs = jnp.exp(scores - log_ref[0, which : which + 1, :])
            grad_probs = dot_nt(values, heads[which])
            grad_scores = (probs * (grad_probs - delta[which])).astype(low)
            part_value = dot_nn(probs.astype(low), heads[which])
            part_key = dot_nn(grad_scores, queries[which])
            part_query = dot_nn(keys_turned, grad_scores)
            grad_value = part_value if grad_value is None else grad_value + part_value
            grad_key = part_key if grad_key is None else grad_key + part_key
            old = grad_query[which]
            grad_query[which] = part_query if old is None else old + part_query
        grad_key_refs[k][...] = grad_key.astype(low)
        grad_value_refs[k][...] = grad_value.astype(low)
    first = lane_of(grad_query[0].shape, 0, 0)
    both = (jnp.where(first, grad_query[0], grad_query[1]) * HEAD_DIM**-0.5).T
    for g in range(GROUPS):
        piece = both[g * tokens : (g + 1) * tokens, :]
        back = turn(piece, cos_ref[...], -sin_ref[...])
        grad_query_ref[:, g * LANES : (g + 1) * LANES] = (back * scale_ref[...]).astype(low)


def attend_back(query, grads, out, logs, key_pos, query_pos, scale, cosine, sine, kv_parts):
    tokens = query.shape[0]
    count = len(kv_parts)
    seq_len = tokens * count
    pairs = pl.BlockSpec((tokens, PAIR_WIDTH), lambda p: (0, p))
    whole = lambda shape: pl.BlockSpec(shape, lambda p: (0, 0))
    half = pl.BlockSpec((tokens, LANES), lambda p: (0, p))
    results = call(
        functools.partial(attend_back_body, count),
        (PAIRS,),
        [
            pairs,
            pairs,
            pairs,
            pl.BlockSpec((1, 2, GROUPS * tokens), lambda p: (p, 0, 0)),
            whole((seq_len, 1)),
            whole((1, tokens)),
            whole((tokens, 1)),
            whole((tokens, LANES)),
            whole((tokens, LANES)),
        ]
        + pair_specs(tokens, count),
        [pairs] + [half] * (2 * count),
        [jax.ShapeDtypeStruct((tokens, QUERY_WIDTH), low)]
        + [jax.ShapeDtypeStruct((tokens, KV_WIDTH), low)] * (2 * count),
        flops=40 * HEADS * tokens * seq_len * HEAD_DIM,
        moved=8 * seq_len * KV_WIDTH,
        exps=HEADS * tokens * seq_len,
    )(query, grads, out, logs, key_pos, query_pos, scale, cosine, sine, *kv_parts, *kv_parts)
    return results[0], results[1 : count + 1], results[count + 1 :]


def hidden_body(sub, rows_ref, grads_ref, gate_ref, weight_ref, hidden_ref, back_ref):
    for t in range(rows_ref.shape[0] // sub):
        part = pl.ds(t * sub, sub)
        joined = dot_nn(rows_ref[part, :], weight_ref[0, :, : 2 * FF])
        grad_hidden = dot_nn(grads_ref[part, :], weight_ref[0, :, 2 * FF :])
        weight = gate_ref[0, part, :]
        gate, up = joined[:, :FF], joined[:, FF:]
        sigmoid = 1.0 / (1.0 + jnp.exp(-gate))
        active = gate * sigmoid
        hidden_ref[0, part, :] = (active * up * weight).astype(low)
        grad_hidden = grad_hidden * weight
        slope = sigmoid * (1.0 + gate * (1.0 - sigmoid))
        back_ref[0, part, :FF] = (grad_hidden * up * slope).astype(low)
        back_ref[0, part, FF:] = (grad_hidden * active).astype(low)


def expert_hidden(rows, grads, gates, weights):
    tokens, width = rows.shape
    experts = weights.shape[0]
    block = min(tokens, 512)
    sub = 256
    return call(
        functools.partial(hidden_body, sub),
        (experts, tokens // block),
        [
            pl.BlockSpec((block, width), lambda e, t: (t, 0)),
            pl.BlockSpec((block, width), lambda e, t: (t, 0)),
            pl.BlockSpec((1, block, 1), lambda e, t: (e, t, 0)),
            pl.BlockSpec((1, width, 3 * FF), lambda e, t: (e, 0, 0)),
        ],
        [
            pl.BlockSpec((1, block, FF), lambda e, t: (e, t, 0)),
            pl.BlockSpec((1, block, 2 * FF), lambda e, t: (e, t, 0)),
        ],
        [
            jax.ShapeDtypeStruct((experts, tokens, FF), low),
            jax.ShapeDtypeStruct((experts, tokens, 2 * FF), low),
        ],
        flops=6 * experts * tokens * width * FF,
        moved=experts * (6 * width * FF + 4 * tokens * width),
        exps=experts * tokens * FF,
    )(rows, grads, gates, weights)


def weight_grad_body(rows_ref, grads_ref, back_ref, hidden_ref, out_ref):
    out_ref[0, :, : 2 * FF] = dot_nn(rows_ref[...], back_ref[0]).astype(low)
    out_ref[0, :, 2 * FF :] = dot_nn(grads_ref[...], hidden_ref[0]).astype(low)


def expert_weight_grads(rows_turned, grads_turned, back, hidden):
    width, tokens = rows_turned.shape
    experts = back.shape[0]
    block = 256
    return call(
        weight_grad_body,
        (experts, width // block),
        [
            pl.BlockSpec((block, tokens), lambda e, m: (m, 0)),
            pl.BlockSpec((block, tokens), lambda e, m: (m, 0)),
            pl.BlockSpec((1, tokens, 2 * FF), lambda e, m: (e, 0, 0)),
            pl.BlockSpec((1, tokens, FF), lambda e, m: (e, 0, 0)),
        ],
        pl.BlockSpec((1, block, 3 * FF), lambda e, m: (e, m, 0)),
        jax.ShapeDtypeStruct((experts, width, 3 * FF), low),
        flops=6 * experts * tokens * width * FF,
        moved=experts * (6 * width * FF + 10 * tokens * width),
    )(rows_turned, grads_turned, back, hidden)


def combine_body(sizes, *refs):
    count = len(sizes)
    part_refs, weight_refs, out_ref, total_ref = (
        refs[:count], refs[count : 2 * count], refs[2 * count], refs[2 * count + 1]
    )
    step = pl.program_id(1)

    @pl.when(step == 0)
    def _():
        total_ref[...] = jnp.zeros_like(total_ref)

    start = 0
    for part_ref, weight_ref, size in zip(part_refs, weight_refs, sizes):

        @pl.when((step >= start) & (step < start + size))
        def _():
            total_ref[...] += dot_nt(part_ref[0], weight_ref[0])

        start += size

    @pl.when(step == start - 1)
    def _():
        out_ref[...] = total_ref[...].astype(low)


def combine(parts, weights, column):
    tokens, depth = parts[0].shape[1:]
    width = weights[0].shape[1]
    sizes = [w.shape[0] for w in weights]
    experts = sum(sizes)
    block = min(tokens, 512)
    starts = [sum(sizes[:i]) for i in range(len(sizes))]
    place = lambda e, start, size: jnp.clip(e - start, 0, size - 1)
    part_specs = [
        pl.BlockSpec((1, block, depth), lambda t, e, s=s, n=n: (place(e, s, n), t, 0))
        for s, n in zip(starts, sizes)
    ]
    weight_specs = [
        pl.BlockSpec((1, width, depth), lambda t, e, s=s, n=n: (place(e, s, n), 0, column))
        for s, n in zip(starts, sizes)
    ]
    return call(
        functools.partial(combine_body, sizes),
        (tokens // block, experts),
        part_specs + weight_specs,
        pl.BlockSpec((block, width), lambda t, e: (t, 0)),
        jax.ShapeDtypeStruct((tokens, width), low),
        scratch=[pltpu.VMEM((block, width), wide)],
        flops=2 * experts * tokens * width * depth,
        moved=2 * experts * width * depth * (tokens // block),
    )(*parts, *weights)


def body(
    layer_input,
    cotangent,
    block_order,
    routes,
    route_gates,
    joined_weight,
    joined_first,
    joined_second,
    output_weight,
    output_first,
    output_second,
    norm_gains,
    gains_first,
    gains_second,
    expand_weight,
    expand_first,
    expand_second,
    contract_weight,
    contract_first,
    contract_second,
):
    experts_dev = expand_weight.shape[0]
    owners = lax.axis_size("expert")
    contexts = lax.axis_size("context")
    cores = lax.axis_size("dp")
    experts = experts_dev * owners
    tokens = layer_input.shape[1]
    width = layer_input.shape[2]
    half_block = tokens // 2
    slice_rows = joined_weight.shape[0]
    own_expert = lax.axis_index("expert")
    own_context = lax.axis_index("context")
    own_core = lax.axis_index("dp")

    gain_rows = norm_gains.astype(low).astype(wide).T
    joined_low = joined_weight.astype(low)
    joined_shard = reorder_columns((gain_rows[:, :1] * joined_low.astype(wide)).astype(low)).astype(low)
    joined_parts = spread_weights(joined_shard)
    query_mat = order_matrix(GROUPS)
    output_shard = jnp.einsum(
        "pod,on->dpn",
        output_weight.astype(low).reshape(PAIRS, PAIR_WIDTH, slice_rows),
        query_mat,
        preferred_element_type=wide,
    ).reshape(slice_rows, QUERY_WIDTH).astype(low)
    output_shard = jnp.concatenate(
        [output_shard, jnp.broadcast_to(gain_rows[:, 1:].astype(low), (slice_rows, LANES))], axis=1
    )
    output_parts = spread_weights(output_shard)

    chunks = [(0, 1), (1, 3), (3, experts_dev)]
    expert_low = [
        jnp.concatenate(
            [
                expand_weight[a:b].astype(low),
                jnp.swapaxes(contract_weight[a:b].astype(low), 1, 2),
            ],
            axis=2,
        )
        for a, b in chunks
    ]
    expert_full = [
        lax.all_gather(shard, ("context", "dp"), axis=1, tiled=True) for shard in expert_low
    ]

    ar = lambda n: jnp.arange(n, dtype=jnp.int32)
    to_relative = (
        ((own_expert ^ ar(owners))[None, :, None] * contexts + (own_context ^ ar(contexts))[None, None, :])
        * cores
        + (own_core ^ ar(cores))[:, None, None]
    ).reshape(-1)
    to_absolute = (
        (own_core ^ ar(cores))[None, None, :] * owners + (own_expert ^ ar(owners))[:, None, None]
    ) * contexts + (own_context ^ ar(contexts))[None, :, None]
    to_absolute = to_absolute.reshape(-1)
    slices = owners * contexts * cores

    def pick_rows(rows, index):
        return jnp.take(
            rows.reshape(slices, slice_rows, -1), index, axis=0, mode="clip", unique_indices=True
        ).reshape(rows.shape)

    hits = routes[0][:, :, None] == ar(experts)[None, None, :]
    gate_table = jnp.sum(jnp.where(hits, route_gates[0][:, :, None], 0.0), axis=1)
    gate_table = gate_table.reshape(tokens, owners, experts_dev)
    gate_parts = [
        lax.dynamic_index_in_dim(gate_table, own_expert ^ k, axis=1, keepdims=False)
        for k in range(owners)
    ]
    gates = jnp.concatenate(
        [gate_parts[0]] + [swap(gate_parts[k], "expert", k) for k in range(1, owners)], axis=0
    )
    gates = gates.T[:, :, None]
    out_grads = jnp.concatenate(spread(cotangent[0], "expert"), axis=0)
    out_grads_turned = out_grads.T

    order = block_order[0]
    offsets = ar(half_block)

    def places_of(index):
        mine = lax.dynamic_slice_in_dim(order, 2 * index, 2)
        return (mine[:, None] * half_block + offsets[None, :]).reshape(-1)

    query_pos = places_of(own_context)
    key_pos = jnp.concatenate([places_of(own_context ^ k) for k in range(contexts)])
    half = HEAD_DIM // 2
    freq = jnp.exp(ar(half).astype(wide) * (2.0 / HEAD_DIM) * -math.log(10000.0))
    angle = query_pos.astype(wide)[:, None] * freq[None, :]
    cosine = jnp.tile(jnp.cos(angle), (1, 4))
    sine = jnp.sin(angle)
    sine = jnp.concatenate([-sine, -sine, sine, sine], axis=1)

    low_input = layer_input[0]
    resid = low_input.astype(wide)
    scale_one = lax.rsqrt(jnp.mean(resid * resid, axis=-1, keepdims=True) + norm_eps)
    unit_one = resid * scale_one
    input_turned = pick_rows(low_input.T, to_relative)
    input_relative = input_turned.T
    query, kv = project(input_relative, scale_one, cosine, sine, joined_parts)
    kv_parts = spread(kv, "context")
    attended_wide, attended, logs = attend(query, key_pos[:, None], query_pos[None, :], kv_parts)

    output_pack = pick_rows(jnp.concatenate(output_parts, axis=0), to_absolute)
    output_turned = output_pack[:, :QUERY_WIDTH]
    gain_two = output_pack[:, QUERY_WIDTH].astype(wide)[None, :]
    middle = resid + dot_nt(attended, output_turned)
    scale_two = lax.rsqrt(jnp.mean(middle * middle, axis=-1, keepdims=True) + norm_eps)
    unit_two = middle * scale_two
    normed_two = (unit_two * gain_two).astype(low)

    rows = jnp.concatenate(spread(normed_two, "expert"), axis=0)
    rows_turned = rows.T
    hiddens, backs, expert_grads = [], [], []
    for (a, b), weights in zip(chunks, expert_full):
        hidden, back = expert_hidden(rows, out_grads, gates[a:b], weights)
        hiddens.append(hidden)
        backs.append(back)
        weight_grads = expert_weight_grads(rows_turned, out_grads_turned, back, hidden)
        expert_grads.append(
            lax.psum_scatter(weight_grads, ("context", "dp"), scatter_dimension=1, tiled=True)
        )

    def to_tokens(part):
        parts = part.reshape(owners, tokens, width)
        total = parts[0].astype(wide)
        for k in range(1, owners):
            total = total + swap(parts[k], "expert", k).astype(wide)
        return total

    grad_normed_two = to_tokens(combine(backs, expert_full, 0))
    mixture = to_tokens(combine(hiddens, expert_full, 2))
    output = (middle + mixture).astype(low)

    grad_out = cotangent[0].astype(wide)
    grad_unit_two = grad_normed_two * gain_two
    gain_grad_two = jnp.sum(grad_normed_two * unit_two, axis=0)
    grad_middle = grad_out + scale_two * (
        grad_unit_two - unit_two * jnp.mean(grad_unit_two * unit_two, axis=-1, keepdims=True)
    )
    grad_proj = grad_middle.astype(low)
    grad_attended = dot_nn(grad_proj, output_turned).astype(low)
    grad_query, grad_keys, grad_values = attend_back(
        query, grad_attended, attended_wide, logs, key_pos[:, None], query_pos[None, :],
        scale_one, cosine, sine, kv_parts,
    )
    grad_kv = [jnp.concatenate([a, b], axis=1) for a, b in zip(grad_keys, grad_values)]
    own_grad_kv = grad_kv[0].astype(wide)
    for k in range(1, contexts):
        own_grad_kv = own_grad_kv + swap(grad_kv[k], "context", k).astype(wide)
    grad_key = own_grad_kv[:, :KV_WIDTH].reshape(tokens, PAIRS, 2, LANES // 2)
    turned_key = jnp.concatenate([grad_key[:, :, 1:], grad_key[:, :, :1]], axis=2)
    grad_key = (
        grad_key.reshape(tokens, PAIRS, LANES) * cosine[:, None]
        - turned_key.reshape(tokens, PAIRS, LANES) * sine[:, None]
    ).reshape(tokens, KV_WIDTH)
    grad_kv_low = (
        jnp.concatenate([grad_key, own_grad_kv[:, KV_WIDTH:]], axis=1) * scale_one
    ).astype(low)

    relative = (cores, owners, contexts, slice_rows)
    proj_turned = pick_rows(grad_proj.T, to_relative)
    grad_output = dot_nn(proj_turned, attended).astype(low)
    gain_column = pick_rows(gain_grad_two[:, None], to_relative).astype(low)
    grad_output = jnp.concatenate(
        [grad_output, jnp.broadcast_to(gain_column, (width, LANES))], axis=1
    )
    sum_output = sum_to_owners(grad_output.reshape(*relative, -1))
    sum_query = sum_to_owners(dot_nn(input_turned, grad_query).astype(low).reshape(*relative, -1))
    sum_kv = sum_to_owners(dot_nn(input_turned, grad_kv_low).astype(low).reshape(*relative, -1))

    grad_joined_low = jnp.concatenate([grad_query, grad_kv_low], axis=1)
    scaled_grad = jnp.concatenate(
        [dot_nt(part, grad_joined_low) for part in joined_parts], axis=0
    )
    scaled_grad = pick_rows(scaled_grad, to_absolute).T
    grad_input = (
        grad_middle
        + scaled_grad
        - unit_one * jnp.mean(scaled_grad * unit_one, axis=-1, keepdims=True)
    ).astype(low)

    unit_grads = reorder_columns(jnp.concatenate([sum_query, sum_kv], axis=1), back=True)
    sum_joined = gain_rows[:, :1] * unit_grads
    sum_gain_one = jnp.sum(joined_low.astype(wide) * unit_grads, axis=1)
    sum_gains = jnp.stack([sum_gain_one, sum_output[:, QUERY_WIDTH]], axis=0)
    sum_output_weight = jnp.einsum(
        "on,dpn->pod",
        query_mat.astype(wide),
        sum_output[:, :QUERY_WIDTH].reshape(slice_rows, PAIRS, PAIR_WIDTH),
        precision=lax.Precision.HIGHEST,
        preferred_element_type=wide,
    ).reshape(QUERY_WIDTH, slice_rows)
    joined_new = adamw(
        joined_weight, joined_first, joined_second, sum_joined, rate_joined, decay_rate
    )
    output_new = adamw(
        output_weight, output_first, output_second, sum_output_weight, rate_output, decay_rate
    )
    gains_new = adamw(norm_gains, gains_first, gains_second, sum_gains, rate_gains, 0.0)
    sum_experts = jnp.concatenate(expert_grads, axis=0).astype(wide)
    expand_new = adamw(
        expand_weight, expand_first, expand_second, sum_experts[:, :, : 2 * FF], rate_expand, decay_rate
    )
    contract_new = adamw(
        contract_weight,
        contract_first,
        contract_second,
        jnp.swapaxes(sum_experts[:, :, 2 * FF :], 1, 2),
        rate_contract,
        decay_rate,
    )
    return (
        output.reshape(1, tokens, width),
        grad_input.reshape(1, tokens, width),
        *joined_new,
        *output_new,
        *gains_new,
        *expand_new,
        *contract_new,
    )


def solution(mesh):
    rows = P(("expert", "dp"), "context", None)
    joined = P(("expert", "context", "dp"), None)
    column = P(None, ("expert", "context", "dp"))
    expand = P("expert", ("context", "dp"), None)
    contract = P("expert", None, ("context", "dp"))
    placed = (
        (rows, rows, P(("expert", "dp"), None), rows, rows)
        + (joined,) * 3
        + (column,) * 6
        + (expand,) * 3
        + (contract,) * 3
    )
    return jax.shard_map(
        body,
        mesh=mesh,
        in_specs=placed,
        out_specs=(rows, rows) + placed[5:],
        check_vma=False,
    )
```

```python
import functools
import math

import jax
import jax.numpy as jnp
import numpy as np
from jax import lax
from jax.experimental import pallas as pl
from jax.experimental.pallas import tpu as pltpu
from jax.sharding import PartitionSpec as P

HEADS = 24
KV_HEADS = 8
HEAD_DIM = 64
FF = 512
TOP = 8
STEP = 10
GROUPS = HEADS // KV_HEADS
PAIRS = KV_HEADS // 2
QUERY_WIDTH = HEADS * HEAD_DIM
KV_WIDTH = KV_HEADS * HEAD_DIM
PAIR_WIDTH = 2 * GROUPS * HEAD_DIM
LANES = 128
VMEM_BYTES = 60 * 1024 * 1024

norm_eps = 1e-06
beta_one = 0.9
beta_two = 0.95
adam_eps = 1e-08
decay_rate = 0.1
rate_joined = 0.08
rate_output = 0.6
rate_gains = 0.6
rate_expand = 0.08
rate_contract = 0.5
masked_score = -1e30

low = jnp.bfloat16
wide = jnp.float32


def adamw(weight, first, second, grad, rate, decay):
    first_new = beta_one * first + (1.0 - beta_one) * grad
    second_new = beta_two * second + (1.0 - beta_two) * grad * grad
    first_hat = first_new / (1.0 - beta_one**STEP)
    second_hat = second_new / (1.0 - beta_two**STEP)
    weight_new = weight - rate * (first_hat / (jnp.sqrt(second_hat) + adam_eps) + decay * weight)
    return (weight_new, first_new, second_new)


def dot_nn(left, right):
    return lax.dot_general(left, right, (((1,), (0,)), ((), ())), preferred_element_type=wide)


def dot_nt(left, right):
    return lax.dot_general(left, right, (((1,), (1,)), ((), ())), preferred_element_type=wide)


def pair_order(groups):
    half = HEAD_DIM // 2
    old = np.arange(2 * groups * HEAD_DIM).reshape(2, groups, 2, half)
    return old.transpose(1, 2, 0, 3).reshape(-1)


def order_matrix(groups):
    order = pair_order(groups)
    size = order.shape[0]
    return jnp.asarray(np.arange(size)[:, None] == order[None, :], dtype=low)


def reorder_columns(rows, back=False):
    count = rows.shape[0]
    query_mat = order_matrix(GROUPS)
    key_mat = order_matrix(1)
    kv = rows[:, QUERY_WIDTH:]
    if back:
        query_mat = query_mat.T
        key_mat = key_mat.T
        kv = jnp.swapaxes(kv.reshape(count, PAIRS, 2, LANES), 1, 2)
    else:
        kv = jnp.swapaxes(kv.reshape(count, 2, PAIRS, LANES), 1, 2)
    exact = lax.Precision.HIGHEST if rows.dtype == wide else None
    query = jnp.einsum(
        "rpo,on->rpn",
        rows[:, :QUERY_WIDTH].reshape(count, PAIRS, PAIR_WIDTH),
        query_mat.astype(rows.dtype),
        precision=exact,
        preferred_element_type=wide,
    ).reshape(count, QUERY_WIDTH)
    others = jnp.einsum(
        "rpo,on->rpn",
        kv.reshape(count, 2 * PAIRS, LANES),
        key_mat.astype(rows.dtype),
        precision=exact,
        preferred_element_type=wide,
    ).reshape(count, 2 * KV_WIDTH)
    return jnp.concatenate([query, others], axis=1)


def swap(block, axis, step):
    count = lax.axis_size(axis)
    return lax.ppermute(block, axis, [(i, i ^ step) for i in range(count)])


def spread(block, axis):
    return [block] + [swap(block, axis, k) for k in range(1, lax.axis_size(axis))]


def after(value, *others):
    return lax.optimization_barrier((value, *others))[0]


def spread_line(shard):
    return jnp.concatenate(spread(shard, "context"), axis=0)


def spread_rest(mine):
    return mine + [swap(part, "dp", 1) for part in mine]


def sum_to_owners(own, other):
    owners, contexts = own.shape[:2]
    came = swap(other, "dp", 1)
    both = [(own[k].astype(wide) + came[k].astype(wide)).astype(low) for k in range(owners)]
    total = both[0].astype(wide)
    for k in range(1, owners):
        total = total + swap(both[k], "expert", k).astype(wide)
    column = [total[k].astype(low) for k in range(contexts)]
    total = total[0]
    for k in range(1, contexts):
        total = total + swap(column[k], "context", k).astype(wide)
    return total


def line_order(own):
    near = jnp.array([1, 2, 3, 0], jnp.int32)
    return jnp.where(own < 2, near, 3 - near)


def sum_on_line(own, other):
    came = swap(other, "dp", 1)
    first = (own[:3].astype(wide) + came[:3].astype(wide)).astype(low)
    last = (own[3].astype(wide) + came[3].astype(wide)).astype(low)
    inward = lax.ppermute(first, "context", [(0, 1), (3, 2)])
    across = (first[1:].astype(wide) + inward[1:].astype(wide)).astype(low)
    across = lax.ppermute(across, "context", [(1, 2), (2, 1)])
    outward = (last.astype(wide) + across[1].astype(wide)).astype(low)
    outward = lax.ppermute(outward, "context", [(1, 0), (2, 3)])
    place = lax.axis_index("context")
    inner = (place == 1) | (place == 2)
    return jnp.where(
        inner,
        first[0].astype(wide) + inward[0].astype(wide) + across[0].astype(wide),
        last.astype(wide) + outward.astype(wide),
    )


def call(body, grid, in_specs, out_specs, out_shape, scratch=(), flops=0, moved=0, exps=0):
    return pl.pallas_call(
        body,
        grid=grid,
        in_specs=in_specs,
        out_specs=out_specs,
        out_shape=out_shape,
        scratch_shapes=list(scratch),
        compiler_params=pltpu.CompilerParams(vmem_limit_bytes=VMEM_BYTES),
        cost_estimate=pl.CostEstimate(flops=flops, bytes_accessed=moved, transcendentals=exps),
    )


def turn(vals, cosine, sine):
    return vals * cosine + pltpu.roll(vals, LANES // 2, 1) * sine


def project_body(count, rows_ref, scale_ref, cos_ref, sin_ref, *refs):
    weight_refs, (query_ref, kv_ref, weight_ref) = refs[:count], refs[count:]
    step = pl.program_id(0)
    depth = weight_refs[0].shape[0]
    for k in range(count):
        weight_ref[k * depth : (k + 1) * depth, :] = weight_refs[k][...]
    total = dot_nn(rows_ref[...], weight_ref[...]) * scale_ref[...]
    block = total.shape[1]
    query_steps = QUERY_WIDTH // block
    cosine, sine = cos_ref[...], sin_ref[...]
    groups = [total[:, i * LANES : (i + 1) * LANES] for i in range(block // LANES)]

    @pl.when(step < query_steps)
    def _():
        for i, group in enumerate(groups):
            turned = turn(group, cosine, sine) * HEAD_DIM**-0.5
            query_ref[:, i * LANES : (i + 1) * LANES] = turned.astype(low)

    @pl.when(step >= query_steps)
    def _():
        for i, group in enumerate(groups):
            kept = turn(group, cosine, sine) if i % 2 == 0 else group
            kv_ref[:, i * LANES : (i + 1) * LANES] = kept.astype(low)


def project(rows, scale, cosine, sine, weights):
    tokens, width = rows.shape
    columns = QUERY_WIDTH + 2 * KV_WIDTH
    block = 512
    query_steps = QUERY_WIDTH // block
    depth = weights[0].shape[0]
    whole = lambda shape: pl.BlockSpec(shape, lambda j: (0, 0))
    return call(
        functools.partial(project_body, len(weights)),
        (columns // block,),
        [whole((tokens, width)), whole((tokens, 1)), whole((tokens, LANES)), whole((tokens, LANES))]
        + [pl.BlockSpec((depth, block), lambda j: (0, j))] * len(weights),
        [
            pl.BlockSpec((tokens, block), lambda j: (0, jnp.minimum(j, query_steps - 1))),
            pl.BlockSpec((tokens, block), lambda j: (0, jnp.maximum(j - query_steps, 0))),
        ],
        [
            jax.ShapeDtypeStruct((tokens, QUERY_WIDTH), low),
            jax.ShapeDtypeStruct((tokens, 2 * KV_WIDTH), low),
        ],
        scratch=[pltpu.VMEM((width, block), low)],
        flops=2 * tokens * width * columns,
        moved=2 * width * columns,
    )(rows, scale, cosine, sine, *weights)


def lane_of(shape, axis, which):
    place = lax.broadcasted_iota(jnp.int32, shape, axis)
    return ((place // (HEAD_DIM // 2)) % 2) == which


def stack_heads(block, which):
    keep = lane_of((block.shape[0], LANES), 1, which)
    return jnp.concatenate(
        [
            jnp.where(keep, block[:, g * LANES : (g + 1) * LANES], jnp.zeros((), block.dtype))
            for g in range(GROUPS)
        ],
        axis=0,
    )


def allowed_pairs(key_pos, query_pos):
    seen = key_pos <= query_pos
    return jnp.concatenate([seen] * GROUPS, axis=1)


def turned_block(block):
    return block.astype(wide).T.astype(low)


def attend_body(count, query_ref, key_pos_ref, query_pos_ref, *refs):
    kv_refs, (out_ref, out_low_ref, log_ref) = refs[:count], refs[count:]
    tokens = query_ref.shape[0]
    seen = allowed_pairs(key_pos_ref[...], query_pos_ref[...])
    keys = jnp.concatenate([ref[:, :LANES] for ref in kv_refs], axis=0)
    values = jnp.concatenate([turned_block(ref[:, LANES:]) for ref in kv_refs], axis=1)
    outs = []
    for which in range(2):
        query = stack_heads(query_ref[...], which)
        scores = jnp.where(seen, dot_nt(keys, query), masked_score)
        peak = jnp.max(scores, axis=0, keepdims=True)
        weight = jnp.exp(scores - peak)
        total = jnp.sum(weight, axis=0, keepdims=True)
        outs.append(dot_nn(values, weight.astype(low)) / total)
        log_ref[0, which : which + 1, :] = peak + jnp.log(total)
    first = lane_of(outs[0].shape, 0, 0)
    both = jnp.where(first, outs[0], outs[1]).T
    for g in range(GROUPS):
        piece = both[g * tokens : (g + 1) * tokens, :]
        out_ref[:, g * LANES : (g + 1) * LANES] = piece
        out_low_ref[:, g * LANES : (g + 1) * LANES] = piece.astype(low)


def attend(query, key_pos, query_pos, kv_parts):
    tokens = query.shape[0]
    count = len(kv_parts)
    seq_len = tokens * count
    pairs = pl.BlockSpec((tokens, PAIR_WIDTH), lambda p: (0, p))
    return call(
        functools.partial(attend_body, count),
        (PAIRS,),
        [
            pairs,
            pl.BlockSpec((seq_len, 1), lambda p: (0, 0)),
            pl.BlockSpec((1, tokens), lambda p: (0, 0)),
        ]
        + [pl.BlockSpec((tokens, 2 * LANES), lambda p: (0, p))] * count,
        [pairs, pairs, pl.BlockSpec((1, 2, GROUPS * tokens), lambda p: (p, 0, 0))],
        [
            jax.ShapeDtypeStruct((tokens, QUERY_WIDTH), wide),
            jax.ShapeDtypeStruct((tokens, QUERY_WIDTH), low),
            jax.ShapeDtypeStruct((PAIRS, 2, GROUPS * tokens), wide),
        ],
        flops=16 * HEADS * tokens * seq_len * HEAD_DIM,
        moved=4 * seq_len * KV_WIDTH,
        exps=HEADS * tokens * seq_len,
    )(query, key_pos, query_pos, *kv_parts)


def attend_back_body(count, query_ref, grad_ref, out_ref, log_ref, key_pos_ref, query_pos_ref,
                     scale_ref, cos_ref, sin_ref, *refs):
    kv_refs, grad_query_ref, grad_kv_refs = refs[:count], refs[count], refs[count + 1 :]
    tokens = query_ref.shape[0]
    grads = grad_ref[...]
    product = jnp.concatenate(
        [
            (grads[:, g * LANES : (g + 1) * LANES].astype(wide)
             * out_ref[:, g * LANES : (g + 1) * LANES]).T
            for g in range(GROUPS)
        ],
        axis=1,
    )
    first = lane_of(product.shape, 0, 0)
    delta = [
        jnp.sum(jnp.where(first, product, 0.0), axis=0, keepdims=True),
        jnp.sum(jnp.where(first, 0.0, product), axis=0, keepdims=True),
    ]
    seen = allowed_pairs(key_pos_ref[...], query_pos_ref[...])
    keys = jnp.concatenate([ref[:, :LANES] for ref in kv_refs], axis=0)
    values = jnp.concatenate([ref[:, LANES:] for ref in kv_refs], axis=0)
    keys_turned = jnp.concatenate([turned_block(ref[:, :LANES]) for ref in kv_refs], axis=1)
    grad_key, grad_value, grad_query = None, None, []
    for which in range(2):
        query = stack_heads(query_ref[...], which)
        head = stack_heads(grads, which)
        scores = jnp.where(seen, dot_nt(keys, query), masked_score)
        probs = jnp.exp(scores - log_ref[0, which : which + 1, :])
        grad_probs = dot_nt(values, head)
        grad_scores = (probs * (grad_probs - delta[which])).astype(low)
        part_value = dot_nn(probs.astype(low), head)
        part_key = dot_nn(grad_scores, query)
        grad_query.append(dot_nn(keys_turned, grad_scores))
        grad_value = part_value if grad_value is None else grad_value + part_value
        grad_key = part_key if grad_key is None else grad_key + part_key
    scale, cosine, sine = scale_ref[...], cos_ref[...], sin_ref[...]
    grad_key = turn(grad_key, cosine, -sine) * scale
    grad_value = grad_value * scale
    for k in range(count):
        rows = slice(k * tokens, (k + 1) * tokens)
        grad_kv_refs[k][:, :LANES] = grad_key[rows, :].astype(low)
        grad_kv_refs[k][:, LANES:] = grad_value[rows, :].astype(low)
    first = lane_of(grad_query[0].shape, 0, 0)
    both = (jnp.where(first, grad_query[0], grad_query[1]) * HEAD_DIM**-0.5).T
    for g in range(GROUPS):
        piece = both[g * tokens : (g + 1) * tokens, :]
        back = turn(piece, cosine[:tokens, :], -sine[:tokens, :])
        grad_query_ref[:, g * LANES : (g + 1) * LANES] = (back * scale[:tokens, :]).astype(low)


def attend_back(query, grads, out, logs, key_pos, query_pos, scale, cosine, sine, kv_parts):
    tokens = query.shape[0]
    count = len(kv_parts)
    seq_len = tokens * count
    pairs = pl.BlockSpec((tokens, PAIR_WIDTH), lambda p: (0, p))
    whole = lambda shape: pl.BlockSpec(shape, lambda p: (0, 0))
    part = pl.BlockSpec((tokens, 2 * LANES), lambda p: (0, p))
    results = call(
        functools.partial(attend_back_body, count),
        (PAIRS,),
        [
            pairs,
            pairs,
            pairs,
            pl.BlockSpec((1, 2, GROUPS * tokens), lambda p: (p, 0, 0)),
            whole((seq_len, 1)),
            whole((1, tokens)),
            whole((seq_len, 1)),
            whole((seq_len, LANES)),
            whole((seq_len, LANES)),
        ]
        + [part] * count,
        [pairs] + [part] * count,
        [jax.ShapeDtypeStruct((tokens, QUERY_WIDTH), low)]
        + [jax.ShapeDtypeStruct((tokens, 2 * KV_WIDTH), low)] * count,
        flops=40 * HEADS * tokens * seq_len * HEAD_DIM,
        moved=8 * seq_len * KV_WIDTH,
        exps=HEADS * tokens * seq_len,
    )(query, grads, out, logs, key_pos, query_pos, scale, cosine, sine, *kv_parts)
    return results[0], results[1:]


def hidden_body(rows_ref, grads_ref, gate_ref, weight_ref, hidden_ref, back_ref):
    rows, grads, weight = rows_ref[...], grads_ref[...], gate_ref[0]
    step = 256
    for h in range(0, FF, step):
        gate = dot_nn(rows, weight_ref[0, :, h : h + step])
        up = dot_nn(rows, weight_ref[0, :, FF + h : FF + h + step])
        grad_hidden = dot_nn(grads, weight_ref[0, :, 2 * FF + h : 2 * FF + h + step]) * weight
        sigmoid = 1.0 / (1.0 + jnp.exp(-gate))
        active = gate * sigmoid
        hidden_ref[0, :, h : h + step] = (active * up * weight).astype(low)
        slope = sigmoid + active * (1.0 - sigmoid)
        back_ref[0, :, h : h + step] = (grad_hidden * up * slope).astype(low)
        back_ref[0, :, FF + h : FF + h + step] = (grad_hidden * active).astype(low)


def expert_hidden(rows, grads, gates, weights):
    tokens, width = rows.shape
    experts = weights.shape[0]
    block = min(tokens, 1024)
    return call(
        hidden_body,
        (experts, tokens // block),
        [
            pl.BlockSpec((block, width), lambda e, t: (t, 0)),
            pl.BlockSpec((block, width), lambda e, t: (t, 0)),
            pl.BlockSpec((1, block, 1), lambda e, t: (e, t, 0)),
            pl.BlockSpec((1, width, 3 * FF), lambda e, t: (e, 0, 0)),
        ],
        [
            pl.BlockSpec((1, block, FF), lambda e, t: (e, t, 0)),
            pl.BlockSpec((1, block, 2 * FF), lambda e, t: (e, t, 0)),
        ],
        [
            jax.ShapeDtypeStruct((experts, tokens, FF), low),
            jax.ShapeDtypeStruct((experts, tokens, 2 * FF), low),
        ],
        flops=6 * experts * tokens * width * FF,
        moved=experts * (6 * width * FF + 4 * tokens * width),
        exps=experts * tokens * FF,
    )(rows, grads, gates, weights)


def weight_grad_body(slices, rows_ref, grads_ref, back_ref, hidden_ref, *out_refs):
    step = pl.program_id(1)
    from_rows = dot_nn(rows_ref[...], back_ref[0]).astype(low)
    from_grads = dot_nn(grads_ref[...], hidden_ref[0]).astype(low)
    size = rows_ref.shape[0] // slices
    for half, out_ref in enumerate(out_refs):

        @pl.when(step == half)
        def _():
            for i in range(slices):
                out_ref[i, 0, :, : 2 * FF] = from_rows[i * size : (i + 1) * size, :]
                out_ref[i, 0, :, 2 * FF :] = from_grads[i * size : (i + 1) * size, :]


def expert_weight_grads(rows_turned, grads_turned, back, hidden, slices):
    width, tokens = rows_turned.shape
    experts = back.shape[0]
    block = width // 2
    shape = (slices, experts, block // slices, 3 * FF)
    return call(
        functools.partial(weight_grad_body, slices),
        (experts, 2),
        [
            pl.BlockSpec((block, tokens), lambda e, m: (m, 0)),
            pl.BlockSpec((block, tokens), lambda e, m: (m, 0)),
            pl.BlockSpec((1, tokens, 2 * FF), lambda e, m: (e, 0, 0)),
            pl.BlockSpec((1, tokens, FF), lambda e, m: (e, 0, 0)),
        ],
        [pl.BlockSpec((slices, 1) + shape[2:], lambda e, m: (0, e, 0, 0))] * 2,
        [jax.ShapeDtypeStruct(shape, low)] * 2,
        flops=6 * experts * tokens * width * FF,
        moved=experts * (6 * width * FF + 10 * tokens * width),
    )(rows_turned, grads_turned, back, hidden)


def combine_body(sizes, held, owners, *refs):
    count = len(sizes)
    part_refs, weight_refs, refs = refs[:count], refs[count : 2 * count], refs[2 * count :]
    if held:
        held_ref, refs = refs[0], refs[1:]
    if owners:
        out_refs, total_ref = refs[:owners], refs[owners]
    else:
        total_ref = refs[0]
    step = pl.program_id(0)

    @pl.when(step == 0)
    def _():
        total_ref[...] = held_ref[...] if held else jnp.zeros_like(total_ref)

    start = 0
    for part_ref, weight_ref, size in zip(part_refs, weight_refs, sizes):

        @pl.when((step >= start) & (step < start + size))
        def _():
            total_ref[...] += dot_nt(part_ref[0], weight_ref[0])

        start += size

    if owners:

        @pl.when(step == start - 1)
        def _():
            tokens = out_refs[0].shape[0]
            for k, out_ref in enumerate(out_refs):
                out_ref[...] = total_ref[k * tokens : (k + 1) * tokens, :].astype(low)


def combine(parts, weights, column, held=None, owners=0):
    tokens, depth = parts[0].shape[1:]
    width = weights[0].shape[1]
    sizes = [w.shape[0] for w in weights]
    starts = [sum(sizes[:i]) for i in range(len(sizes))]
    place = lambda e, start, size: jnp.clip(e - start, 0, size - 1)
    part_specs = [
        pl.BlockSpec((1, tokens, depth), lambda e, s=s, n=n: (place(e, s, n), 0, 0))
        for s, n in zip(starts, sizes)
    ]
    weight_specs = [
        pl.BlockSpec((1, width, depth), lambda e, s=s, n=n: (place(e, s, n), 0, column))
        for s, n in zip(starts, sizes)
    ]
    total = pl.BlockSpec((tokens, width), lambda e: (0, 0), pipeline_mode=pl.Buffered(1))
    block = pl.BlockSpec((tokens // max(owners, 1), width), lambda e: (0, 0))
    return call(
        functools.partial(combine_body, sizes, held is not None, owners),
        (sum(sizes),),
        part_specs + weight_specs + ([] if held is None else [total]),
        [block] * owners if owners else total,
        [jax.ShapeDtypeStruct((tokens // owners, width), low)] * owners
        if owners
        else jax.ShapeDtypeStruct((tokens, width), wide),
        scratch=[pltpu.VMEM((tokens, width), wide)] if owners else [],
        flops=2 * sum(sizes) * tokens * width * depth,
        moved=2 * sum(sizes) * width * depth,
    )(*parts, *weights, *([] if held is None else [held]))


def body(
    layer_input,
    cotangent,
    block_order,
    routes,
    route_gates,
    joined_weight,
    joined_first,
    joined_second,
    output_weight,
    output_first,
    output_second,
    norm_gains,
    gains_first,
    gains_second,
    expand_weight,
    expand_first,
    expand_second,
    contract_weight,
    contract_first,
    contract_second,
):
    experts_dev = expand_weight.shape[0]
    owners = lax.axis_size("expert")
    contexts = lax.axis_size("context")
    cores = lax.axis_size("dp")
    experts = experts_dev * owners
    tokens = layer_input.shape[1]
    width = layer_input.shape[2]
    half_block = tokens // 2
    slice_rows = joined_weight.shape[0]
    own_expert = lax.axis_index("expert")
    own_context = lax.axis_index("context")
    own_core = lax.axis_index("dp")

    gain_rows = norm_gains.astype(low).astype(wide).T
    joined_low = joined_weight.astype(low)
    joined_shard = reorder_columns((gain_rows[:, :1] * joined_low.astype(wide)).astype(low)).astype(low)
    joined_line = spread_line(joined_shard)
    joined_mine = spread(joined_line, "expert")
    joined_parts = spread_rest(joined_mine)
    query_mat = order_matrix(GROUPS)
    output_shard = jnp.einsum(
        "pod,on->dpn",
        output_weight.astype(low).reshape(PAIRS, PAIR_WIDTH, slice_rows),
        query_mat,
        preferred_element_type=wide,
    ).reshape(slice_rows, QUERY_WIDTH).astype(low)
    output_shard = jnp.concatenate(
        [output_shard, jnp.broadcast_to(gain_rows[:, 1:].astype(low), (slice_rows, LANES))], axis=1
    )
    output_line = spread_line(after(output_shard, joined_line))
    output_parts = spread_rest(spread(after(output_line, *joined_mine), "expert"))

    bounds = [0, 2, 4, experts_dev]
    chunks = list(zip(bounds[:-1], bounds[1:]))
    expert_low = [
        jnp.concatenate(
            [
                expand_weight[a:b].astype(low),
                jnp.swapaxes(contract_weight[a:b].astype(low), 1, 2),
            ],
            axis=2,
        )
        for a, b in chunks
    ]
    expert_low[0] = after(expert_low[0], joined_line)
    expert_full = [
        lax.all_gather(shard, ("context", "dp"), axis=1, tiled=True) for shard in expert_low
    ]

    ar = lambda n: jnp.arange(n, dtype=jnp.int32)
    to_relative = (
        ((own_expert ^ ar(owners))[None, :, None] * contexts + (own_context ^ ar(contexts))[None, None, :])
        * cores
        + (own_core ^ ar(cores))[:, None, None]
    ).reshape(-1)
    to_absolute = (
        (own_core ^ ar(cores))[None, None, :] * owners + (own_expert ^ ar(owners))[:, None, None]
    ) * contexts + (own_context ^ ar(contexts))[None, :, None]
    to_absolute = to_absolute.reshape(-1)
    slices = owners * contexts * cores

    def pick_rows(rows, index):
        return jnp.take(
            rows.reshape(slices, slice_rows, -1), index, axis=0, mode="clip", unique_indices=True
        ).reshape(rows.shape)

    hits = routes[0][:, :, None] == ar(experts)[None, None, :]
    gate_table = jnp.sum(jnp.where(hits, route_gates[0][:, :, None], 0.0), axis=1)
    gate_table = gate_table.reshape(tokens, owners, experts_dev)
    gate_parts = [
        lax.dynamic_index_in_dim(gate_table, own_expert ^ k, axis=1, keepdims=False)
        for k in range(owners)
    ]
    gates = jnp.concatenate(
        [gate_parts[0]] + [swap(gate_parts[k], "expert", k) for k in range(1, owners)], axis=0
    )
    gates = gates.T[:, :, None]
    cotangent_rows = after(cotangent[0], *joined_mine)
    out_grads = jnp.concatenate(spread(cotangent_rows, "expert"), axis=0)

    on_line = contexts == 4 and cores == 2
    if on_line:
        along = line_order(own_context)
        grad_slices = (along[None, :] * cores + (own_core ^ ar(cores))[:, None]).reshape(-1)
    else:
        grad_slices = None

    def turned_rows(block):
        turned = block.T
        if on_line:
            shape = (contexts * cores, width // (contexts * cores), block.shape[0])
            turned = jnp.take(turned.reshape(shape), grad_slices, axis=0, mode="clip")
        return turned.reshape(width, block.shape[0])

    out_grads_turned = turned_rows(out_grads)

    order = block_order[0]
    offsets = ar(half_block)

    def places_of(index):
        mine = lax.dynamic_slice_in_dim(order, 2 * index, 2)
        return (mine[:, None] * half_block + offsets[None, :]).reshape(-1)

    query_pos = places_of(own_context)
    key_pos = jnp.concatenate([places_of(own_context ^ k) for k in range(contexts)])
    half = HEAD_DIM // 2
    freq = jnp.exp(ar(half).astype(wide) * (2.0 / HEAD_DIM) * -math.log(10000.0))
    angle = key_pos.astype(wide)[:, None] * freq[None, :]
    cosine = jnp.tile(jnp.cos(angle), (1, 4))
    sine = jnp.sin(angle)
    sine = jnp.concatenate([-sine, -sine, sine, sine], axis=1)
    query_cosine, query_sine = cosine[:tokens], sine[:tokens]

    low_input = layer_input[0]
    resid = low_input.astype(wide)
    scale_one = lax.rsqrt(jnp.mean(resid * resid, axis=-1, keepdims=True) + norm_eps)
    unit_one = resid * scale_one
    input_turned = pick_rows(low_input.T, to_relative)
    input_relative = input_turned.T
    query, kv = project(input_relative, scale_one, query_cosine, query_sine, joined_parts)
    kv_parts = spread(kv, "context")
    attended_wide, attended, logs = attend(query, key_pos[:, None], query_pos[None, :], kv_parts)

    output_pack = pick_rows(jnp.concatenate(output_parts, axis=0), to_absolute)
    output_turned = output_pack[:, :QUERY_WIDTH]
    gain_two = output_pack[:, QUERY_WIDTH].astype(wide)[None, :]
    middle = resid + dot_nt(attended, output_turned)
    scale_two = lax.rsqrt(jnp.mean(middle * middle, axis=-1, keepdims=True) + norm_eps)
    unit_two = middle * scale_two
    normed_two = (unit_two * gain_two).astype(low)

    rows = jnp.concatenate(spread(normed_two, "expert"), axis=0)
    rows_turned = turned_rows(rows)
    hiddens, backs, expert_grads = [], [], []
    held = None
    for (a, b), weights in zip(chunks, expert_full):
        hidden, back = expert_hidden(rows, out_grads, gates[a:b], weights)
        hiddens.append(hidden)
        backs.append(back)
        held = combine([back], [weights], 0, held, owners if b == experts_dev else 0)
        if on_line:
            own, other = expert_weight_grads(rows_turned, out_grads_turned, back, hidden, contexts)
            expert_grads.append(sum_on_line(own, other))
        else:
            both = expert_weight_grads(rows_turned, out_grads_turned, back, hidden, 1)
            weight_grads = jnp.concatenate([part[0] for part in both], axis=1)
            expert_grads.append(
                lax.psum_scatter(
                    weight_grads, ("context", "dp"), scatter_dimension=1, tiled=True
                ).astype(wide)
            )

    def to_tokens(parts):
        total = parts[0].astype(wide)
        for k in range(1, owners):
            total = total + swap(parts[k], "expert", k).astype(wide)
        return total

    grad_normed_two = to_tokens(held)
    mixture = to_tokens(combine(hiddens, expert_full, 2, None, owners))
    output = (middle + mixture).astype(low)

    grad_out = cotangent[0].astype(wide)
    grad_unit_two = grad_normed_two * gain_two
    gain_grad_two = jnp.sum(grad_normed_two * unit_two, axis=0)
    grad_middle = grad_out + scale_two * (
        grad_unit_two - unit_two * jnp.mean(grad_unit_two * unit_two, axis=-1, keepdims=True)
    )
    grad_proj = grad_middle.astype(low)
    grad_attended = dot_nn(grad_proj, output_turned).astype(low)
    sequence = jnp.concatenate(spread(after(low_input, normed_two), "context"), axis=0)
    sequence_wide = sequence.astype(wide)
    sequence_scale = lax.rsqrt(
        jnp.mean(sequence_wide * sequence_wide, axis=-1, keepdims=True) + norm_eps
    )
    sequence_turned = pick_rows(sequence.T, to_relative)
    grad_query, grad_kv = attend_back(
        query, grad_attended, attended_wide, logs, key_pos[:, None], query_pos[None, :],
        sequence_scale, cosine, sine, kv_parts,
    )
    grad_kv_all = jnp.concatenate(grad_kv, axis=0)

    relative = (owners, contexts, slice_rows)
    split = width // cores
    proj_turned = pick_rows(grad_proj.T, to_relative)
    gain_column = pick_rows(gain_grad_two[:, None], to_relative).astype(low)

    def output_grads(part):
        grads = dot_nn(proj_turned[part], attended).astype(low)
        extra = jnp.broadcast_to(gain_column[part], (split, LANES))
        return jnp.concatenate([grads, extra], axis=1).reshape(*relative, -1)

    def joined_grads(part):
        grads = jnp.concatenate(
            [
                dot_nn(input_turned[part], grad_query).astype(low),
                dot_nn(sequence_turned[part], grad_kv_all).astype(low),
            ],
            axis=1,
        )
        return grads.reshape(*relative, -1)

    sum_output = sum_to_owners(*[output_grads(slice(k * split, (k + 1) * split)) for k in range(cores)])
    sum_joined = sum_to_owners(*[joined_grads(slice(k * split, (k + 1) * split)) for k in range(cores)])

    own_grad_kv = grad_kv[0].astype(wide)
    for k in range(1, contexts):
        own_grad_kv = own_grad_kv + swap(grad_kv[k], "context", k).astype(wide)
    grad_joined = jnp.concatenate([grad_query, own_grad_kv.astype(low)], axis=1)
    scaled_grad = jnp.concatenate([dot_nt(part, grad_joined) for part in joined_parts], axis=0)
    scaled_grad = pick_rows(scaled_grad, to_absolute).T
    grad_input = (
        grad_middle
        + scaled_grad
        - unit_one * jnp.mean(scaled_grad * unit_one, axis=-1, keepdims=True)
    ).astype(low)

    unit_grads = reorder_columns(sum_joined, back=True)
    sum_joined = gain_rows[:, :1] * unit_grads
    sum_gain_one = jnp.sum(joined_low.astype(wide) * unit_grads, axis=1)
    sum_gains = jnp.stack([sum_gain_one, sum_output[:, QUERY_WIDTH]], axis=0)
    sum_output_weight = jnp.einsum(
        "on,dpn->pod",
        query_mat.astype(wide),
        sum_output[:, :QUERY_WIDTH].reshape(slice_rows, PAIRS, PAIR_WIDTH),
        precision=lax.Precision.HIGHEST,
        preferred_element_type=wide,
    ).reshape(QUERY_WIDTH, slice_rows)
    joined_new = adamw(
        joined_weight, joined_first, joined_second, sum_joined, rate_joined, decay_rate
    )
    output_new = adamw(
        output_weight, output_first, output_second, sum_output_weight, rate_output, decay_rate
    )
    gains_new = adamw(norm_gains, gains_first, gains_second, sum_gains, rate_gains, 0.0)
    sum_experts = jnp.concatenate(expert_grads, axis=0)
    expand_new = adamw(
        expand_weight, expand_first, expand_second, sum_experts[:, :, : 2 * FF], rate_expand, decay_rate
    )
    contract_new = adamw(
        contract_weight,
        contract_first,
        contract_second,
        jnp.swapaxes(sum_experts[:, :, 2 * FF :], 1, 2),
        rate_contract,
        decay_rate,
    )
    return (
        output.reshape(1, tokens, width),
        grad_input.reshape(1, tokens, width),
        *joined_new,
        *output_new,
        *gains_new,
        *expand_new,
        *contract_new,
    )


def solution(mesh):
    rows = P(("expert", "dp"), "context", None)
    joined = P(("expert", "context", "dp"), None)
    column = P(None, ("expert", "context", "dp"))
    expand = P("expert", ("context", "dp"), None)
    contract = P("expert", None, ("context", "dp"))
    placed = (
        (rows, rows, P(("expert", "dp"), None), rows, rows)
        + (joined,) * 3
        + (column,) * 6
        + (expand,) * 3
        + (contract,) * 3
    )
    return jax.shard_map(
        body,
        mesh=mesh,
        in_specs=placed,
        out_specs=(rows, rows) + placed[5:],
        check_vma=False,
    )
```

```python
import functools
import math

import jax
import jax.numpy as jnp
import numpy as np
from jax import lax
from jax.experimental import pallas as pl
from jax.experimental.pallas import tpu as pltpu
from jax.sharding import PartitionSpec as P

HEADS = 24
KV_HEADS = 8
HEAD_DIM = 64
FF = 512
TOP = 8
STEP = 10
GROUPS = HEADS // KV_HEADS
PAIRS = KV_HEADS // 2
QUERY_WIDTH = HEADS * HEAD_DIM
KV_WIDTH = KV_HEADS * HEAD_DIM
PAIR_WIDTH = 2 * GROUPS * HEAD_DIM
LANES = 128
VMEM_BYTES = 60 * 1024 * 1024

norm_eps = 1e-06
beta_one = 0.9
beta_two = 0.95
adam_eps = 1e-08
decay_rate = 0.1
rate_joined = 0.08
rate_output = 0.6
rate_gains = 0.6
rate_expand = 0.08
rate_contract = 0.5
masked_score = -1e30

low = jnp.bfloat16
wide = jnp.float32


def adamw(weight, first, second, grad, rate, decay):
    first_new = beta_one * first + (1.0 - beta_one) * grad
    second_new = beta_two * second + (1.0 - beta_two) * grad * grad
    first_hat = first_new / (1.0 - beta_one**STEP)
    second_hat = second_new / (1.0 - beta_two**STEP)
    weight_new = weight - rate * (first_hat / (jnp.sqrt(second_hat) + adam_eps) + decay * weight)
    return (weight_new, first_new, second_new)


def dot_nn(left, right):
    return lax.dot_general(left, right, (((1,), (0,)), ((), ())), preferred_element_type=wide)


def dot_nt(left, right):
    return lax.dot_general(left, right, (((1,), (1,)), ((), ())), preferred_element_type=wide)


def pair_order(groups):
    half = HEAD_DIM // 2
    old = np.arange(2 * groups * HEAD_DIM).reshape(2, groups, 2, half)
    return old.transpose(1, 2, 0, 3).reshape(-1)


def order_matrix(groups):
    order = pair_order(groups)
    size = order.shape[0]
    return jnp.asarray(np.arange(size)[:, None] == order[None, :], dtype=low)


def reorder_columns(rows, back=False):
    count = rows.shape[0]
    query_mat = order_matrix(GROUPS)
    key_mat = order_matrix(1)
    kv = rows[:, QUERY_WIDTH:]
    if back:
        query_mat = query_mat.T
        key_mat = key_mat.T
        kv = jnp.swapaxes(kv.reshape(count, PAIRS, 2, LANES), 1, 2)
    else:
        kv = jnp.swapaxes(kv.reshape(count, 2, PAIRS, LANES), 1, 2)
    exact = lax.Precision.HIGHEST if rows.dtype == wide else None
    query = jnp.einsum(
        "rpo,on->rpn",
        rows[:, :QUERY_WIDTH].reshape(count, PAIRS, PAIR_WIDTH),
        query_mat.astype(rows.dtype),
        precision=exact,
        preferred_element_type=wide,
    ).reshape(count, QUERY_WIDTH)
    others = jnp.einsum(
        "rpo,on->rpn",
        kv.reshape(count, 2 * PAIRS, LANES),
        key_mat.astype(rows.dtype),
        precision=exact,
        preferred_element_type=wide,
    ).reshape(count, 2 * KV_WIDTH)
    return jnp.concatenate([query, others], axis=1)


def swap(block, axis, step):
    count = lax.axis_size(axis)
    return lax.ppermute(block, axis, [(i, i ^ step) for i in range(count)])


def spread(block, axis):
    return [block] + [swap(block, axis, k) for k in range(1, lax.axis_size(axis))]


def after(value, *others):
    return lax.optimization_barrier((value, *others))[0]


def all_after(values, *others):
    count = len(values)
    return list(lax.optimization_barrier((*values, *others))[:count])


def share(block, axis):
    return trade(jnp.broadcast_to(block[None], (lax.axis_size(axis), *block.shape)), axis)


def trade(blocks, axis):
    return lax.all_to_all(blocks, axis, split_axis=0, concat_axis=0, tiled=True)


def in_order(parts, own):
    rows = parts[0].shape[0]
    joined = jnp.zeros((len(parts) * rows, *parts[0].shape[1:]), parts[0].dtype)
    for k, part in enumerate(parts):
        joined = lax.dynamic_update_slice_in_dim(joined, part, (own ^ k) * rows, 0)
    return joined


class OwnerSum:
    def __init__(self, own, other):
        self.own = own
        self.came = swap(other, "dp", 1)

    def spread_experts(self, *others):
        came = after(self.came, *others)
        both = [
            (self.own[k].astype(wide) + came[k].astype(wide)).astype(low)
            for k in range(self.own.shape[0])
        ]
        self.parts = [both[0]] + [swap(both[k], "expert", k) for k in range(1, len(both))]
        return both

    def spread_contexts(self, *others):
        parts = all_after(self.parts, *others)
        total = functools.reduce(jnp.add, [part.astype(wide) for part in parts])
        column = [total[k].astype(low) for k in range(1, total.shape[0])]
        self.parts = [total[0]] + [swap(part, "context", k + 1) for k, part in enumerate(column)]
        return column

    def finish(self, *others):
        parts = all_after(self.parts, *others)
        return functools.reduce(jnp.add, [part.astype(wide) for part in parts])


def line_order(own):
    near = jnp.array([1, 2, 3, 0], jnp.int32)
    return jnp.where(own < 2, near, 3 - near)


class LineSum:
    def __init__(self, own, other):
        self.own = own
        self.came = swap(other, "dp", 1)

    def inward(self, *others):
        came = after(self.came, *others)
        first = (self.own[:3].astype(wide) + came[:3].astype(wide)).astype(low)
        self.last = (self.own[3].astype(wide) + came[3].astype(wide)).astype(low)
        self.first = first
        self.from_end = lax.ppermute(first, "context", [(0, 1), (3, 2)])
        return first

    def across(self, *others):
        self.from_end = after(self.from_end, *others)
        both = (self.first[1:].astype(wide) + self.from_end[1:].astype(wide)).astype(low)
        self.from_inner = lax.ppermute(both, "context", [(1, 2), (2, 1)])
        return both

    def outward(self, *others):
        self.from_inner = after(self.from_inner, *others)
        near = (self.last.astype(wide) + self.from_inner[1].astype(wide)).astype(low)
        self.to_end = lax.ppermute(near, "context", [(1, 0), (2, 3)])
        return near

    def finish(self, *others):
        to_end = after(self.to_end, *others)
        place = lax.axis_index("context")
        inner = (place == 1) | (place == 2)
        return jnp.where(
            inner,
            self.first[0].astype(wide) + self.from_end[0].astype(wide)
            + self.from_inner[0].astype(wide),
            self.last.astype(wide) + to_end.astype(wide),
        )


def call(body, grid, in_specs, out_specs, out_shape, scratch=()):
    return pl.pallas_call(
        body,
        grid=grid,
        in_specs=in_specs,
        out_specs=out_specs,
        out_shape=out_shape,
        scratch_shapes=list(scratch),
        compiler_params=pltpu.CompilerParams(vmem_limit_bytes=VMEM_BYTES),
        cost_estimate=pl.CostEstimate(flops=1, bytes_accessed=1, transcendentals=0),
    )


def turn(vals, cosine, sine):
    return vals * cosine + pltpu.roll(vals, LANES // 2, 1) * sine


def project_body(count, rows_ref, scale_ref, cos_ref, sin_ref, *refs):
    weight_refs, (query_ref, kv_ref, weight_ref) = refs[:count], refs[count:]
    step = pl.program_id(0)
    depth = weight_refs[0].shape[0]
    for k in range(count):
        weight_ref[k * depth : (k + 1) * depth, :] = weight_refs[k][...]
    total = dot_nn(rows_ref[...], weight_ref[...]) * scale_ref[...]
    block = total.shape[1]
    query_steps = QUERY_WIDTH // block
    cosine, sine = cos_ref[...], sin_ref[...]
    groups = [total[:, i * LANES : (i + 1) * LANES] for i in range(block // LANES)]

    @pl.when(step < query_steps)
    def _():
        for i, group in enumerate(groups):
            turned = turn(group, cosine, sine) * HEAD_DIM**-0.5
            query_ref[:, i * LANES : (i + 1) * LANES] = turned.astype(low)

    @pl.when(step >= query_steps)
    def _():
        for i, group in enumerate(groups):
            kept = turn(group, cosine, sine) if i % 2 == 0 else group
            kv_ref[:, i * LANES : (i + 1) * LANES] = kept.astype(low)


def project(rows, scale, cosine, sine, weights):
    tokens, width = rows.shape
    columns = QUERY_WIDTH + 2 * KV_WIDTH
    block = 512
    query_steps = QUERY_WIDTH // block
    depth = weights[0].shape[0]
    whole = lambda shape: pl.BlockSpec(shape, lambda j: (0, 0))
    return call(
        functools.partial(project_body, len(weights)),
        (columns // block,),
        [whole((tokens, width)), whole((tokens, 1)), whole((tokens, LANES)), whole((tokens, LANES))]
        + [pl.BlockSpec((depth, block), lambda j: (0, j))] * len(weights),
        [
            pl.BlockSpec((tokens, block), lambda j: (0, jnp.minimum(j, query_steps - 1))),
            pl.BlockSpec((tokens, block), lambda j: (0, jnp.maximum(j - query_steps, 0))),
        ],
        [
            jax.ShapeDtypeStruct((tokens, QUERY_WIDTH), low),
            jax.ShapeDtypeStruct((tokens, 2 * KV_WIDTH), low),
        ],
        scratch=[pltpu.VMEM((width, block), low)],
    )(rows, scale, cosine, sine, *weights)


def lane_of(shape, axis, which):
    place = lax.broadcasted_iota(jnp.int32, shape, axis)
    return ((place // (HEAD_DIM // 2)) % 2) == which


def stack_heads(block, which):
    keep = lane_of((block.shape[0], LANES), 1, which)
    return jnp.concatenate(
        [
            jnp.where(keep, block[:, g * LANES : (g + 1) * LANES], jnp.zeros((), block.dtype))
            for g in range(GROUPS)
        ],
        axis=0,
    )


def allowed_pairs(key_pos, query_pos):
    seen = key_pos <= query_pos
    return jnp.concatenate([seen] * GROUPS, axis=1)


def turned_block(block):
    return block.astype(wide).T.astype(low)


def attend_body(count, query_ref, key_pos_ref, query_pos_ref, *refs):
    kv_refs, (out_ref, out_low_ref, log_ref) = refs[:count], refs[count:]
    tokens = query_ref.shape[0]
    seen = allowed_pairs(key_pos_ref[...], query_pos_ref[...])
    keys = jnp.concatenate([ref[:, :LANES] for ref in kv_refs], axis=0)
    values = jnp.concatenate([turned_block(ref[:, LANES:]) for ref in kv_refs], axis=1)
    outs = []
    for which in range(2):
        query = stack_heads(query_ref[...], which)
        scores = jnp.where(seen, dot_nt(keys, query), masked_score)
        peak = jnp.max(scores, axis=0, keepdims=True)
        weight = jnp.exp(scores - peak)
        total = jnp.sum(weight, axis=0, keepdims=True)
        outs.append(dot_nn(values, weight.astype(low)) / total)
        log_ref[0, which : which + 1, :] = peak + jnp.log(total)
    first = lane_of(outs[0].shape, 0, 0)
    both = jnp.where(first, outs[0], outs[1]).T
    for g in range(GROUPS):
        piece = both[g * tokens : (g + 1) * tokens, :]
        out_ref[:, g * LANES : (g + 1) * LANES] = piece
        out_low_ref[:, g * LANES : (g + 1) * LANES] = piece.astype(low)


def attend(query, key_pos, query_pos, kv_parts):
    tokens = query.shape[0]
    count = len(kv_parts)
    seq_len = tokens * count
    pairs = pl.BlockSpec((tokens, PAIR_WIDTH), lambda p: (0, p))
    return call(
        functools.partial(attend_body, count),
        (PAIRS,),
        [
            pairs,
            pl.BlockSpec((seq_len, 1), lambda p: (0, 0)),
            pl.BlockSpec((1, tokens), lambda p: (0, 0)),
        ]
        + [pl.BlockSpec((tokens, 2 * LANES), lambda p: (0, p))] * count,
        [pairs, pairs, pl.BlockSpec((1, 2, GROUPS * tokens), lambda p: (p, 0, 0))],
        [
            jax.ShapeDtypeStruct((tokens, QUERY_WIDTH), wide),
            jax.ShapeDtypeStruct((tokens, QUERY_WIDTH), low),
            jax.ShapeDtypeStruct((PAIRS, 2, GROUPS * tokens), wide),
        ],
    )(query, key_pos, query_pos, *kv_parts)


def attend_back_body(count, query_ref, grad_ref, out_ref, log_ref, key_pos_ref, query_pos_ref,
                     scale_ref, cos_ref, sin_ref, *refs):
    kv_refs, (grad_query_ref, grad_kv_ref) = refs[:count], refs[count:]
    tokens = query_ref.shape[0]
    grads = grad_ref[...]
    product = jnp.concatenate(
        [
            (grads[:, g * LANES : (g + 1) * LANES].astype(wide)
             * out_ref[:, g * LANES : (g + 1) * LANES]).T
            for g in range(GROUPS)
        ],
        axis=1,
    )
    first = lane_of(product.shape, 0, 0)
    delta = [
        jnp.sum(jnp.where(first, product, 0.0), axis=0, keepdims=True),
        jnp.sum(jnp.where(first, 0.0, product), axis=0, keepdims=True),
    ]
    seen = allowed_pairs(key_pos_ref[...], query_pos_ref[...])
    keys = jnp.concatenate([ref[:, :LANES] for ref in kv_refs], axis=0)
    values = jnp.concatenate([ref[:, LANES:] for ref in kv_refs], axis=0)
    keys_turned = jnp.concatenate([turned_block(ref[:, :LANES]) for ref in kv_refs], axis=1)
    grad_key, grad_value, grad_query = None, None, []
    for which in range(2):
        query = stack_heads(query_ref[...], which)
        head = stack_heads(grads, which)
        scores = jnp.where(seen, dot_nt(keys, query), masked_score)
        probs = jnp.exp(scores - log_ref[0, which : which + 1, :])
        grad_probs = dot_nt(values, head)
        grad_scores = (probs * (grad_probs - delta[which])).astype(low)
        part_value = dot_nn(probs.astype(low), head)
        part_key = dot_nn(grad_scores, query)
        grad_query.append(dot_nn(keys_turned, grad_scores))
        grad_value = part_value if grad_value is None else grad_value + part_value
        grad_key = part_key if grad_key is None else grad_key + part_key
    scale, cosine, sine = scale_ref[...], cos_ref[...], sin_ref[...]
    grad_key = turn(grad_key, cosine, -sine) * scale
    grad_value = grad_value * scale
    for k in range(count):
        rows = slice(k * tokens, (k + 1) * tokens)
        grad_kv_ref[k, :, :LANES] = grad_key[rows, :].astype(low)
        grad_kv_ref[k, :, LANES:] = grad_value[rows, :].astype(low)
    first = lane_of(grad_query[0].shape, 0, 0)
    both = (jnp.where(first, grad_query[0], grad_query[1]) * HEAD_DIM**-0.5).T
    for g in range(GROUPS):
        piece = both[g * tokens : (g + 1) * tokens, :]
        back = turn(piece, cosine[:tokens, :], -sine[:tokens, :])
        grad_query_ref[:, g * LANES : (g + 1) * LANES] = (back * scale[:tokens, :]).astype(low)


def attend_back(query, grads, out, logs, key_pos, query_pos, scale, cosine, sine, kv_parts):
    tokens = query.shape[0]
    count = len(kv_parts)
    seq_len = tokens * count
    pairs = pl.BlockSpec((tokens, PAIR_WIDTH), lambda p: (0, p))
    whole = lambda shape: pl.BlockSpec(shape, lambda p: (0, 0))
    part = pl.BlockSpec((tokens, 2 * LANES), lambda p: (0, p))
    return call(
        functools.partial(attend_back_body, count),
        (PAIRS,),
        [
            pairs,
            pairs,
            pairs,
            pl.BlockSpec((1, 2, GROUPS * tokens), lambda p: (p, 0, 0)),
            whole((seq_len, 1)),
            whole((1, tokens)),
            whole((seq_len, 1)),
            whole((seq_len, LANES)),
            whole((seq_len, LANES)),
        ]
        + [part] * count,
        [pairs, pl.BlockSpec((count, tokens, 2 * LANES), lambda p: (0, 0, p))],
        [
            jax.ShapeDtypeStruct((tokens, QUERY_WIDTH), low),
            jax.ShapeDtypeStruct((count, tokens, 2 * KV_WIDTH), low),
        ],
    )(query, grads, out, logs, key_pos, query_pos, scale, cosine, sine, *kv_parts)


def hidden_body(rows_ref, grads_ref, gate_ref, weight_ref, hidden_ref, back_ref):
    rows, grads, weight = rows_ref[...], grads_ref[...], gate_ref[0]
    step = 256
    for h in range(0, FF, step):
        gate = dot_nn(rows, weight_ref[0, :, h : h + step])
        up = dot_nn(rows, weight_ref[0, :, FF + h : FF + h + step])
        grad_hidden = dot_nn(grads, weight_ref[0, :, 2 * FF + h : 2 * FF + h + step]) * weight
        sigmoid = 1.0 / (1.0 + jnp.exp(-gate))
        active = gate * sigmoid
        hidden_ref[0, :, h : h + step] = (active * up * weight).astype(low)
        slope = sigmoid + active * (1.0 - sigmoid)
        back_ref[0, :, h : h + step] = (grad_hidden * up * slope).astype(low)
        back_ref[0, :, FF + h : FF + h + step] = (grad_hidden * active).astype(low)


def expert_hidden(rows, grads, gates, weights):
    tokens, width = rows.shape
    experts = weights.shape[0]
    block = min(tokens, 1024)
    return call(
        hidden_body,
        (experts, tokens // block),
        [
            pl.BlockSpec((block, width), lambda e, t: (t, 0)),
            pl.BlockSpec((block, width), lambda e, t: (t, 0)),
            pl.BlockSpec((1, block, 1), lambda e, t: (e, t, 0)),
            pl.BlockSpec((1, width, 3 * FF), lambda e, t: (e, 0, 0)),
        ],
        [
            pl.BlockSpec((1, block, FF), lambda e, t: (e, t, 0)),
            pl.BlockSpec((1, block, 2 * FF), lambda e, t: (e, t, 0)),
        ],
        [
            jax.ShapeDtypeStruct((experts, tokens, FF), low),
            jax.ShapeDtypeStruct((experts, tokens, 2 * FF), low),
        ],
    )(rows, grads, gates, weights)


def weight_grad_body(slices, rows_ref, grads_ref, back_ref, hidden_ref, *out_refs):
    step = pl.program_id(1)
    from_rows = dot_nn(rows_ref[...], back_ref[0]).astype(low)
    from_grads = dot_nn(grads_ref[...], hidden_ref[0]).astype(low)
    size = rows_ref.shape[0] // slices
    for half, out_ref in enumerate(out_refs):

        @pl.when(step == half)
        def _():
            for i in range(slices):
                out_ref[i, 0, :, : 2 * FF] = from_rows[i * size : (i + 1) * size, :]
                out_ref[i, 0, :, 2 * FF :] = from_grads[i * size : (i + 1) * size, :]


def expert_weight_grads(rows_turned, grads_turned, back, hidden, slices):
    width, tokens = rows_turned.shape
    experts = back.shape[0]
    block = width // 2
    shape = (slices, experts, block // slices, 3 * FF)
    return call(
        functools.partial(weight_grad_body, slices),
        (experts, 2),
        [
            pl.BlockSpec((block, tokens), lambda e, m: (m, 0)),
            pl.BlockSpec((block, tokens), lambda e, m: (m, 0)),
            pl.BlockSpec((1, tokens, 2 * FF), lambda e, m: (e, 0, 0)),
            pl.BlockSpec((1, tokens, FF), lambda e, m: (e, 0, 0)),
        ],
        [pl.BlockSpec((slices, 1) + shape[2:], lambda e, m: (0, e, 0, 0))] * 2,
        [jax.ShapeDtypeStruct(shape, low)] * 2,
    )(rows_turned, grads_turned, back, hidden)


def combine_body(sizes, held, last, *refs):
    count = len(sizes)
    part_refs, weight_refs, refs = refs[:count], refs[count : 2 * count], refs[2 * count :]
    if held:
        held_ref, refs = refs[0], refs[1:]
    out_ref, total_ref = refs[0], refs[-1]
    step = pl.program_id(0)

    @pl.when(step == 0)
    def _():
        total_ref[...] = held_ref[...] if held else jnp.zeros_like(total_ref)

    start = 0
    for part_ref, weight_ref, size in zip(part_refs, weight_refs, sizes):

        @pl.when((step >= start) & (step < start + size))
        def _():
            total_ref[...] += dot_nt(part_ref[0], weight_ref[0])

        start += size

    if last:

        @pl.when(step == start - 1)
        def _():
            out_ref[...] = total_ref[...].astype(low)


def combine(parts, weights, column, held=None, last=True):
    tokens, depth = parts[0].shape[1:]
    width = weights[0].shape[1]
    sizes = [w.shape[0] for w in weights]
    starts = [sum(sizes[:i]) for i in range(len(sizes))]
    place = lambda e, start, size: jnp.clip(e - start, 0, size - 1)
    part_specs = [
        pl.BlockSpec((1, tokens, depth), lambda e, s=s, n=n: (place(e, s, n), 0, 0))
        for s, n in zip(starts, sizes)
    ]
    weight_specs = [
        pl.BlockSpec((1, width, depth), lambda e, s=s, n=n: (place(e, s, n), 0, column))
        for s, n in zip(starts, sizes)
    ]
    total = pl.BlockSpec((tokens, width), lambda e: (0, 0), pipeline_mode=pl.Buffered(1))
    return call(
        functools.partial(combine_body, sizes, held is not None, last),
        (sum(sizes),),
        part_specs + weight_specs + ([] if held is None else [total]),
        total,
        jax.ShapeDtypeStruct((tokens, width), low if last else wide),
        scratch=[pltpu.VMEM((tokens, width), wide)] if last else [],
    )(*parts, *weights, *([] if held is None else [held]))


def body(
    layer_input,
    cotangent,
    block_order,
    routes,
    route_gates,
    joined_weight,
    joined_first,
    joined_second,
    output_weight,
    output_first,
    output_second,
    norm_gains,
    gains_first,
    gains_second,
    expand_weight,
    expand_first,
    expand_second,
    contract_weight,
    contract_first,
    contract_second,
):
    experts_dev = expand_weight.shape[0]
    owners = lax.axis_size("expert")
    contexts = lax.axis_size("context")
    cores = lax.axis_size("dp")
    experts = experts_dev * owners
    tokens = layer_input.shape[1]
    width = layer_input.shape[2]
    half_block = tokens // 2
    slice_rows = joined_weight.shape[0]
    own_expert = lax.axis_index("expert")
    own_context = lax.axis_index("context")
    own_core = lax.axis_index("dp")

    gain_rows = norm_gains.astype(low).astype(wide).T
    joined_low = joined_weight.astype(low)
    joined_shard = reorder_columns((gain_rows[:, :1] * joined_low.astype(wide)).astype(low)).astype(low)
    query_mat = order_matrix(GROUPS)
    output_shard = jnp.einsum(
        "pod,on->dpn",
        output_weight.astype(low).reshape(PAIRS, PAIR_WIDTH, slice_rows),
        query_mat,
        preferred_element_type=wide,
    ).reshape(slice_rows, QUERY_WIDTH).astype(low)
    gain_column = jnp.broadcast_to(gain_rows[:, 1:].astype(low), (slice_rows, LANES))
    columns = joined_shard.shape[1]
    shard = jnp.concatenate([joined_shard, output_shard, gain_column], axis=1)

    on_line = contexts == 4 and cores == 2
    bounds = [0, 2, 4, experts_dev] if on_line else [0, experts_dev]
    chunks = list(zip(bounds[:-1], bounds[1:]))
    expert_low = [
        jnp.concatenate(
            [
                expand_weight[a:b].astype(low),
                jnp.swapaxes(contract_weight[a:b].astype(low), 1, 2),
            ],
            axis=2,
        )
        for a, b in chunks
    ]
    line, *expert_low = lax.optimization_barrier(
        (jnp.concatenate(spread(shard, "context"), axis=0), *expert_low)
    )
    joined_mine = spread(line[:, :columns], "expert")
    joined_parts = joined_mine + [swap(part, "dp", 1) for part in joined_mine]
    output_mine = share(after(line[:, columns:], *joined_mine), "expert")
    expert_full = [
        lax.all_gather(part, ("context", "dp"), axis=1, tiled=True) for part in expert_low
    ]

    ar = lambda n: jnp.arange(n, dtype=jnp.int32)
    to_relative = (
        ((own_expert ^ ar(owners))[None, :, None] * contexts + (own_context ^ ar(contexts))[None, None, :])
        * cores
        + (own_core ^ ar(cores))[:, None, None]
    ).reshape(-1)
    to_absolute = (
        (own_core ^ ar(cores))[None, None, :] * owners + (own_expert ^ ar(owners))[:, None, None]
    ) * contexts + (own_context ^ ar(contexts))[None, :, None]
    to_absolute = to_absolute.reshape(-1)
    slices = owners * contexts * cores

    def pick_rows(rows, index):
        return jnp.take(
            rows.reshape(slices, slice_rows, -1), index, axis=0, mode="clip", unique_indices=True
        ).reshape(rows.shape)

    hits = routes[0][:, :, None] == ar(experts)[None, None, :]
    gate_table = jnp.sum(jnp.where(hits, route_gates[0][:, :, None], 0.0), axis=1)
    gate_table = gate_table.reshape(tokens, owners, experts_dev)
    gate_sent = [
        lax.dynamic_index_in_dim(gate_table, own_expert ^ k, axis=1, keepdims=False)
        for k in range(owners)
    ]
    gate_parts = [gate_sent[0]] + [swap(gate_sent[k], "expert", k) for k in range(1, owners)]
    gates = in_order(gate_parts, own_expert).T[:, :, None]

    if on_line:
        along = line_order(own_context)
        grad_slices = (along[None, :] * cores + (own_core ^ ar(cores))[:, None]).reshape(-1)
    else:
        grad_slices = None

    def turned_rows(block):
        turned = block.T
        if on_line:
            shape = (contexts * cores, width // (contexts * cores), block.shape[0])
            turned = jnp.take(turned.reshape(shape), grad_slices, axis=0, mode="clip")
        return turned.reshape(width, block.shape[0])

    order = block_order[0]
    offsets = ar(half_block)

    def places_of(index):
        mine = lax.dynamic_slice_in_dim(order, 2 * index, 2)
        return (mine[:, None] * half_block + offsets[None, :]).reshape(-1)

    query_pos = places_of(own_context)
    key_pos = jnp.concatenate([places_of(own_context ^ k) for k in range(contexts)])
    half = HEAD_DIM // 2
    freq = jnp.exp(ar(half).astype(wide) * (2.0 / HEAD_DIM) * -math.log(10000.0))
    angle = key_pos.astype(wide)[:, None] * freq[None, :]
    cosine = jnp.tile(jnp.cos(angle), (1, 4))
    sine = jnp.sin(angle)
    sine = jnp.concatenate([-sine, -sine, sine, sine], axis=1)
    query_cosine, query_sine = cosine[:tokens], sine[:tokens]

    low_input = layer_input[0]
    resid = low_input.astype(wide)
    scale_one = lax.rsqrt(jnp.mean(resid * resid, axis=-1, keepdims=True) + norm_eps)
    unit_one = resid * scale_one
    input_turned = pick_rows(low_input.T, to_relative)
    input_relative = input_turned.T
    query, kv = project(input_relative, scale_one, query_cosine, query_sine, joined_parts)
    kv_parts = spread(kv, "context")
    output_mine = after(output_mine, kv)
    output_parts = [output_mine, swap(output_mine, "dp", 1)]
    out_grads = share(after(cotangent[0], output_mine), "expert").reshape(-1, width)
    kv_parts = all_after(kv_parts, output_mine)
    attended_wide, attended, logs = attend(query, key_pos[:, None], query_pos[None, :], kv_parts)

    output_parts = all_after(output_parts, attended)
    output_pack = jnp.stack([part.reshape(owners, contexts, -1) for part in output_parts])
    output_pack = jnp.take(
        output_pack, own_context ^ ar(contexts), axis=2, mode="clip", unique_indices=True
    )
    output_pack = jnp.take(output_pack, own_core ^ ar(cores), axis=0, mode="clip", unique_indices=True)
    output_pack = output_pack.transpose(1, 2, 0, 3).reshape(width, -1)
    output_turned = output_pack[:, :QUERY_WIDTH]
    gain_two = output_pack[:, QUERY_WIDTH].astype(wide)[None, :]
    middle = resid + dot_nt(attended, output_turned)
    scale_two = lax.rsqrt(jnp.mean(middle * middle, axis=-1, keepdims=True) + norm_eps)
    unit_two = middle * scale_two
    normed_two = (unit_two * gain_two).astype(low)

    rows_parts = spread(normed_two, "expert")
    out_grads = after(out_grads, normed_two)
    out_grads_turned = turned_rows(out_grads)
    rows = in_order(all_after(rows_parts, out_grads_turned), own_expert)
    rows_turned = turned_rows(rows)

    def forward_unit(unit, *others):
        a, b = chunks[unit]
        return expert_hidden(after(rows, *others), out_grads, gates[a:b], expert_full[unit])

    def grads_unit(back, hidden, *others):
        turned = after(rows_turned, *others)
        if on_line:
            return LineSum(*expert_weight_grads(turned, out_grads_turned, back, hidden, contexts))
        both = expert_weight_grads(turned, out_grads_turned, back, hidden, 1)
        return jnp.concatenate([part[0] for part in both], axis=1)

    def to_tokens(part):
        return trade(part.reshape(owners, tokens, width), "expert")

    def total_of(parts):
        return jnp.sum(parts.astype(wide), axis=0)

    hiddens, backs, sums = [], [], []
    if on_line:
        for unit in range(3):
            hidden, back = forward_unit(unit, *([] if unit == 0 else [latest]))
            hiddens.append(hidden)
            backs.append(back)
            latest = hidden
            if unit == 1:
                latest = sums[0].inward(latest)
            if unit < 2:
                sums.append(grads_unit(back, hidden, latest))
                latest = sums[-1].own
            if unit == 1:
                held = combine(all_after(backs, latest), expert_full[:2], 0, None, False)
                latest = sums[1].inward(held)
        grad_sent = combine(backs[2:], expert_full[2:], 0, held)
        grad_parts = to_tokens(grad_sent)
        sums.append(grads_unit(backs[2], hiddens[2], grad_sent))
        latest = sums[0].across(sums[2].own)
        mixture_sent = combine(all_after(hiddens, latest), expert_full, 2)
        latest = sums[2].inward(mixture_sent)
        grad_parts = after(grad_parts, latest)
        mixture_parts = to_tokens(after(mixture_sent, grad_parts))
    else:
        for unit in range(len(chunks)):
            hidden, back = forward_unit(unit)
            hiddens.append(hidden)
            backs.append(back)
            sums.append(
                lax.psum_scatter(
                    grads_unit(back, hidden), ("context", "dp"), scatter_dimension=1, tiled=True
                ).astype(wide)
            )
        grad_parts = to_tokens(combine(backs, expert_full, 0))
        mixture_parts = to_tokens(combine(hiddens, expert_full, 2))

    grad_normed_two = total_of(grad_parts)

    grad_out = cotangent[0].astype(wide)
    grad_unit_two = grad_normed_two * gain_two
    gain_grad_two = jnp.sum(grad_normed_two * unit_two, axis=0)
    grad_middle = grad_out + scale_two * (
        grad_unit_two - unit_two * jnp.mean(grad_unit_two * unit_two, axis=-1, keepdims=True)
    )
    grad_proj = grad_middle.astype(low)
    grad_attended = dot_nn(grad_proj, output_turned).astype(low)
    sequence = lax.all_gather(after(low_input, expert_full[0]), "context", axis=0)
    sequence = jnp.take(
        sequence, own_context ^ ar(contexts), axis=0, mode="clip", unique_indices=True
    ).reshape(-1, width)
    sequence_wide = sequence.astype(wide)
    sequence_scale = lax.rsqrt(
        jnp.mean(sequence_wide * sequence_wide, axis=-1, keepdims=True) + norm_eps
    )
    sequence_turned = pick_rows(sequence.T, to_relative)

    grad_output = dot_nn(grad_proj.T, attended).astype(low)
    grad_output = jnp.concatenate(
        [grad_output, jnp.broadcast_to(gain_grad_two[:, None].astype(low), (width, LANES))], axis=1
    )
    sum_output = lax.psum_scatter(
        grad_output, ("expert", "context", "dp"), scatter_dimension=0, tiled=True
    ).astype(wide)
    latest = [grad_output]
    if on_line:
        latest = [sums[1].across(*latest), sums[0].outward(*latest)]
    grad_query, grad_kv = attend_back(
        after(query, *latest), grad_attended, attended_wide, logs, key_pos[:, None],
        query_pos[None, :], sequence_scale, cosine, sine, kv_parts,
    )
    grad_kv_all = grad_kv.reshape(-1, 2 * KV_WIDTH)

    relative = (owners, contexts, slice_rows)
    split = width // cores
    halves = [slice(k * split, (k + 1) * split) for k in range(cores)]

    def joined_grads(part):
        grads = jnp.concatenate(
            [
                dot_nn(input_turned[part], grad_query).astype(low),
                dot_nn(sequence_turned[part], grad_kv_all).astype(low),
            ],
            axis=1,
        )
        return grads.reshape(*relative, -1)

    joined_sum = OwnerSum(*[joined_grads(part) for part in halves])
    grad_kv_sent = jnp.take(
        after(grad_kv, joined_sum.own), own_context ^ ar(contexts), axis=0, mode="clip",
        unique_indices=True,
    )
    grad_kv_parts = trade(grad_kv_sent, "context")
    latest = joined_sum.spread_experts(grad_kv_sent)
    if on_line:
        latest = [sums[2].across(*latest), sums[1].outward(*latest)]

    own_grad_kv = total_of(after(grad_kv_parts, *latest))
    grad_joined = jnp.concatenate([grad_query, own_grad_kv.astype(low)], axis=1)
    scaled_grad = jnp.concatenate([dot_nt(part, grad_joined) for part in joined_parts], axis=0)
    scaled_grad = pick_rows(scaled_grad, to_absolute).T
    grad_input = (
        grad_middle
        + scaled_grad
        - unit_one * jnp.mean(scaled_grad * unit_one, axis=-1, keepdims=True)
    ).astype(low)
    mixture = total_of(after(mixture_parts, grad_input))
    output = (middle + mixture).astype(low)

    latest = joined_sum.spread_contexts(output)
    if on_line:
        latest = [sums[2].outward(*latest)]
        expert_grads = [part.finish(*latest) for part in sums]
    else:
        expert_grads = sums
    sum_joined = joined_sum.finish(*latest)

    unit_grads = reorder_columns(sum_joined, back=True)
    sum_joined = gain_rows[:, :1] * unit_grads
    sum_gain_one = jnp.sum(joined_low.astype(wide) * unit_grads, axis=1)
    sum_gains = jnp.stack([sum_gain_one, sum_output[:, QUERY_WIDTH]], axis=0)
    sum_output_weight = jnp.einsum(
        "on,dpn->pod",
        query_mat.astype(wide),
        sum_output[:, :QUERY_WIDTH].reshape(slice_rows, PAIRS, PAIR_WIDTH),
        precision=lax.Precision.HIGHEST,
        preferred_element_type=wide,
    ).reshape(QUERY_WIDTH, slice_rows)
    joined_new = adamw(
        joined_weight, joined_first, joined_second, sum_joined, rate_joined, decay_rate
    )
    output_new = adamw(
        output_weight, output_first, output_second, sum_output_weight, rate_output, decay_rate
    )
    gains_new = adamw(norm_gains, gains_first, gains_second, sum_gains, rate_gains, 0.0)
    sum_experts = jnp.concatenate(expert_grads, axis=0)
    expand_new = adamw(
        expand_weight, expand_first, expand_second, sum_experts[:, :, : 2 * FF], rate_expand, decay_rate
    )
    contract_new = adamw(
        contract_weight,
        contract_first,
        contract_second,
        jnp.swapaxes(sum_experts[:, :, 2 * FF :], 1, 2),
        rate_contract,
        decay_rate,
    )
    return (
        output.reshape(1, tokens, width),
        grad_input.reshape(1, tokens, width),
        *joined_new,
        *output_new,
        *gains_new,
        *expand_new,
        *contract_new,
    )


def solution(mesh):
    rows = P(("expert", "dp"), "context", None)
    joined = P(("expert", "context", "dp"), None)
    column = P(None, ("expert", "context", "dp"))
    expand = P("expert", ("context", "dp"), None)
    contract = P("expert", None, ("context", "dp"))
    placed = (
        (rows, rows, P(("expert", "dp"), None), rows, rows)
        + (joined,) * 3
        + (column,) * 6
        + (expand,) * 3
        + (contract,) * 3
    )
    return jax.shard_map(
        body,
        mesh=mesh,
        in_specs=placed,
        out_specs=(rows, rows) + placed[5:],
        check_vma=False,
    )
```

```python
import functools
import math

import jax
import jax.numpy as jnp
import numpy as np
from jax import lax
from jax.experimental import pallas as pl
from jax.experimental.pallas import tpu as pltpu
from jax.sharding import PartitionSpec as P

HEADS = 24
KV_HEADS = 8
HEAD_DIM = 64
FF = 512
TOP = 8
STEP = 10
GROUPS = HEADS // KV_HEADS
PAIRS = KV_HEADS // 2
QUERY_WIDTH = HEADS * HEAD_DIM
KV_WIDTH = KV_HEADS * HEAD_DIM
PAIR_WIDTH = 2 * GROUPS * HEAD_DIM
LANES = 128
VMEM_BYTES = 60 * 1024 * 1024

norm_eps = 1e-06
beta_one = 0.9
beta_two = 0.95
adam_eps = 1e-08
decay_rate = 0.1
rate_joined = 0.08
rate_output = 0.6
rate_gains = 0.6
rate_expand = 0.08
rate_contract = 0.5
masked_score = -1e30

low = jnp.bfloat16
wide = jnp.float32


def adamw(weight, first, second, grad, rate, decay):
    first_new = beta_one * first + (1.0 - beta_one) * grad
    second_new = beta_two * second + (1.0 - beta_two) * grad * grad
    first_hat = first_new / (1.0 - beta_one**STEP)
    second_hat = second_new / (1.0 - beta_two**STEP)
    weight_new = weight - rate * (first_hat / (jnp.sqrt(second_hat) + adam_eps) + decay * weight)
    return (weight_new, first_new, second_new)


def dot_nn(left, right):
    return lax.dot_general(left, right, (((1,), (0,)), ((), ())), preferred_element_type=wide)


def dot_nt(left, right):
    return lax.dot_general(left, right, (((1,), (1,)), ((), ())), preferred_element_type=wide)


def pair_order(groups):
    half = HEAD_DIM // 2
    old = np.arange(2 * groups * HEAD_DIM).reshape(2, groups, 2, half)
    return old.transpose(1, 2, 0, 3).reshape(-1)


def order_matrix(groups):
    order = pair_order(groups)
    size = order.shape[0]
    return jnp.asarray(np.arange(size)[:, None] == order[None, :], dtype=low)


def reorder_columns(rows, back=False):
    count = rows.shape[0]
    query_mat = order_matrix(GROUPS)
    key_mat = order_matrix(1)
    kv = rows[:, QUERY_WIDTH:]
    if back:
        query_mat = query_mat.T
        key_mat = key_mat.T
        kv = jnp.swapaxes(kv.reshape(count, PAIRS, 2, LANES), 1, 2)
    else:
        kv = jnp.swapaxes(kv.reshape(count, 2, PAIRS, LANES), 1, 2)
    exact = lax.Precision.HIGHEST if rows.dtype == wide else None
    query = jnp.einsum(
        "rpo,on->rpn",
        rows[:, :QUERY_WIDTH].reshape(count, PAIRS, PAIR_WIDTH),
        query_mat.astype(rows.dtype),
        precision=exact,
        preferred_element_type=wide,
    ).reshape(count, QUERY_WIDTH)
    others = jnp.einsum(
        "rpo,on->rpn",
        kv.reshape(count, 2 * PAIRS, LANES),
        key_mat.astype(rows.dtype),
        precision=exact,
        preferred_element_type=wide,
    ).reshape(count, 2 * KV_WIDTH)
    return jnp.concatenate([query, others], axis=1)


def swap(block, axis, step):
    count = lax.axis_size(axis)
    return lax.ppermute(block, axis, [(i, i ^ step) for i in range(count)])


def spread(block, axis):
    return [block] + [swap(block, axis, k) for k in range(1, lax.axis_size(axis))]


def after(value, *others):
    return lax.optimization_barrier((value, *others))[0]


def all_after(values, *others):
    count = len(values)
    return list(lax.optimization_barrier((*values, *others))[:count])


def share(block, axis):
    return trade(jnp.broadcast_to(block[None], (lax.axis_size(axis), *block.shape)), axis)


def trade(blocks, axis):
    return lax.all_to_all(blocks, axis, split_axis=0, concat_axis=0, tiled=True)


def in_order(parts, own):
    rows = parts[0].shape[0]
    joined = jnp.zeros((len(parts) * rows, *parts[0].shape[1:]), parts[0].dtype)
    for k, part in enumerate(parts):
        joined = lax.dynamic_update_slice_in_dim(joined, part, (own ^ k) * rows, 0)
    return joined


class OwnerSum:
    def __init__(self, own, other):
        self.own = own
        self.came = swap(other, "dp", 1)

    def spread_experts(self, *others):
        came = after(self.came, *others)
        both = [
            (self.own[k].astype(wide) + came[k].astype(wide)).astype(low)
            for k in range(self.own.shape[0])
        ]
        self.parts = [both[0]] + [swap(both[k], "expert", k) for k in range(1, len(both))]
        return both

    def spread_contexts(self, *others):
        parts = all_after(self.parts, *others)
        total = functools.reduce(jnp.add, [part.astype(wide) for part in parts])
        column = [total[k].astype(low) for k in range(1, total.shape[0])]
        self.parts = [total[0]] + [swap(part, "context", k + 1) for k, part in enumerate(column)]
        return column

    def finish(self, *others):
        parts = all_after(self.parts, *others)
        return functools.reduce(jnp.add, [part.astype(wide) for part in parts])


def line_order(own):
    near = jnp.array([1, 2, 3, 0], jnp.int32)
    return jnp.where(own < 2, near, 3 - near)


class LineSum:
    def __init__(self, own, other):
        self.own = own
        self.came = swap(other, "dp", 1)

    def inward(self, *others):
        came = after(self.came, *others)
        first = (self.own[:3].astype(wide) + came[:3].astype(wide)).astype(low)
        self.last = (self.own[3].astype(wide) + came[3].astype(wide)).astype(low)
        self.first = first
        self.from_end = lax.ppermute(first, "context", [(0, 1), (3, 2)])
        return first

    def across(self, *others):
        self.from_end = after(self.from_end, *others)
        both = (self.first[1:].astype(wide) + self.from_end[1:].astype(wide)).astype(low)
        self.from_inner = lax.ppermute(both, "context", [(1, 2), (2, 1)])
        return both

    def outward(self, *others):
        self.from_inner = after(self.from_inner, *others)
        near = (self.last.astype(wide) + self.from_inner[1].astype(wide)).astype(low)
        self.to_end = lax.ppermute(near, "context", [(1, 0), (2, 3)])
        return near

    def finish(self, *others):
        to_end = after(self.to_end, *others)
        place = lax.axis_index("context")
        inner = (place == 1) | (place == 2)
        return jnp.where(
            inner,
            self.first[0].astype(wide) + self.from_end[0].astype(wide)
            + self.from_inner[0].astype(wide),
            self.last.astype(wide) + to_end.astype(wide),
        )


def call(body, grid, in_specs, out_specs, out_shape, scratch=()):
    return pl.pallas_call(
        body,
        grid=grid,
        in_specs=in_specs,
        out_specs=out_specs,
        out_shape=out_shape,
        scratch_shapes=list(scratch),
        compiler_params=pltpu.CompilerParams(vmem_limit_bytes=VMEM_BYTES),
        cost_estimate=pl.CostEstimate(flops=1, bytes_accessed=1, transcendentals=0),
    )


def turn(vals, cosine, sine):
    return vals * cosine + pltpu.roll(vals, LANES // 2, 1) * sine


def project_body(count, rows_ref, scale_ref, cos_ref, sin_ref, *refs):
    weight_refs, (query_ref, kv_ref, weight_ref) = refs[:count], refs[count:]
    step = pl.program_id(0)
    depth = weight_refs[0].shape[0]
    for k in range(count):
        weight_ref[k * depth : (k + 1) * depth, :] = weight_refs[k][...]
    total = dot_nn(rows_ref[...], weight_ref[...]) * scale_ref[...]
    block = total.shape[1]
    query_steps = QUERY_WIDTH // block
    cosine, sine = cos_ref[...], sin_ref[...]
    groups = [total[:, i * LANES : (i + 1) * LANES] for i in range(block // LANES)]

    @pl.when(step < query_steps)
    def _():
        for i, group in enumerate(groups):
            turned = turn(group, cosine, sine) * HEAD_DIM**-0.5
            query_ref[:, i * LANES : (i + 1) * LANES] = turned.astype(low)

    @pl.when(step >= query_steps)
    def _():
        for i, group in enumerate(groups):
            kept = turn(group, cosine, sine) if i % 2 == 0 else group
            kv_ref[:, i * LANES : (i + 1) * LANES] = kept.astype(low)


def project(rows, scale, cosine, sine, weights):
    tokens, width = rows.shape
    columns = QUERY_WIDTH + 2 * KV_WIDTH
    block = 512
    query_steps = QUERY_WIDTH // block
    depth = weights[0].shape[0]
    whole = lambda shape: pl.BlockSpec(shape, lambda j: (0, 0))
    return call(
        functools.partial(project_body, len(weights)),
        (columns // block,),
        [whole((tokens, width)), whole((tokens, 1)), whole((tokens, LANES)), whole((tokens, LANES))]
        + [pl.BlockSpec((depth, block), lambda j: (0, j))] * len(weights),
        [
            pl.BlockSpec((tokens, block), lambda j: (0, jnp.minimum(j, query_steps - 1))),
            pl.BlockSpec((tokens, block), lambda j: (0, jnp.maximum(j - query_steps, 0))),
        ],
        [
            jax.ShapeDtypeStruct((tokens, QUERY_WIDTH), low),
            jax.ShapeDtypeStruct((tokens, 2 * KV_WIDTH), low),
        ],
        scratch=[pltpu.VMEM((width, block), low)],
    )(rows, scale, cosine, sine, *weights)


def lane_of(shape, axis, which):
    place = lax.broadcasted_iota(jnp.int32, shape, axis)
    return ((place // (HEAD_DIM // 2)) % 2) == which


def stack_heads(block, which):
    keep = lane_of((block.shape[0], LANES), 1, which)
    return jnp.concatenate(
        [
            jnp.where(keep, block[:, g * LANES : (g + 1) * LANES], jnp.zeros((), block.dtype))
            for g in range(GROUPS)
        ],
        axis=0,
    )


def allowed_pairs(key_pos, query_pos):
    seen = key_pos <= query_pos
    return jnp.concatenate([seen] * GROUPS, axis=1)


def turned_block(block):
    return block.astype(wide).T.astype(low)


def attend_body(count, query_ref, key_pos_ref, query_pos_ref, *refs):
    kv_refs, (out_ref, out_low_ref, log_ref) = refs[:count], refs[count:]
    tokens = query_ref.shape[0]
    seen = allowed_pairs(key_pos_ref[...], query_pos_ref[...])
    keys = jnp.concatenate([ref[:, :LANES] for ref in kv_refs], axis=0)
    values = jnp.concatenate([turned_block(ref[:, LANES:]) for ref in kv_refs], axis=1)
    outs = []
    for which in range(2):
        query = stack_heads(query_ref[...], which)
        scores = jnp.where(seen, dot_nt(keys, query), masked_score)
        peak = jnp.max(scores, axis=0, keepdims=True)
        weight = jnp.exp(scores - peak)
        total = jnp.sum(weight, axis=0, keepdims=True)
        outs.append(dot_nn(values, weight.astype(low)) / total)
        log_ref[0, which : which + 1, :] = peak + jnp.log(total)
    first = lane_of(outs[0].shape, 0, 0)
    both = jnp.where(first, outs[0], outs[1]).T
    for g in range(GROUPS):
        piece = both[g * tokens : (g + 1) * tokens, :]
        out_ref[:, g * LANES : (g + 1) * LANES] = piece
        out_low_ref[:, g * LANES : (g + 1) * LANES] = piece.astype(low)


def attend(query, key_pos, query_pos, kv_parts):
    tokens = query.shape[0]
    count = len(kv_parts)
    seq_len = tokens * count
    pairs = pl.BlockSpec((tokens, PAIR_WIDTH), lambda p: (0, p))
    return call(
        functools.partial(attend_body, count),
        (PAIRS,),
        [
            pairs,
            pl.BlockSpec((seq_len, 1), lambda p: (0, 0)),
            pl.BlockSpec((1, tokens), lambda p: (0, 0)),
        ]
        + [pl.BlockSpec((tokens, 2 * LANES), lambda p: (0, p))] * count,
        [pairs, pairs, pl.BlockSpec((1, 2, GROUPS * tokens), lambda p: (p, 0, 0))],
        [
            jax.ShapeDtypeStruct((tokens, QUERY_WIDTH), wide),
            jax.ShapeDtypeStruct((tokens, QUERY_WIDTH), low),
            jax.ShapeDtypeStruct((PAIRS, 2, GROUPS * tokens), wide),
        ],
    )(query, key_pos, query_pos, *kv_parts)


def attend_back_body(count, query_ref, grad_ref, out_ref, log_ref, key_pos_ref, query_pos_ref,
                     scale_ref, cos_ref, sin_ref, *refs):
    kv_refs, (grad_query_ref, grad_kv_ref) = refs[:count], refs[count:]
    tokens = query_ref.shape[0]
    grads = grad_ref[...]
    product = jnp.concatenate(
        [
            (grads[:, g * LANES : (g + 1) * LANES].astype(wide)
             * out_ref[:, g * LANES : (g + 1) * LANES]).T
            for g in range(GROUPS)
        ],
        axis=1,
    )
    first = lane_of(product.shape, 0, 0)
    delta = [
        jnp.sum(jnp.where(first, product, 0.0), axis=0, keepdims=True),
        jnp.sum(jnp.where(first, 0.0, product), axis=0, keepdims=True),
    ]
    seen = allowed_pairs(key_pos_ref[...], query_pos_ref[...])
    keys = jnp.concatenate([ref[:, :LANES] for ref in kv_refs], axis=0)
    values = jnp.concatenate([ref[:, LANES:] for ref in kv_refs], axis=0)
    keys_turned = jnp.concatenate([turned_block(ref[:, :LANES]) for ref in kv_refs], axis=1)
    grad_key, grad_value, grad_query = None, None, []
    for which in range(2):
        query = stack_heads(query_ref[...], which)
        head = stack_heads(grads, which)
        scores = jnp.where(seen, dot_nt(keys, query), masked_score)
        probs = jnp.exp(scores - log_ref[0, which : which + 1, :])
        grad_probs = dot_nt(values, head)
        grad_scores = (probs * (grad_probs - delta[which])).astype(low)
        part_value = dot_nn(probs.astype(low), head)
        part_key = dot_nn(grad_scores, query)
        grad_query.append(dot_nn(keys_turned, grad_scores))
        grad_value = part_value if grad_value is None else grad_value + part_value
        grad_key = part_key if grad_key is None else grad_key + part_key
    scale, cosine, sine = scale_ref[...], cos_ref[...], sin_ref[...]
    grad_key = turn(grad_key, cosine, -sine) * scale
    grad_value = grad_value * scale
    for k in range(count):
        rows = slice(k * tokens, (k + 1) * tokens)
        grad_kv_ref[k, :, :LANES] = grad_key[rows, :].astype(low)
        grad_kv_ref[k, :, LANES:] = grad_value[rows, :].astype(low)
    first = lane_of(grad_query[0].shape, 0, 0)
    both = (jnp.where(first, grad_query[0], grad_query[1]) * HEAD_DIM**-0.5).T
    for g in range(GROUPS):
        piece = both[g * tokens : (g + 1) * tokens, :]
        back = turn(piece, cosine[:tokens, :], -sine[:tokens, :])
        grad_query_ref[:, g * LANES : (g + 1) * LANES] = (back * scale[:tokens, :]).astype(low)


def attend_back(query, grads, out, logs, key_pos, query_pos, scale, cosine, sine, kv_parts):
    tokens = query.shape[0]
    count = len(kv_parts)
    seq_len = tokens * count
    pairs = pl.BlockSpec((tokens, PAIR_WIDTH), lambda p: (0, p))
    whole = lambda shape: pl.BlockSpec(shape, lambda p: (0, 0))
    part = pl.BlockSpec((tokens, 2 * LANES), lambda p: (0, p))
    return call(
        functools.partial(attend_back_body, count),
        (PAIRS,),
        [
            pairs,
            pairs,
            pairs,
            pl.BlockSpec((1, 2, GROUPS * tokens), lambda p: (p, 0, 0)),
            whole((seq_len, 1)),
            whole((1, tokens)),
            whole((seq_len, 1)),
            whole((seq_len, LANES)),
            whole((seq_len, LANES)),
        ]
        + [part] * count,
        [pairs, pl.BlockSpec((count, tokens, 2 * LANES), lambda p: (0, 0, p))],
        [
            jax.ShapeDtypeStruct((tokens, QUERY_WIDTH), low),
            jax.ShapeDtypeStruct((count, tokens, 2 * KV_WIDTH), low),
        ],
    )(query, grads, out, logs, key_pos, query_pos, scale, cosine, sine, *kv_parts)


def hidden_body(rows_ref, grads_ref, gate_ref, weight_ref, hidden_ref, back_ref):
    rows, grads, weight = rows_ref[...], grads_ref[...], gate_ref[0]
    step = 256
    for h in range(0, FF, step):
        gate = dot_nn(rows, weight_ref[0, :, h : h + step])
        up = dot_nn(rows, weight_ref[0, :, FF + h : FF + h + step])
        grad_hidden = dot_nn(grads, weight_ref[0, :, 2 * FF + h : 2 * FF + h + step]) * weight
        sigmoid = 1.0 / (1.0 + jnp.exp(-gate))
        active = gate * sigmoid
        hidden_ref[0, :, h : h + step] = (active * up * weight).astype(low)
        slope = sigmoid + active * (1.0 - sigmoid)
        back_ref[0, :, h : h + step] = (grad_hidden * up * slope).astype(low)
        back_ref[0, :, FF + h : FF + h + step] = (grad_hidden * active).astype(low)


def expert_hidden(rows, grads, gates, weights):
    tokens, width = rows.shape
    experts = weights.shape[0]
    block = min(tokens, 1024)
    return call(
        hidden_body,
        (experts, tokens // block),
        [
            pl.BlockSpec((block, width), lambda e, t: (t, 0)),
            pl.BlockSpec((block, width), lambda e, t: (t, 0)),
            pl.BlockSpec((1, block, 1), lambda e, t: (e, t, 0)),
            pl.BlockSpec((1, width, 3 * FF), lambda e, t: (e, 0, 0)),
        ],
        [
            pl.BlockSpec((1, block, FF), lambda e, t: (e, t, 0)),
            pl.BlockSpec((1, block, 2 * FF), lambda e, t: (e, t, 0)),
        ],
        [
            jax.ShapeDtypeStruct((experts, tokens, FF), low),
            jax.ShapeDtypeStruct((experts, tokens, 2 * FF), low),
        ],
    )(rows, grads, gates, weights)


def weight_grad_body(slices, rows_ref, grads_ref, back_ref, hidden_ref, *out_refs):
    step = pl.program_id(1)
    from_rows = dot_nn(rows_ref[...], back_ref[0]).astype(low)
    from_grads = dot_nn(grads_ref[...], hidden_ref[0]).astype(low)
    if not slices:
        out_refs[0][0, :, : 2 * FF] = from_rows
        out_refs[0][0, :, 2 * FF :] = from_grads
        return
    size = rows_ref.shape[0] // slices
    for half, out_ref in enumerate(out_refs):

        @pl.when(step == half)
        def _():
            for i in range(slices):
                out_ref[i, 0, :, : 2 * FF] = from_rows[i * size : (i + 1) * size, :]
                out_ref[i, 0, :, 2 * FF :] = from_grads[i * size : (i + 1) * size, :]


def expert_weight_grads(rows_turned, grads_turned, back, hidden, slices=0):
    width, tokens = rows_turned.shape
    experts = back.shape[0]
    block = width // 2
    if slices:
        shape = (slices, experts, block // slices, 3 * FF)
        out_specs = [pl.BlockSpec((slices, 1) + shape[2:], lambda e, m: (0, e, 0, 0))] * 2
        out_shape = [jax.ShapeDtypeStruct(shape, low)] * 2
    else:
        out_specs = pl.BlockSpec((1, block, 3 * FF), lambda e, m: (e, m, 0))
        out_shape = jax.ShapeDtypeStruct((experts, width, 3 * FF), low)
    return call(
        functools.partial(weight_grad_body, slices),
        (experts, 2),
        [
            pl.BlockSpec((block, tokens), lambda e, m: (m, 0)),
            pl.BlockSpec((block, tokens), lambda e, m: (m, 0)),
            pl.BlockSpec((1, tokens, 2 * FF), lambda e, m: (e, 0, 0)),
            pl.BlockSpec((1, tokens, FF), lambda e, m: (e, 0, 0)),
        ],
        out_specs,
        out_shape,
    )(rows_turned, grads_turned, back, hidden)


def combine_body(sizes, held, last, *refs):
    count = len(sizes)
    part_refs, weight_refs, refs = refs[:count], refs[count : 2 * count], refs[2 * count :]
    if held:
        held_ref, refs = refs[0], refs[1:]
    out_ref, total_ref = refs[0], refs[-1]
    step = pl.program_id(0)

    @pl.when(step == 0)
    def _():
        total_ref[...] = held_ref[...] if held else jnp.zeros_like(total_ref)

    start = 0
    for part_ref, weight_ref, size in zip(part_refs, weight_refs, sizes):

        @pl.when((step >= start) & (step < start + size))
        def _():
            total_ref[...] += dot_nt(part_ref[0], weight_ref[0])

        start += size

    if last:

        @pl.when(step == start - 1)
        def _():
            out_ref[...] = total_ref[...].astype(low)


def combine(parts, weights, column, held=None, last=True):
    tokens, depth = parts[0].shape[1:]
    width = weights[0].shape[1]
    sizes = [w.shape[0] for w in weights]
    starts = [sum(sizes[:i]) for i in range(len(sizes))]
    place = lambda e, start, size: jnp.clip(e - start, 0, size - 1)
    part_specs = [
        pl.BlockSpec((1, tokens, depth), lambda e, s=s, n=n: (place(e, s, n), 0, 0))
        for s, n in zip(starts, sizes)
    ]
    weight_specs = [
        pl.BlockSpec((1, width, depth), lambda e, s=s, n=n: (place(e, s, n), 0, column))
        for s, n in zip(starts, sizes)
    ]
    total = pl.BlockSpec((tokens, width), lambda e: (0, 0), pipeline_mode=pl.Buffered(1))
    return call(
        functools.partial(combine_body, sizes, held is not None, last),
        (sum(sizes),),
        part_specs + weight_specs + ([] if held is None else [total]),
        total,
        jax.ShapeDtypeStruct((tokens, width), low if last else wide),
        scratch=[pltpu.VMEM((tokens, width), wide)] if last else [],
    )(*parts, *weights, *([] if held is None else [held]))


def body(
    layer_input,
    cotangent,
    block_order,
    routes,
    route_gates,
    joined_weight,
    joined_first,
    joined_second,
    output_weight,
    output_first,
    output_second,
    norm_gains,
    gains_first,
    gains_second,
    expand_weight,
    expand_first,
    expand_second,
    contract_weight,
    contract_first,
    contract_second,
):
    experts_dev = expand_weight.shape[0]
    owners = lax.axis_size("expert")
    contexts = lax.axis_size("context")
    cores = lax.axis_size("dp")
    experts = experts_dev * owners
    tokens = layer_input.shape[1]
    width = layer_input.shape[2]
    half_block = tokens // 2
    slice_rows = joined_weight.shape[0]
    own_expert = lax.axis_index("expert")
    own_context = lax.axis_index("context")
    own_core = lax.axis_index("dp")

    gain_rows = norm_gains.astype(low).astype(wide).T
    joined_low = joined_weight.astype(low)
    joined_shard = reorder_columns((gain_rows[:, :1] * joined_low.astype(wide)).astype(low)).astype(low)
    query_mat = order_matrix(GROUPS)
    output_shard = jnp.einsum(
        "pod,on->dpn",
        output_weight.astype(low).reshape(PAIRS, PAIR_WIDTH, slice_rows),
        query_mat,
        preferred_element_type=wide,
    ).reshape(slice_rows, QUERY_WIDTH).astype(low)
    gain_column = jnp.broadcast_to(gain_rows[:, 1:].astype(low), (slice_rows, LANES))
    columns = joined_shard.shape[1]
    shard = jnp.concatenate([joined_shard, output_shard, gain_column], axis=1)

    on_line = contexts == 4 and cores == 2
    bounds = [0, 2, 4, experts_dev] if on_line else [0, experts_dev]
    chunks = list(zip(bounds[:-1], bounds[1:]))
    expert_low = [
        jnp.concatenate(
            [
                expand_weight[a:b].astype(low),
                jnp.swapaxes(contract_weight[a:b].astype(low), 1, 2),
            ],
            axis=2,
        )
        for a, b in chunks
    ]
    line, *expert_low = lax.optimization_barrier(
        (jnp.concatenate(spread(shard, "context"), axis=0), *expert_low)
    )
    joined_mine = spread(line[:, :columns], "expert")
    joined_parts = joined_mine + [swap(part, "dp", 1) for part in joined_mine]
    output_mine = share(after(line[:, columns:], *joined_mine), "expert")
    gather_expert = lambda part: lax.all_gather(part, ("context", "dp"), axis=1, tiled=True)
    expert_full = [gather_expert(expert_low[0])]

    ar = lambda n: jnp.arange(n, dtype=jnp.int32)
    to_relative = (
        ((own_expert ^ ar(owners))[None, :, None] * contexts + (own_context ^ ar(contexts))[None, None, :])
        * cores
        + (own_core ^ ar(cores))[:, None, None]
    ).reshape(-1)
    to_absolute = (
        (own_core ^ ar(cores))[None, None, :] * owners + (own_expert ^ ar(owners))[:, None, None]
    ) * contexts + (own_context ^ ar(contexts))[None, :, None]
    to_absolute = to_absolute.reshape(-1)
    slices = owners * contexts * cores

    def pick_rows(rows, index):
        return jnp.take(
            rows.reshape(slices, slice_rows, -1), index, axis=0, mode="clip", unique_indices=True
        ).reshape(rows.shape)

    hits = routes[0][:, :, None] == ar(experts)[None, None, :]
    gate_table = jnp.sum(jnp.where(hits, route_gates[0][:, :, None], 0.0), axis=1)
    gate_table = gate_table.reshape(tokens, owners, experts_dev)
    gate_sent = [
        lax.dynamic_index_in_dim(gate_table, own_expert ^ k, axis=1, keepdims=False)
        for k in range(owners)
    ]
    gate_parts = [gate_sent[0]] + [swap(gate_sent[k], "expert", k) for k in range(1, owners)]
    gates = in_order(gate_parts, own_expert).T[:, :, None]

    def line_rows(turned):
        along = line_order(own_context)
        index = (along[None, :] * cores + (own_core ^ ar(cores))[:, None]).reshape(-1)
        shape = (contexts * cores, width // (contexts * cores), turned.shape[1])
        return jnp.take(
            turned.reshape(shape), index, axis=0, mode="clip", unique_indices=True
        ).reshape(turned.shape)

    order = block_order[0]
    offsets = ar(half_block)

    def places_of(index):
        mine = lax.dynamic_slice_in_dim(order, 2 * index, 2)
        return (mine[:, None] * half_block + offsets[None, :]).reshape(-1)

    query_pos = places_of(own_context)
    key_pos = jnp.concatenate([places_of(own_context ^ k) for k in range(contexts)])
    half = HEAD_DIM // 2
    freq = jnp.exp(ar(half).astype(wide) * (2.0 / HEAD_DIM) * -math.log(10000.0))
    angle = key_pos.astype(wide)[:, None] * freq[None, :]
    cosine = jnp.tile(jnp.cos(angle), (1, 4))
    sine = jnp.sin(angle)
    sine = jnp.concatenate([-sine, -sine, sine, sine], axis=1)
    query_cosine, query_sine = cosine[:tokens], sine[:tokens]

    low_input = layer_input[0]
    resid = low_input.astype(wide)
    scale_one = lax.rsqrt(jnp.mean(resid * resid, axis=-1, keepdims=True) + norm_eps)
    unit_one = resid * scale_one
    input_turned = pick_rows(low_input.T, to_relative)
    input_relative = input_turned.T
    query, kv = project(input_relative, scale_one, query_cosine, query_sine, joined_parts)
    kv_parts = spread(kv, "context")
    output_mine = after(output_mine, kv)
    output_parts = [output_mine, swap(output_mine, "dp", 1)]
    out_grads = share(after(cotangent[0], output_mine), "expert").reshape(-1, width)
    kv_parts = all_after(kv_parts, output_mine)
    kv_parts, later = lax.optimization_barrier((kv_parts, expert_low[1:]))
    expert_full += [gather_expert(part) for part in later]
    attended_wide, attended, logs = attend(query, key_pos[:, None], query_pos[None, :], kv_parts)

    output_parts = all_after(output_parts, attended)
    output_place = (
        (own_core ^ ar(cores))[None, None, :] * owners + ar(owners)[:, None, None]
    ) * contexts + (own_context ^ ar(contexts))[None, :, None]
    output_pack = pick_rows(
        jnp.concatenate([part.reshape(-1, output_mine.shape[-1]) for part in output_parts], axis=0),
        output_place.reshape(-1),
    )
    output_turned = output_pack[:, :QUERY_WIDTH]
    gain_two = output_pack[:, QUERY_WIDTH].astype(wide)[None, :]
    middle = resid + dot_nt(attended, output_turned)
    scale_two = lax.rsqrt(jnp.mean(middle * middle, axis=-1, keepdims=True) + norm_eps)
    unit_two = middle * scale_two
    normed_two = (unit_two * gain_two).astype(low)

    rows_parts = spread(normed_two, "expert")
    out_grads = after(out_grads, normed_two)
    out_grads_turned = out_grads.T
    out_grads_line = line_rows(out_grads_turned) if on_line else out_grads_turned
    rows = in_order(all_after(rows_parts, out_grads_line), own_expert)
    rows_turned = rows.T

    def forward_unit(unit, *others):
        a, b = chunks[unit]
        return expert_hidden(after(rows, *others), out_grads, gates[a:b], expert_full[unit])

    def grads_unit(unit, *others):
        turned = after(rows_turned, *others)
        return expert_weight_grads(turned, out_grads_turned, backs[unit], hiddens[unit])

    def to_owners(grads):
        return lax.psum_scatter(
            grads, ("context", "dp"), scatter_dimension=1, tiled=True
        ).astype(wide)

    def to_tokens(part):
        return trade(part.reshape(owners, tokens, width), "expert")

    def total_of(parts):
        return jnp.sum(parts.astype(wide), axis=0)

    hiddens, backs, expert_grads = [], [], []

    def run_forward(unit, *others):
        hidden, back = forward_unit(unit, *others)
        hiddens.append(hidden)
        backs.append(back)
        return back

    if on_line:
        run_forward(0)
        line_sum = LineSum(
            *expert_weight_grads(
                line_rows(after(rows_turned, hiddens[0])), out_grads_line, backs[0], hiddens[0], contexts
            )
        )
        run_forward(1, line_sum.own)
        latest = line_sum.inward(backs[1])
        held = combine(all_after(backs, latest), expert_full[:2], 0, None, False)
        run_forward(2, held)
        grad_sent = combine(backs[2:], expert_full[2:], 0, held)
        grad_parts = to_tokens(grad_sent)
        grads = grads_unit(1, grad_sent)
        expert_grads.append(to_owners(grads))
        mixture_sent = combine(all_after(hiddens, grads), expert_full, 2)
        grads = grads_unit(2, mixture_sent)
        expert_grads.append(to_owners(grads))
        grad_parts = after(grad_parts, grads)
        mixture_parts = to_tokens(after(mixture_sent, grad_parts))
    else:
        for unit in range(len(chunks)):
            run_forward(unit)
            expert_grads.append(to_owners(grads_unit(unit)))
        grad_parts = to_tokens(combine(backs, expert_full, 0))
        mixture_parts = to_tokens(combine(hiddens, expert_full, 2))

    grad_normed_two = total_of(grad_parts)

    grad_out = cotangent[0].astype(wide)
    grad_unit_two = grad_normed_two * gain_two
    gain_grad_two = jnp.sum(grad_normed_two * unit_two, axis=0)
    grad_middle = grad_out + scale_two * (
        grad_unit_two - unit_two * jnp.mean(grad_unit_two * unit_two, axis=-1, keepdims=True)
    )
    grad_proj = grad_middle.astype(low)
    grad_attended = dot_nn(grad_proj, output_turned).astype(low)
    sequence_parts = spread(after(low_input, expert_full[-1]), "context")
    sequence = jnp.concatenate(sequence_parts, axis=0)
    sequence_wide = sequence.astype(wide)
    sequence_scale = lax.rsqrt(
        jnp.mean(sequence_wide * sequence_wide, axis=-1, keepdims=True) + norm_eps
    )
    sequence_turned = pick_rows(sequence.T, to_relative)

    relative = (owners, contexts, slice_rows)
    split = width // cores
    halves = [slice(k * split, (k + 1) * split) for k in range(cores)]
    proj_turned = pick_rows(grad_proj.T, to_relative)
    gain_grads = pick_rows(gain_grad_two[:, None], to_relative).astype(low)

    def output_grads(part):
        grads = dot_nn(proj_turned[part], attended).astype(low)
        extra = jnp.broadcast_to(gain_grads[part], (split, LANES))
        return jnp.concatenate([grads, extra], axis=1).reshape(*relative, -1)

    output_sum = OwnerSum(*[output_grads(part) for part in halves])
    latest = [output_sum.own]
    if on_line:
        latest = [line_sum.across(*latest)]
    latest = output_sum.spread_experts(*latest)
    grad_query, grad_kv = attend_back(
        after(query, *latest), grad_attended, attended_wide, logs, key_pos[:, None],
        query_pos[None, :], sequence_scale, cosine, sine, kv_parts,
    )
    grad_kv_all = grad_kv.reshape(-1, 2 * KV_WIDTH)

    def joined_grads(part):
        grads = jnp.concatenate(
            [
                dot_nn(input_turned[part], grad_query).astype(low),
                dot_nn(sequence_turned[part], grad_kv_all).astype(low),
            ],
            axis=1,
        )
        return grads.reshape(*relative, -1)

    joined_sum = OwnerSum(*[joined_grads(part) for part in halves])
    grad_kv_sent = jnp.take(
        after(grad_kv, joined_sum.own), own_context ^ ar(contexts), axis=0, mode="clip",
        unique_indices=True,
    )
    grad_kv_parts = trade(grad_kv_sent, "context")
    latest = joined_sum.spread_experts(grad_kv_sent)
    if on_line:
        latest = [line_sum.outward(*latest)]
    own_grad_kv = total_of(after(grad_kv_parts, *latest))
    grad_joined = jnp.concatenate([grad_query, own_grad_kv.astype(low)], axis=1)
    scaled_grad = jnp.concatenate([dot_nt(part, grad_joined) for part in joined_parts], axis=0)
    scaled_grad = pick_rows(scaled_grad, to_absolute).T
    grad_input = (
        grad_middle
        + scaled_grad
        - unit_one * jnp.mean(scaled_grad * unit_one, axis=-1, keepdims=True)
    ).astype(low)
    mixture = total_of(after(mixture_parts, grad_input))
    output = (middle + mixture).astype(low)

    latest = output_sum.spread_contexts(output)
    latest = joined_sum.spread_contexts(*latest)
    if on_line:
        expert_grads.insert(0, line_sum.finish(*latest))
    sum_output = output_sum.finish(*latest)
    sum_joined = joined_sum.finish(sum_output)

    unit_grads = reorder_columns(sum_joined, back=True)
    sum_joined = gain_rows[:, :1] * unit_grads
    sum_gain_one = jnp.sum(joined_low.astype(wide) * unit_grads, axis=1)
    sum_gains = jnp.stack([sum_gain_one, sum_output[:, QUERY_WIDTH]], axis=0)
    sum_output_weight = jnp.einsum(
        "on,dpn->pod",
        query_mat.astype(wide),
        sum_output[:, :QUERY_WIDTH].reshape(slice_rows, PAIRS, PAIR_WIDTH),
        precision=lax.Precision.HIGHEST,
        preferred_element_type=wide,
    ).reshape(QUERY_WIDTH, slice_rows)
    joined_new = adamw(
        joined_weight, joined_first, joined_second, sum_joined, rate_joined, decay_rate
    )
    output_new = adamw(
        output_weight, output_first, output_second, sum_output_weight, rate_output, decay_rate
    )
    gains_new = adamw(norm_gains, gains_first, gains_second, sum_gains, rate_gains, 0.0)
    sum_experts = jnp.concatenate(expert_grads, axis=0)
    expand_new = adamw(
        expand_weight, expand_first, expand_second, sum_experts[:, :, : 2 * FF], rate_expand, decay_rate
    )
    contract_new = adamw(
        contract_weight,
        contract_first,
        contract_second,
        jnp.swapaxes(sum_experts[:, :, 2 * FF :], 1, 2),
        rate_contract,
        decay_rate,
    )
    return (
        output.reshape(1, tokens, width),
        grad_input.reshape(1, tokens, width),
        *joined_new,
        *output_new,
        *gains_new,
        *expand_new,
        *contract_new,
    )


def solution(mesh):
    rows = P(("expert", "dp"), "context", None)
    joined = P(("expert", "context", "dp"), None)
    column = P(None, ("expert", "context", "dp"))
    expand = P("expert", ("context", "dp"), None)
    contract = P("expert", None, ("context", "dp"))
    placed = (
        (rows, rows, P(("expert", "dp"), None), rows, rows)
        + (joined,) * 3
        + (column,) * 6
        + (expand,) * 3
        + (contract,) * 3
    )
    return jax.shard_map(
        body,
        mesh=mesh,
        in_specs=placed,
        out_specs=(rows, rows) + placed[5:],
        check_vma=False,
    )
```

```python
import functools
import math

import jax
import jax.numpy as jnp
import numpy as np
from jax import lax
from jax.experimental import pallas as pl
from jax.experimental.pallas import tpu as pltpu
from jax.sharding import PartitionSpec as P

HEADS = 24
KV_HEADS = 8
HEAD_DIM = 64
FF = 512
TOP = 8
STEP = 10
GROUPS = HEADS // KV_HEADS
PAIRS = KV_HEADS // 2
QUERY_WIDTH = HEADS * HEAD_DIM
KV_WIDTH = KV_HEADS * HEAD_DIM
PAIR_WIDTH = 2 * GROUPS * HEAD_DIM
LANES = 128
VMEM_BYTES = 60 * 1024 * 1024
TOKEN = (8, 128)
SCALAR = pl.BlockSpec(memory_space=pltpu.SMEM)

norm_eps = 1e-06
beta_one = 0.9
beta_two = 0.95
adam_eps = 1e-08
decay_rate = 0.1
rate_joined = 0.08
rate_output = 0.6
rate_gains = 0.6
rate_expand = 0.08
rate_contract = 0.5
masked_score = -1e30

low = jnp.bfloat16
wide = jnp.float32


def adamw(weight, first, second, grad, rate, decay):
    first_new = beta_one * first + (1.0 - beta_one) * grad
    second_new = beta_two * second + (1.0 - beta_two) * grad * grad
    first_hat = first_new / (1.0 - beta_one**STEP)
    second_hat = second_new / (1.0 - beta_two**STEP)
    weight_new = weight - rate * (first_hat / (jnp.sqrt(second_hat) + adam_eps) + decay * weight)
    return (weight_new, first_new, second_new)


def dot_nn(left, right):
    return lax.dot_general(left, right, (((1,), (0,)), ((), ())), preferred_element_type=wide)


def dot_nt(left, right):
    return lax.dot_general(left, right, (((1,), (1,)), ((), ())), preferred_element_type=wide)


def pair_order(groups):
    half = HEAD_DIM // 2
    old = np.arange(2 * groups * HEAD_DIM).reshape(2, groups, 2, half)
    return old.transpose(1, 2, 0, 3).reshape(-1)


def order_matrix(groups):
    order = pair_order(groups)
    size = order.shape[0]
    return jnp.asarray(np.arange(size)[:, None] == order[None, :], dtype=low)


def reorder_columns(rows, back=False):
    count = rows.shape[0]
    query_mat = order_matrix(GROUPS)
    key_mat = order_matrix(1)
    kv = rows[:, QUERY_WIDTH:]
    if back:
        query_mat = query_mat.T
        key_mat = key_mat.T
        kv = jnp.swapaxes(kv.reshape(count, PAIRS, 2, LANES), 1, 2)
    else:
        kv = jnp.swapaxes(kv.reshape(count, 2, PAIRS, LANES), 1, 2)
    exact = lax.Precision.HIGHEST if rows.dtype == wide else None
    query = jnp.einsum(
        "rpo,on->rpn",
        rows[:, :QUERY_WIDTH].reshape(count, PAIRS, PAIR_WIDTH),
        query_mat.astype(rows.dtype),
        precision=exact,
        preferred_element_type=wide,
    ).reshape(count, QUERY_WIDTH)
    others = jnp.einsum(
        "rpo,on->rpn",
        kv.reshape(count, 2 * PAIRS, LANES),
        key_mat.astype(rows.dtype),
        precision=exact,
        preferred_element_type=wide,
    ).reshape(count, 2 * KV_WIDTH)
    return jnp.concatenate([query, others], axis=1)


def swap(block, axis, step):
    count = lax.axis_size(axis)
    return lax.ppermute(block, axis, [(i, i ^ step) for i in range(count)])


def spread(block, axis):
    return [block] + [swap(block, axis, k) for k in range(1, lax.axis_size(axis))]


def after(value, *others):
    return lax.optimization_barrier((value, *others))[0]


def all_after(values, *others):
    count = len(values)
    return list(lax.optimization_barrier((*values, *others))[:count])


def share(block, axis):
    return trade(jnp.broadcast_to(block[None], (lax.axis_size(axis), *block.shape)), axis)


def trade(blocks, axis):
    return lax.all_to_all(blocks, axis, split_axis=0, concat_axis=0, tiled=True)


def in_order(parts, own):
    rows = parts[0].shape[0]
    joined = jnp.zeros((len(parts) * rows, *parts[0].shape[1:]), parts[0].dtype)
    for k, part in enumerate(parts):
        joined = lax.dynamic_update_slice_in_dim(joined, part, (own ^ k) * rows, 0)
    return joined


class OwnerSum:
    def __init__(self, own, other, shape):
        self.own = own.reshape(shape)
        self.came = swap(other, "dp", 1).reshape(shape)

    def spread_experts(self, *others):
        came = after(self.came, *others)
        both = [
            (self.own[k].astype(wide) + came[k].astype(wide)).astype(low)
            for k in range(self.own.shape[0])
        ]
        self.parts = [both[0]] + [swap(both[k], "expert", k) for k in range(1, len(both))]
        return both

    def spread_contexts(self, *others):
        parts = all_after(self.parts, *others)
        total = functools.reduce(jnp.add, [part.astype(wide) for part in parts])
        column = [total[k].astype(low) for k in range(1, total.shape[0])]
        self.parts = [total[0]] + [swap(part, "context", k + 1) for k, part in enumerate(column)]
        return column

    def finish(self, *others):
        parts = all_after(self.parts, *others)
        return functools.reduce(jnp.add, [part.astype(wide) for part in parts])


def call(body, grid, in_specs, out_specs, out_shape, scratch=(), aliases=None):
    order = pl.BlockSpec(TOKEN, lambda *_: (0, 0))

    def ordered(*refs):
        place = len(in_specs)
        body(*refs[:place], *refs[place + 1 :])

    return pl.pallas_call(
        ordered,
        grid=grid,
        in_specs=[*in_specs, order],
        out_specs=out_specs,
        out_shape=out_shape,
        scratch_shapes=list(scratch),
        input_output_aliases=aliases or {},
        compiler_params=pltpu.CompilerParams(vmem_limit_bytes=VMEM_BYTES),
        cost_estimate=pl.CostEstimate(flops=1, bytes_accessed=1, transcendentals=0),
    )


def token(*others):
    return lax.optimization_barrier((jnp.zeros(TOKEN, wide), *others))[0]


def turn(vals, cosine, sine):
    return vals * cosine + pltpu.roll(vals, LANES // 2, 1) * sine


def project_body(count, rows_ref, scale_ref, cos_ref, sin_ref, *refs):
    weight_refs, (query_ref, kv_ref, weight_ref) = refs[:count], refs[count:]
    step = pl.program_id(0)
    depth = weight_refs[0].shape[0]
    for k in range(count):
        weight_ref[k * depth : (k + 1) * depth, :] = weight_refs[k][...]
    total = dot_nn(rows_ref[...], weight_ref[...]) * scale_ref[...]
    block = total.shape[1]
    query_steps = QUERY_WIDTH // block
    cosine, sine = cos_ref[...], sin_ref[...]
    groups = [total[:, i * LANES : (i + 1) * LANES] for i in range(block // LANES)]

    @pl.when(step < query_steps)
    def _():
        for i, group in enumerate(groups):
            turned = turn(group, cosine, sine) * HEAD_DIM**-0.5
            query_ref[:, i * LANES : (i + 1) * LANES] = turned.astype(low)

    @pl.when(step >= query_steps)
    def _():
        for i, group in enumerate(groups):
            kept = turn(group, cosine, sine) if i % 2 == 0 else group
            kv_ref[:, i * LANES : (i + 1) * LANES] = kept.astype(low)


def project(rows, scale, cosine, sine, weights, order):
    tokens, width = rows.shape
    columns = QUERY_WIDTH + 2 * KV_WIDTH
    block = 512
    query_steps = QUERY_WIDTH // block
    depth = weights[0].shape[0]
    whole = lambda shape: pl.BlockSpec(shape, lambda j: (0, 0))
    return call(
        functools.partial(project_body, len(weights)),
        (columns // block,),
        [whole((tokens, width)), whole((tokens, 1)), whole((tokens, LANES)), whole((tokens, LANES))]
        + [pl.BlockSpec((depth, block), lambda j: (0, j))] * len(weights),
        [
            pl.BlockSpec((tokens, block), lambda j: (0, jnp.minimum(j, query_steps - 1))),
            pl.BlockSpec((tokens, block), lambda j: (0, jnp.maximum(j - query_steps, 0))),
        ],
        [
            jax.ShapeDtypeStruct((tokens, QUERY_WIDTH), low),
            jax.ShapeDtypeStruct((tokens, 2 * KV_WIDTH), low),
        ],
        scratch=[pltpu.VMEM((width, block), low)],
    )(rows, scale, cosine, sine, *weights, order)


def lane_of(shape, axis, which):
    place = lax.broadcasted_iota(jnp.int32, shape, axis)
    return ((place // (HEAD_DIM // 2)) % 2) == which


def stack_heads(block, which):
    keep = lane_of((block.shape[0], LANES), 1, which)
    return jnp.concatenate(
        [
            jnp.where(keep, block[:, g * LANES : (g + 1) * LANES], jnp.zeros((), block.dtype))
            for g in range(GROUPS)
        ],
        axis=0,
    )


def allowed_pairs(key_pos, query_pos):
    seen = key_pos <= query_pos
    return jnp.concatenate([seen] * GROUPS, axis=1)


def turned_block(block):
    return block.astype(wide).T.astype(low)


def attend_body(count, query_ref, key_pos_ref, query_pos_ref, *refs):
    kv_refs, (out_ref, out_low_ref, log_ref) = refs[:count], refs[count:]
    tokens = query_ref.shape[0]
    seen = allowed_pairs(key_pos_ref[...], query_pos_ref[...])
    keys = jnp.concatenate([ref[:, :LANES] for ref in kv_refs], axis=0)
    values = jnp.concatenate([turned_block(ref[:, LANES:]) for ref in kv_refs], axis=1)
    outs = []
    for which in range(2):
        query = stack_heads(query_ref[...], which)
        scores = jnp.where(seen, dot_nt(keys, query), masked_score)
        peak = jnp.max(scores, axis=0, keepdims=True)
        weight = jnp.exp(scores - peak)
        total = jnp.sum(weight, axis=0, keepdims=True)
        outs.append(dot_nn(values, weight.astype(low)) / total)
        log_ref[0, which : which + 1, :] = peak + jnp.log(total)
    first = lane_of(outs[0].shape, 0, 0)
    both = jnp.where(first, outs[0], outs[1]).T
    for g in range(GROUPS):
        piece = both[g * tokens : (g + 1) * tokens, :]
        out_ref[:, g * LANES : (g + 1) * LANES] = piece
        out_low_ref[:, g * LANES : (g + 1) * LANES] = piece.astype(low)


def attend(query, key_pos, query_pos, kv_parts, order):
    tokens = query.shape[0]
    count = len(kv_parts)
    seq_len = tokens * count
    pairs = pl.BlockSpec((tokens, PAIR_WIDTH), lambda p: (0, p))
    return call(
        functools.partial(attend_body, count),
        (PAIRS,),
        [
            pairs,
            pl.BlockSpec((seq_len, 1), lambda p: (0, 0)),
            pl.BlockSpec((1, tokens), lambda p: (0, 0)),
        ]
        + [pl.BlockSpec((tokens, 2 * LANES), lambda p: (0, p))] * count,
        [pairs, pairs, pl.BlockSpec((1, 2, GROUPS * tokens), lambda p: (p, 0, 0))],
        [
            jax.ShapeDtypeStruct((tokens, QUERY_WIDTH), wide),
            jax.ShapeDtypeStruct((tokens, QUERY_WIDTH), low),
            jax.ShapeDtypeStruct((PAIRS, 2, GROUPS * tokens), wide),
        ],
    )(query, key_pos, query_pos, *kv_parts, order)


def attend_back_body(count, own_ref, query_ref, grad_ref, out_ref, log_ref, key_pos_ref, query_pos_ref,
                     scale_ref, cos_ref, sin_ref, *refs):
    kv_refs, (grad_query_ref, grad_kv_ref) = refs[:count], refs[count:]
    tokens = query_ref.shape[0]
    grads = grad_ref[...]
    product = jnp.concatenate(
        [
            (grads[:, g * LANES : (g + 1) * LANES].astype(wide)
             * out_ref[:, g * LANES : (g + 1) * LANES]).T
            for g in range(GROUPS)
        ],
        axis=1,
    )
    first = lane_of(product.shape, 0, 0)
    delta = [
        jnp.sum(jnp.where(first, product, 0.0), axis=0, keepdims=True),
        jnp.sum(jnp.where(first, 0.0, product), axis=0, keepdims=True),
    ]
    seen = allowed_pairs(key_pos_ref[...], query_pos_ref[...])
    keys = jnp.concatenate([ref[:, :LANES] for ref in kv_refs], axis=0)
    values = jnp.concatenate([ref[:, LANES:] for ref in kv_refs], axis=0)
    keys_turned = jnp.concatenate([turned_block(ref[:, :LANES]) for ref in kv_refs], axis=1)
    grad_key, grad_value, grad_query = None, None, []
    for which in range(2):
        query = stack_heads(query_ref[...], which)
        head = stack_heads(grads, which)
        scores = jnp.where(seen, dot_nt(keys, query), masked_score)
        probs = jnp.exp(scores - log_ref[0, which : which + 1, :])
        grad_probs = dot_nt(values, head)
        grad_scores = (probs * (grad_probs - delta[which])).astype(low)
        part_value = dot_nn(probs.astype(low), head)
        part_key = dot_nn(grad_scores, query)
        grad_query.append(dot_nn(keys_turned, grad_scores))
        grad_value = part_value if grad_value is None else grad_value + part_value
        grad_key = part_key if grad_key is None else grad_key + part_key
    scale, cosine, sine = scale_ref[...], cos_ref[...], sin_ref[...]
    for k in range(count):
        rows = slice(k * tokens, (k + 1) * tokens)
        grad_kv_ref[own_ref[0] ^ k, :, :LANES] = grad_key[rows, :].astype(low)
        grad_kv_ref[own_ref[0] ^ k, :, LANES:] = grad_value[rows, :].astype(low)
    first = lane_of(grad_query[0].shape, 0, 0)
    both = (jnp.where(first, grad_query[0], grad_query[1]) * HEAD_DIM**-0.5).T
    for g in range(GROUPS):
        piece = both[g * tokens : (g + 1) * tokens, :]
        back = turn(piece, cosine, -sine) * scale
        grad_query_ref[:, g * LANES : (g + 1) * LANES] = back.astype(low)


def attend_back(
    own, query, grads, out, logs, key_pos, query_pos, scale, cosine, sine, kv_parts, order
):
    tokens = query.shape[0]
    count = len(kv_parts)
    seq_len = tokens * count
    pairs = pl.BlockSpec((tokens, PAIR_WIDTH), lambda p: (0, p))
    whole = lambda shape: pl.BlockSpec(shape, lambda p: (0, 0))
    part = pl.BlockSpec((tokens, 2 * LANES), lambda p: (0, p))
    return call(
        functools.partial(attend_back_body, count),
        (PAIRS,),
        [
            SCALAR,
            pairs,
            pairs,
            pairs,
            pl.BlockSpec((1, 2, GROUPS * tokens), lambda p: (p, 0, 0)),
            whole((seq_len, 1)),
            whole((1, tokens)),
            whole((tokens, 1)),
            whole((tokens, LANES)),
            whole((tokens, LANES)),
        ]
        + [part] * count,
        [pairs, pl.BlockSpec((count, tokens, 2 * LANES), lambda p: (0, 0, p))],
        [
            jax.ShapeDtypeStruct((tokens, QUERY_WIDTH), low),
            jax.ShapeDtypeStruct((count, tokens, 2 * KV_WIDTH), low),
        ],
    )(own, query, grads, out, logs, key_pos, query_pos, scale, cosine, sine, *kv_parts, order)


def hidden_body(count, first, own_ref, grads_ref, gate_ref, weight_ref, *refs):
    part_refs, (hidden_ref, back_ref, rows_ref) = refs[:count], refs[count:]
    expert, place = pl.program_id(0), pl.program_id(1)
    block = grads_ref.shape[0]
    tokens = part_refs[0].shape[0]

    @pl.when((expert == 0) & (place == 0))
    def _():
        for k, part_ref in enumerate(part_refs):
            start = pl.multiple_of((own_ref[0] ^ k) * tokens, tokens)
            rows_ref[pl.ds(start, tokens), :] = part_ref[...]

    rows = rows_ref[pl.ds(pl.multiple_of(place * block, block), block), :]
    grads = grads_ref[...]
    lane = lax.broadcasted_iota(jnp.int32, gate_ref.shape, 1)
    weight = jnp.sum(
        jnp.where(lane == expert + first, gate_ref[...], 0.0), axis=1, keepdims=True
    )
    step = 256
    for h in range(0, FF, step):
        gate = dot_nn(rows, weight_ref[0, :, h : h + step])
        up = dot_nn(rows, weight_ref[0, :, FF + h : FF + h + step])
        grad_hidden = dot_nn(grads, weight_ref[0, :, 2 * FF + h : 2 * FF + h + step]) * weight
        sigmoid = 1.0 / (1.0 + jnp.exp(-gate))
        active = gate * sigmoid
        hidden_ref[0, :, h : h + step] = (active * up * weight).astype(low)
        slope = sigmoid + active * (1.0 - sigmoid)
        back_ref[0, :, h : h + step] = (grad_hidden * up * slope).astype(low)
        back_ref[0, :, FF + h : FF + h + step] = (grad_hidden * active).astype(low)


def expert_hidden(own, parts, grads, gates, first, weights, order):
    tokens, width = grads.shape
    experts = weights.shape[0]
    block = min(tokens, 1024)
    part_rows = parts[0].shape[0]
    return call(
        functools.partial(hidden_body, len(parts), first),
        (experts, tokens // block),
        [
            SCALAR,
            pl.BlockSpec((block, width), lambda e, t: (t, 0)),
            pl.BlockSpec((block, gates.shape[1]), lambda e, t: (t, 0)),
            pl.BlockSpec((1, width, 3 * FF), lambda e, t: (e, 0, 0)),
        ]
        + [
            pl.BlockSpec((part_rows, width), lambda e, t: (0, 0), pipeline_mode=pl.Buffered(1))
        ]
        * len(parts),
        [
            pl.BlockSpec((1, block, FF), lambda e, t: (e, t, 0)),
            pl.BlockSpec((1, block, 2 * FF), lambda e, t: (e, t, 0)),
        ],
        [
            jax.ShapeDtypeStruct((experts, tokens, FF), low),
            jax.ShapeDtypeStruct((experts, tokens, 2 * FF), low),
        ],
        scratch=[pltpu.VMEM((tokens, width), low)],
    )(own, grads, gates, weights, *parts, order)


def turn_body(count, own_ref, *refs):
    part_refs, out_ref = refs[:count], refs[count]
    tokens = part_refs[0].shape[0]
    for k, part_ref in enumerate(part_refs):
        start = pl.multiple_of((own_ref[0] ^ k) * tokens, tokens)
        out_ref[:, pl.ds(start, tokens)] = turned_block(part_ref[...])


def turn_rows(own, parts, order):
    count = len(parts)
    if count == 1:
        count = parts[0].shape[0] // 256
    width = parts[0].shape[1]
    tokens = parts[0].shape[0] if len(parts) > 1 else 256
    specs = [
        pl.BlockSpec((tokens, width), (lambda i, k=k: (k, 0)) if len(parts) == 1 else (lambda i: (0, 0)))
        for k in range(count)
    ]
    return call(
        functools.partial(turn_body, count),
        (1,),
        [SCALAR, *specs],
        pl.BlockSpec((width, count * tokens), lambda i: (0, 0)),
        jax.ShapeDtypeStruct((width, count * tokens), low),
    )(own, *(parts * count if len(parts) == 1 else parts), order)


def weight_grad_body(sizes, rows_ref, grads_ref, *refs):
    count = len(sizes)
    back_refs, hidden_refs, out_ref = refs[:count], refs[count : 2 * count], refs[2 * count]
    step = pl.program_id(0)
    start = 0
    for back_ref, hidden_ref, size in zip(back_refs, hidden_refs, sizes):

        @pl.when((step >= start) & (step < start + size))
        def _():
            out_ref[0, :, : 2 * FF] = dot_nn(rows_ref[...], back_ref[0]).astype(low)
            out_ref[0, :, 2 * FF :] = dot_nn(grads_ref[...], hidden_ref[0]).astype(low)

        start += size


def expert_weight_grads(rows_turned, grads_turned, parts, order):
    width, tokens = rows_turned.shape
    sizes = [last - first for _, _, first, last in parts]
    firsts = [first for _, _, first, _ in parts]
    starts = [sum(sizes[:i]) for i in range(len(sizes))]
    block = width // 2
    place = lambda e, first, start, size: first + jnp.clip(e - start, 0, size - 1)

    def specs(depth):
        return [
            pl.BlockSpec((1, tokens, depth), lambda e, m, f=f, s=s, n=n: (place(e, f, s, n), 0, 0))
            for f, s, n in zip(firsts, starts, sizes)
        ]

    return call(
        functools.partial(weight_grad_body, sizes),
        (sum(sizes), width // block),
        [
            pl.BlockSpec((block, tokens), lambda e, m: (m, 0)),
            pl.BlockSpec((block, tokens), lambda e, m: (m, 0)),
            *specs(2 * FF),
            *specs(FF),
        ],
        pl.BlockSpec((1, block, 3 * FF), lambda e, m: (e, m, 0)),
        jax.ShapeDtypeStruct((sum(sizes), width, 3 * FF), low),
    )(
        rows_turned,
        grads_turned,
        *[back for _, back, _, _ in parts],
        *[hidden for hidden, _, _, _ in parts],
        order,
    )


def combine_body(sizes, own_ref, *refs):
    count = len(sizes)
    part_refs, weight_refs = refs[:count], refs[count : 2 * count]
    out_refs, total_ref = refs[2 * count : -1], refs[-1]
    step = pl.program_id(0)

    @pl.when(step == 0)
    def _():
        total_ref[...] = jnp.zeros_like(total_ref)

    start = 0
    for part_ref, weight_ref, size in zip(part_refs, weight_refs, sizes):

        @pl.when((step >= start) & (step < start + size))
        def _():
            total_ref[...] += dot_nt(part_ref[0], weight_ref[0])

        start += size

    @pl.when(step == start - 1)
    def _():
        tokens = out_refs[0].shape[0]
        for k, out_ref in enumerate(out_refs):
            place = pl.multiple_of((own_ref[0] ^ k) * tokens, tokens)
            out_ref[...] = total_ref[pl.ds(place, tokens), :].astype(low)


def combine(own, owners, parts, weights, column, order):
    tokens, depth = parts[0].shape[1:]
    width = weights[0].shape[1]
    sizes = [w.shape[0] for w in weights]
    starts = [sum(sizes[:i]) for i in range(len(sizes))]
    place = lambda e, start, size: jnp.clip(e - start, 0, size - 1)
    part_specs = [
        pl.BlockSpec((1, tokens, depth), lambda e, s=s, n=n: (place(e, s, n), 0, 0))
        for s, n in zip(starts, sizes)
    ]
    weight_specs = [
        pl.BlockSpec((1, width, depth), lambda e, s=s, n=n: (place(e, s, n), 0, column))
        for s, n in zip(starts, sizes)
    ]
    return call(
        functools.partial(combine_body, sizes),
        (sum(sizes),),
        [SCALAR] + part_specs + weight_specs,
        [pl.BlockSpec((tokens // owners, width), lambda e: (0, 0))] * owners,
        [jax.ShapeDtypeStruct((tokens // owners, width), low)] * owners,
        scratch=[pltpu.VMEM((tokens, width), wide)],
    )(own, *parts, *weights, order)


def norm_back_body(count, scale_ref, gain_ref, middle_ref, cotangent_ref, weight_ref, *refs):
    part_refs = refs[:count]
    middle_grad_ref, turned_ref, attended_ref, gain_grad_ref, proj_ref = refs[count:]

    @pl.when(pl.program_id(0) == 0)
    def _():
        grad = functools.reduce(jnp.add, [ref[...].astype(wide) for ref in part_refs])
        scale = scale_ref[...]
        unit = middle_ref[...] * scale
        gain_grad_ref[...] = jnp.sum(grad * unit, axis=0, keepdims=True)
        grad = grad * gain_ref[...]
        mean = jnp.mean(grad * unit, axis=1, keepdims=True)
        grad = cotangent_ref[...].astype(wide) + scale * (grad - unit * mean)
        middle_grad_ref[...] = grad
        proj_ref[...] = grad.astype(low)
        turned_ref[...] = grad.T.astype(low)

    attended_ref[...] = dot_nn(proj_ref[...], weight_ref[...]).astype(low)


def norm_back_two(parts, middle, scale, gain, cotangent, output_pack, order):
    tokens, width = middle.shape
    block = 512
    whole = lambda shape: pl.BlockSpec(shape, lambda j: (0, 0))
    return call(
        functools.partial(norm_back_body, len(parts)),
        (QUERY_WIDTH // block,),
        [
            whole((tokens, 1)),
            whole((1, width)),
            whole((tokens, width)),
            whole((tokens, width)),
            pl.BlockSpec((width, block), lambda j: (0, j)),
        ]
        + [whole((tokens, width))] * len(parts),
        [
            whole((tokens, width)),
            whole((width, tokens)),
            pl.BlockSpec((tokens, block), lambda j: (0, j)),
            whole((1, width)),
        ],
        [
            jax.ShapeDtypeStruct((tokens, width), wide),
            jax.ShapeDtypeStruct((width, tokens), low),
            jax.ShapeDtypeStruct((tokens, QUERY_WIDTH), low),
            jax.ShapeDtypeStruct((1, width), wide),
        ],
        scratch=[pltpu.VMEM((tokens, width), low)],
    )(scale, gain, middle, cotangent, output_pack, *parts, order)


def outer_body(input_ref, proj_ref, gain_ref, query_ref, attended_ref, out_ref):
    out_ref[:, :QUERY_WIDTH] = dot_nn(input_ref[...], query_ref[...]).astype(low)
    out_ref[:, QUERY_WIDTH : 2 * QUERY_WIDTH] = dot_nn(proj_ref[...], attended_ref[...]).astype(low)
    out_ref[:, 2 * QUERY_WIDTH :] = jnp.broadcast_to(
        gain_ref[...], (gain_ref.shape[0], LANES)
    ).astype(low)


def outer_grads(half, cores, input_turned, proj_turned, gain_grads, grad_query, attended, order):
    width, tokens = input_turned.shape
    rows = width // cores
    part = lambda columns: pl.BlockSpec((rows, columns), lambda i: (half, 0))
    whole = pl.BlockSpec((tokens, QUERY_WIDTH), lambda i: (0, 0))
    columns = 2 * QUERY_WIDTH + LANES
    return call(
        outer_body,
        (1,),
        [part(tokens), part(tokens), part(1), whole, whole],
        pl.BlockSpec((rows, columns), lambda i: (0, 0)),
        jax.ShapeDtypeStruct((rows, columns), low),
    )(input_turned, proj_turned, gain_grads, grad_query, attended, order)


def kv_body(parts_ref, scale_ref, cos_ref, sin_ref, input_ref, grad_ref, *out_refs):
    total = jnp.sum(parts_ref[...].astype(wide), axis=0)
    cosine, sine, scale = cos_ref[...], sin_ref[...], scale_ref[...]
    for i in range(2 * PAIRS):
        group = total[:, i * LANES : (i + 1) * LANES]
        group = turn(group, cosine, -sine) if i % 2 == 0 else group
        grad_ref[:, i * LANES : (i + 1) * LANES] = (group * scale).astype(low)
    grads = grad_ref[...]
    rows = out_refs[0].shape[0]
    for k, out_ref in enumerate(out_refs):
        out_ref[...] = dot_nn(input_ref[k * rows : (k + 1) * rows, :], grads).astype(low)


def kv_grads(cores, parts, scale, cosine, sine, input_turned, order):
    tokens, columns = parts.shape[1:]
    width = input_turned.shape[0]
    shapes = [(tokens, columns)] + [(width // cores, columns)] * cores
    whole = lambda shape: pl.BlockSpec(shape, lambda i: (0,) * len(shape))
    return call(
        kv_body,
        (1,),
        [
            whole(parts.shape),
            whole((tokens, 1)),
            whole((tokens, LANES)),
            whole((tokens, LANES)),
            whole((width, tokens)),
        ],
        [whole(shape) for shape in shapes],
        [jax.ShapeDtypeStruct(shape, low) for shape in shapes],
    )(parts, scale, cosine, sine, input_turned, order)


def input_body(count, rows, place_ref, query_ref, kv_ref, scale_ref, input_ref, middle_ref, *refs):
    weight_refs, (out_ref, turned_ref) = refs[:count], refs[count:]
    weights = jnp.concatenate([ref[...] for ref in weight_refs], axis=0)
    part = dot_nt(weights[:, :QUERY_WIDTH], query_ref[...])
    part += dot_nt(weights[:, QUERY_WIDTH:], kv_ref[...])
    for i in range(part.shape[0] // rows):
        start = pl.multiple_of(place_ref[i] * rows, rows)
        turned_ref[pl.ds(start, rows), :] = part[i * rows : (i + 1) * rows, :]
    grad = turned_ref[...].T
    unit = input_ref[...].astype(wide) * scale_ref[...]
    mean = jnp.mean(grad * unit, axis=1, keepdims=True)
    out_ref[...] = (middle_ref[...] + grad - unit * mean).astype(low)


def input_grads(place, grad_query, grad_kv, scale, rows, grad_middle, weights, order):
    tokens, width = rows.shape
    whole = lambda array: pl.BlockSpec(array.shape, lambda i: (0, 0))
    operands = [grad_query, grad_kv, scale, rows, grad_middle, *weights]
    return call(
        functools.partial(input_body, len(weights), width // place.shape[0]),
        (1,),
        [SCALAR] + [whole(operand) for operand in operands],
        pl.BlockSpec((tokens, width), lambda i: (0, 0)),
        jax.ShapeDtypeStruct((tokens, width), low),
        scratch=[pltpu.VMEM((width, tokens), wide)],
    )(place, *operands, order)


def adam_body(held, grad_ref, *refs):
    expand, contract, refs = refs[:3], refs[3:6], refs[6 + held :]
    grads = grad_ref[0].astype(wide)
    split = expand[0].shape[2]
    for arrays, grad, rate, out_refs in (
        (expand, grads[:, :split], rate_expand, refs[:3]),
        (contract, grads[:, split:].T, rate_contract, refs[3:]),
    ):
        results = adamw(*[array[0] for array in arrays], grad, rate, decay_rate)
        for out_ref, result in zip(out_refs, results):
            out_ref[0] = result


def adam_experts(first, grads, arrays, held, order):
    count = grads.shape[0]
    held = held or []
    block = lambda array: pl.BlockSpec((1, *array.shape[1:]), lambda e: (first + e, 0, 0))
    return call(
        functools.partial(adam_body, len(held)),
        (count,),
        [pl.BlockSpec((1, *grads.shape[1:]), lambda e: (e, 0, 0))]
        + [block(array) for array in arrays]
        + [pl.BlockSpec(memory_space=pl.ANY)] * len(held),
        [block(array) for array in arrays],
        [jax.ShapeDtypeStruct(array.shape, wide) for array in arrays],
        aliases={1 + len(arrays) + i: i for i in range(len(held))},
    )(grads, *arrays, *held, order)


def body(
    layer_input,
    cotangent,
    block_order,
    routes,
    route_gates,
    joined_weight,
    joined_first,
    joined_second,
    output_weight,
    output_first,
    output_second,
    norm_gains,
    gains_first,
    gains_second,
    expand_weight,
    expand_first,
    expand_second,
    contract_weight,
    contract_first,
    contract_second,
):
    experts_dev = expand_weight.shape[0]
    owners = lax.axis_size("expert")
    contexts = lax.axis_size("context")
    cores = lax.axis_size("dp")
    experts = experts_dev * owners
    tokens = layer_input.shape[1]
    width = layer_input.shape[2]
    half_block = tokens // 2
    slice_rows = joined_weight.shape[0]
    own_expert = lax.axis_index("expert")
    own_context = lax.axis_index("context")
    own_core = lax.axis_index("dp")

    gain_rows = norm_gains.astype(low).astype(wide).T
    joined_low = joined_weight.astype(low)
    joined_shard = reorder_columns((gain_rows[:, :1] * joined_low.astype(wide)).astype(low)).astype(low)
    query_mat = order_matrix(GROUPS)
    output_shard = jnp.einsum(
        "pod,on->dpn",
        output_weight.astype(low).reshape(PAIRS, PAIR_WIDTH, slice_rows),
        query_mat,
        preferred_element_type=wide,
    ).reshape(slice_rows, QUERY_WIDTH).astype(low)
    gain_column = jnp.broadcast_to(gain_rows[:, 1:].astype(low), (slice_rows, LANES))
    columns = joined_shard.shape[1]
    shard = jnp.concatenate([joined_shard, output_shard, gain_column], axis=1)

    bounds = [0, experts_dev // 2, experts_dev]
    chunks = list(zip(bounds[:-1], bounds[1:]))
    expert_low = [
        jnp.concatenate(
            [
                expand_weight[a:b].astype(low),
                jnp.swapaxes(contract_weight[a:b].astype(low), 1, 2),
            ],
            axis=2,
        )
        for a, b in chunks
    ]
    line, *expert_low = lax.optimization_barrier(
        (jnp.concatenate(spread(shard, "context"), axis=0), *expert_low)
    )
    joined_mine = spread(line[:, :columns], "expert")
    joined_parts = joined_mine + [swap(part, "dp", 1) for part in joined_mine]
    output_mine = share(after(line[:, columns:], *joined_mine), "expert")
    gather_expert = lambda part: lax.all_gather(part, ("context", "dp"), axis=1, tiled=True)
    expert_full = [gather_expert(expert_low[0])]

    ar = lambda n: jnp.arange(n, dtype=jnp.int32)
    to_relative = (
        ((own_expert ^ ar(owners))[None, :, None] * contexts + (own_context ^ ar(contexts))[None, None, :])
        * cores
        + (own_core ^ ar(cores))[:, None, None]
    ).reshape(-1)
    to_absolute = (
        (own_core ^ ar(cores))[None, None, :] * owners + (own_expert ^ ar(owners))[:, None, None]
    ) * contexts + (own_context ^ ar(contexts))[None, :, None]
    to_absolute = to_absolute.reshape(-1)
    slices = owners * contexts * cores

    def pick_rows(rows, index):
        return jnp.take(
            rows.reshape(slices, slice_rows, -1), index, axis=0, mode="clip", unique_indices=True
        ).reshape(rows.shape)

    hits = routes[0][:, :, None] == ar(experts)[None, None, :]
    gate_table = jnp.sum(jnp.where(hits, route_gates[0][:, :, None], 0.0), axis=1)
    gate_table = gate_table.reshape(tokens, owners, experts_dev)
    gate_sent = [
        lax.dynamic_index_in_dim(gate_table, own_expert ^ k, axis=1, keepdims=False)
        for k in range(owners)
    ]
    gate_parts = [gate_sent[0]] + [swap(gate_sent[k], "expert", k) for k in range(1, owners)]
    gates = in_order(gate_parts, own_expert)
    own = own_expert.reshape(1)
    zero = jnp.zeros((1,), jnp.int32)

    order = block_order[0]
    offsets = ar(half_block)

    def places_of(index):
        mine = lax.dynamic_slice_in_dim(order, 2 * index, 2)
        return (mine[:, None] * half_block + offsets[None, :]).reshape(-1)

    query_pos = places_of(own_context)
    key_pos = jnp.concatenate([places_of(own_context ^ k) for k in range(contexts)])
    half = HEAD_DIM // 2
    freq = jnp.exp(ar(half).astype(wide) * (2.0 / HEAD_DIM) * -math.log(10000.0))
    angle = query_pos.astype(wide)[:, None] * freq[None, :]
    cosine = jnp.tile(jnp.cos(angle), (1, 4))
    sine = jnp.sin(angle)
    sine = jnp.concatenate([-sine, -sine, sine, sine], axis=1)

    low_input = layer_input[0]
    resid = low_input.astype(wide)
    scale_one = lax.rsqrt(jnp.mean(resid * resid, axis=-1, keepdims=True) + norm_eps)
    unit_one = resid * scale_one
    input_turned = pick_rows(low_input.T, to_relative)
    input_relative = input_turned.T
    query, kv = project(input_relative, scale_one, cosine, sine, joined_parts, token())
    kv_parts = spread(kv, "context")
    output_mine = after(output_mine, kv)
    output_parts = [output_mine, swap(output_mine, "dp", 1)]
    out_grads = share(after(cotangent[0], output_mine), "expert").reshape(-1, width)
    output_place = (
        (own_core ^ ar(cores))[None, None, :] * owners + ar(owners)[:, None, None]
    ) * contexts + (own_context ^ ar(contexts))[None, :, None]
    output_pack = pick_rows(
        jnp.concatenate([part.reshape(-1, output_mine.shape[-1]) for part in output_parts], axis=0),
        output_place.reshape(-1),
    )
    output_turned = output_pack[:, :QUERY_WIDTH]
    gain_two = output_pack[:, QUERY_WIDTH].astype(wide)[None, :]
    kv_parts = all_after(kv_parts, output_pack)
    kv_parts, later = lax.optimization_barrier((kv_parts, expert_low[1:]))
    expert_full += [gather_expert(part) for part in later]
    attended_wide, attended, logs = attend(
        query, key_pos[:, None], query_pos[None, :], kv_parts, token()
    )
    middle = resid + dot_nt(attended, output_turned)
    scale_two = lax.rsqrt(jnp.mean(middle * middle, axis=-1, keepdims=True) + norm_eps)
    unit_two = middle * scale_two
    normed_two = (unit_two * gain_two).astype(low)

    row_parts = spread(normed_two, "expert")
    out_grads_turned = turn_rows(zero, [out_grads], token(normed_two))

    def grads_of(hidden, back, *others):
        return expert_weight_grads(
            rows_turned, out_grads_turned, [(hidden, back, 0, back.shape[0])], token(*others)
        )

    def to_owners(grads):
        return lax.psum_scatter(grads, ("context", "dp"), scatter_dimension=1, tiled=True)

    def to_tokens(parts):
        return [parts[0]] + [swap(parts[k], "expert", k) for k in range(1, owners)]

    cut = bounds[1]
    first_unit = expert_hidden(
        own, row_parts, out_grads, gates, 0, expert_full[0], token(out_grads_turned)
    )
    rows_turned = turn_rows(own, row_parts, token(first_unit[0]))
    first_grads = grads_of(*first_unit)
    second_unit = expert_hidden(
        own, row_parts, out_grads, gates, cut, expert_full[1], token(first_grads)
    )
    backs = [first_unit[1], second_unit[1]]
    grad_sent = combine(own, owners, backs, expert_full, 0, token())
    first_sum = to_owners(first_grads)
    grad_parts = to_tokens(grad_sent)
    second_grads = grads_of(*second_unit, *grad_sent)
    mixture_sent = combine(
        own, owners, [first_unit[0], second_unit[0]], expert_full, 2, token(second_grads)
    )
    mixture_parts = to_tokens(mixture_sent)

    grad_middle, proj_turned, grad_attended, gain_grad_two = norm_back_two(
        grad_parts, middle, scale_two, gain_two, cotangent[0], output_pack, token(*mixture_sent)
    )
    grad_query, grad_kv = attend_back(
        own_context.reshape(1), query, grad_attended, attended_wide, logs, key_pos[:, None], query_pos[None, :],
        scale_one, cosine, sine, kv_parts, token(grad_attended, first_sum),
    )
    expert_grads = [first_sum, to_owners(after(second_grads, first_sum))]
    grad_kv_parts = trade(grad_kv, "context")

    mixture = functools.reduce(
        jnp.add, [part.astype(wide) for part in all_after(mixture_parts, grad_query)]
    )
    output = (middle + mixture).astype(low)
    relative = (owners, contexts, slice_rows, -1)
    proj_turned = pick_rows(after(proj_turned, output), to_relative)
    gain_grads = pick_rows(gain_grad_two.reshape(width, 1), to_relative)
    other, own_part = [
        outer_grads(
            half, cores, input_turned, proj_turned, gain_grads, grad_query, attended, token()
        )
        for half in (1, 0)
    ]
    query_sum = OwnerSum(own_part, other, relative)
    latest = query_sum.spread_experts(own_part)
    latest = query_sum.spread_contexts(*latest)
    own_grad_kv, *kv_parts_sent = kv_grads(
        cores, grad_kv_parts, scale_one, cosine, sine, input_turned, token(*latest)
    )
    kv_sum = OwnerSum(*kv_parts_sent, relative)
    latest = kv_sum.spread_experts(own_grad_kv)
    if slice_rows % 16 == 0:
        grad_input = input_grads(
            to_relative, grad_query, own_grad_kv, scale_one, low_input, grad_middle, joined_parts,
            token(*latest),
        )
    else:
        grad_joined = jnp.concatenate([grad_query, own_grad_kv], axis=1)
        scaled_grad = jnp.concatenate([dot_nt(part, grad_joined) for part in joined_parts], axis=0)
        scaled_grad = pick_rows(scaled_grad, to_absolute).T
        grad_input = (
            grad_middle
            + scaled_grad
            - unit_one * jnp.mean(scaled_grad * unit_one, axis=-1, keepdims=True)
        ).astype(low)

    latest = kv_sum.spread_contexts(grad_input)
    arrays = [
        expand_weight, expand_first, expand_second, contract_weight, contract_first, contract_second
    ]
    expert_new = adam_experts(0, expert_grads[0], arrays, None, token(*latest))
    expert_new = adam_experts(cut, expert_grads[1], arrays, expert_new, token())
    expand_new, contract_new = expert_new[:3], expert_new[3:]
    sum_query = query_sum.finish(*latest, expand_new[0])
    sum_kv = kv_sum.finish(sum_query)
    sum_output = sum_query[:, QUERY_WIDTH:]
    sum_joined = jnp.concatenate([sum_query[:, :QUERY_WIDTH], sum_kv], axis=1)

    unit_grads = reorder_columns(sum_joined, back=True)
    sum_joined = gain_rows[:, :1] * unit_grads
    sum_gain_one = jnp.sum(joined_low.astype(wide) * unit_grads, axis=1)
    sum_gains = jnp.stack([sum_gain_one, sum_output[:, QUERY_WIDTH]], axis=0)
    sum_output_weight = jnp.einsum(
        "on,dpn->pod",
        query_mat.astype(wide),
        sum_output[:, :QUERY_WIDTH].reshape(slice_rows, PAIRS, PAIR_WIDTH),
        precision=lax.Precision.HIGHEST,
        preferred_element_type=wide,
    ).reshape(QUERY_WIDTH, slice_rows)
    joined_new = adamw(
        joined_weight, joined_first, joined_second, sum_joined, rate_joined, decay_rate
    )
    output_new = adamw(
        output_weight, output_first, output_second, sum_output_weight, rate_output, decay_rate
    )
    gains_new = adamw(norm_gains, gains_first, gains_second, sum_gains, rate_gains, 0.0)
    return (
        output.reshape(1, tokens, width),
        grad_input.reshape(1, tokens, width),
        *joined_new,
        *output_new,
        *gains_new,
        *expand_new,
        *contract_new,
    )


def solution(mesh):
    rows = P(("expert", "dp"), "context", None)
    joined = P(("expert", "context", "dp"), None)
    column = P(None, ("expert", "context", "dp"))
    expand = P("expert", ("context", "dp"), None)
    contract = P("expert", None, ("context", "dp"))
    placed = (
        (rows, rows, P(("expert", "dp"), None), rows, rows)
        + (joined,) * 3
        + (column,) * 6
        + (expand,) * 3
        + (contract,) * 3
    )
    return jax.shard_map(
        body,
        mesh=mesh,
        in_specs=placed,
        out_specs=(rows, rows) + placed[5:],
        check_vma=False,
    )
```

```python
import functools
import math

import jax
import jax.numpy as jnp
import numpy as np
from jax import lax
from jax.experimental import pallas as pl
from jax.experimental.pallas import tpu as pltpu
from jax.sharding import PartitionSpec as P

HEADS = 24
KV_HEADS = 8
HEAD_DIM = 64
FF = 512
TOP = 8
STEP = 10
GROUPS = HEADS // KV_HEADS
PAIRS = KV_HEADS // 2
QUERY_WIDTH = HEADS * HEAD_DIM
KV_WIDTH = KV_HEADS * HEAD_DIM
PAIR_WIDTH = 2 * GROUPS * HEAD_DIM
LANES = 128
VMEM_BYTES = 60 * 1024 * 1024
TOKEN = (8, 128)
SCALAR = pl.BlockSpec(memory_space=pltpu.SMEM)

norm_eps = 1e-06
beta_one = 0.9
beta_two = 0.95
adam_eps = 1e-08
decay_rate = 0.1
rate_joined = 0.08
rate_output = 0.6
rate_gains = 0.6
rate_expand = 0.08
rate_contract = 0.5
masked_score = -1e30

low = jnp.bfloat16
wide = jnp.float32


def adamw(weight, first, second, grad, rate, decay):
    first_new = beta_one * first + (1.0 - beta_one) * grad
    second_new = beta_two * second + (1.0 - beta_two) * grad * grad
    first_hat = first_new / (1.0 - beta_one**STEP)
    second_hat = second_new / (1.0 - beta_two**STEP)
    weight_new = weight - rate * (first_hat / (jnp.sqrt(second_hat) + adam_eps) + decay * weight)
    return (weight_new, first_new, second_new)


def dot_nn(left, right):
    return lax.dot_general(left, right, (((1,), (0,)), ((), ())), preferred_element_type=wide)


def dot_nt(left, right):
    return lax.dot_general(left, right, (((1,), (1,)), ((), ())), preferred_element_type=wide)


def pair_order(groups):
    half = HEAD_DIM // 2
    old = np.arange(2 * groups * HEAD_DIM).reshape(2, groups, 2, half)
    return old.transpose(1, 2, 0, 3).reshape(-1)


def order_matrix(groups):
    order = pair_order(groups)
    size = order.shape[0]
    return jnp.asarray(np.arange(size)[:, None] == order[None, :], dtype=low)


def reorder_columns(rows, back=False):
    count = rows.shape[0]
    query_mat = order_matrix(GROUPS)
    key_mat = order_matrix(1)
    kv = rows[:, QUERY_WIDTH:]
    if back:
        query_mat = query_mat.T
        key_mat = key_mat.T
        kv = jnp.swapaxes(kv.reshape(count, PAIRS, 2, LANES), 1, 2)
    else:
        kv = jnp.swapaxes(kv.reshape(count, 2, PAIRS, LANES), 1, 2)
    exact = lax.Precision.HIGHEST if rows.dtype == wide else None
    query = jnp.einsum(
        "rpo,on->rpn",
        rows[:, :QUERY_WIDTH].reshape(count, PAIRS, PAIR_WIDTH),
        query_mat.astype(rows.dtype),
        precision=exact,
        preferred_element_type=wide,
    ).reshape(count, QUERY_WIDTH)
    others = jnp.einsum(
        "rpo,on->rpn",
        kv.reshape(count, 2 * PAIRS, LANES),
        key_mat.astype(rows.dtype),
        precision=exact,
        preferred_element_type=wide,
    ).reshape(count, 2 * KV_WIDTH)
    return jnp.concatenate([query, others], axis=1)


def swap(block, axis, step):
    count = lax.axis_size(axis)
    return lax.ppermute(block, axis, [(i, i ^ step) for i in range(count)])


def spread(block, axis):
    return [block] + [swap(block, axis, k) for k in range(1, lax.axis_size(axis))]


def after(value, *others):
    return lax.optimization_barrier((value, *others))[0]


def all_after(values, *others):
    count = len(values)
    return list(lax.optimization_barrier((*values, *others))[:count])


def share(block, axis):
    return trade(jnp.broadcast_to(block[None], (lax.axis_size(axis), *block.shape)), axis)


def trade(blocks, axis):
    return lax.all_to_all(blocks, axis, split_axis=0, concat_axis=0, tiled=True)


def in_order(parts, own):
    rows = parts[0].shape[0]
    joined = jnp.zeros((len(parts) * rows, *parts[0].shape[1:]), parts[0].dtype)
    for k, part in enumerate(parts):
        joined = lax.dynamic_update_slice_in_dim(joined, part, (own ^ k) * rows, 0)
    return joined


def call(body, grid, in_specs, out_specs, out_shape, scratch=(), aliases=None):
    order = pl.BlockSpec(TOKEN, lambda *_: (0, 0))

    def ordered(*refs):
        place = len(in_specs)
        body(*refs[:place], *refs[place + 1 :])

    return pl.pallas_call(
        ordered,
        grid=grid,
        in_specs=[*in_specs, order],
        out_specs=out_specs,
        out_shape=out_shape,
        scratch_shapes=list(scratch),
        input_output_aliases=aliases or {},
        compiler_params=pltpu.CompilerParams(vmem_limit_bytes=VMEM_BYTES),
        cost_estimate=pl.CostEstimate(flops=1, bytes_accessed=1, transcendentals=0),
    )


def token(*others):
    return lax.optimization_barrier((jnp.zeros(TOKEN, wide), *others))[0]


def halves_body(own_ref, came_ref, *out_refs):
    total = own_ref[...].astype(wide) + came_ref[...].astype(wide)
    rows = out_refs[0].shape[0]
    for k, out_ref in enumerate(out_refs):
        out_ref[...] = total[k * rows : (k + 1) * rows, :].astype(low)


def add_halves(own, came, parts, order):
    rows, columns = own.shape
    block = max(b for b in (128, 256, 512, 640) if columns % b == 0)
    spec = pl.BlockSpec((rows, block), lambda j: (0, j))
    out = pl.BlockSpec((rows // parts, block), lambda j: (0, j))
    return call(
        halves_body,
        (columns // block,),
        [spec, spec],
        [out] * parts,
        [jax.ShapeDtypeStruct((rows // parts, columns), low)] * parts,
    )(own, came, order)


def parts_body(count, *refs):
    part_refs, out_refs = refs[:count], refs[count:]
    total = functools.reduce(jnp.add, [ref[...].astype(wide) for ref in part_refs])
    rows = out_refs[0].shape[0]
    for k, out_ref in enumerate(out_refs):
        out_ref[...] = total[k * rows : (k + 1) * rows, :].astype(out_ref.dtype)


def add_parts(parts, cuts, order):
    rows, columns = parts[0].shape
    block = max(b for b in (128, 256, 512, 640) if columns % b == 0)
    spec = pl.BlockSpec((rows, block), lambda j: (0, j))
    out = pl.BlockSpec((rows // cuts, block), lambda j: (0, j))
    shape = (rows // cuts, columns)
    return call(
        functools.partial(parts_body, len(parts)),
        (columns // block,),
        [spec] * len(parts),
        [out] * cuts,
        [jax.ShapeDtypeStruct(shape, wide)] + [jax.ShapeDtypeStruct(shape, low)] * (cuts - 1),
    )(*parts, order)


class OwnerSum:
    def __init__(self, own, other, owners, contexts):
        self.own = own
        self.came = swap(other, "dp", 1)
        self.owners, self.contexts = owners, contexts

    def spread_experts(self, *others):
        if self.own.shape[0] // self.owners // self.contexts % 16 == 0:
            both = add_halves(self.own, self.came, self.owners, token(*others))
        else:
            came = after(self.came, *others)
            total = (self.own.astype(wide) + came.astype(wide)).astype(low)
            both = list(total.reshape(self.owners, -1, total.shape[1]))
        self.parts = [both[0]] + [swap(both[k], "expert", k) for k in range(1, len(both))]
        return both

    def spread_contexts(self, *others):
        if self.parts[0].shape[0] // self.contexts % 16 == 0:
            total = add_parts(self.parts, self.contexts, token(*others))
        else:
            parts = all_after(self.parts, *others)
            total = functools.reduce(jnp.add, [part.astype(wide) for part in parts])
            total = total.reshape(self.contexts, -1, total.shape[1])
            total = [total[0]] + [part.astype(low) for part in total[1:]]
        self.parts = [total[0]] + [swap(part, "context", k) for k, part in enumerate(total) if k]
        return total[1:]


def turn(vals, cosine, sine):
    return vals * cosine + pltpu.roll(vals, LANES // 2, 1) * sine


def project_body(count, rows_ref, scale_ref, cos_ref, sin_ref, *refs):
    weight_refs, (query_ref, kv_ref, weight_ref) = refs[:count], refs[count:]
    step = pl.program_id(0)
    depth = weight_refs[0].shape[0]
    for k in range(count):
        weight_ref[k * depth : (k + 1) * depth, :] = weight_refs[k][...]
    total = dot_nn(rows_ref[...], weight_ref[...]) * scale_ref[...]
    block = total.shape[1]
    query_steps = QUERY_WIDTH // block
    cosine, sine = cos_ref[...], sin_ref[...]
    groups = [total[:, i * LANES : (i + 1) * LANES] for i in range(block // LANES)]

    @pl.when(step < query_steps)
    def _():
        for i, group in enumerate(groups):
            turned = turn(group, cosine, sine) * HEAD_DIM**-0.5
            query_ref[:, i * LANES : (i + 1) * LANES] = turned.astype(low)

    @pl.when(step >= query_steps)
    def _():
        for i, group in enumerate(groups):
            kept = turn(group, cosine, sine) if i % 2 == 0 else group
            kv_ref[:, i * LANES : (i + 1) * LANES] = kept.astype(low)


def project(rows, scale, cosine, sine, weights, order):
    tokens, width = rows.shape
    columns = QUERY_WIDTH + 2 * KV_WIDTH
    block = 512
    query_steps = QUERY_WIDTH // block
    depth = weights[0].shape[0]
    whole = lambda shape: pl.BlockSpec(shape, lambda j: (0, 0))
    return call(
        functools.partial(project_body, len(weights)),
        (columns // block,),
        [whole((tokens, width)), whole((tokens, 1)), whole((tokens, LANES)), whole((tokens, LANES))]
        + [pl.BlockSpec((depth, block), lambda j: (0, j))] * len(weights),
        [
            pl.BlockSpec((tokens, block), lambda j: (0, jnp.minimum(j, query_steps - 1))),
            pl.BlockSpec((tokens, block), lambda j: (0, jnp.maximum(j - query_steps, 0))),
        ],
        [
            jax.ShapeDtypeStruct((tokens, QUERY_WIDTH), low),
            jax.ShapeDtypeStruct((tokens, 2 * KV_WIDTH), low),
        ],
        scratch=[pltpu.VMEM((width, block), low)],
    )(rows, scale, cosine, sine, *weights, order)


def lane_of(shape, axis, which):
    place = lax.broadcasted_iota(jnp.int32, shape, axis)
    return ((place // (HEAD_DIM // 2)) % 2) == which


def stack_heads(block, which):
    keep = lane_of((block.shape[0], LANES), 1, which)
    return jnp.concatenate(
        [
            jnp.where(keep, block[:, g * LANES : (g + 1) * LANES], jnp.zeros((), block.dtype))
            for g in range(GROUPS)
        ],
        axis=0,
    )


def allowed_pairs(key_pos, query_pos):
    seen = key_pos <= query_pos
    return jnp.concatenate([seen] * GROUPS, axis=1)


def turned_block(block):
    return block.astype(wide).T.astype(low)


def attend_body(count, query_ref, key_pos_ref, query_pos_ref, *refs):
    kv_refs, (out_ref, out_low_ref, log_ref) = refs[:count], refs[count:]
    tokens = query_ref.shape[0]
    seen = allowed_pairs(key_pos_ref[...], query_pos_ref[...])
    keys = jnp.concatenate([ref[:, :LANES] for ref in kv_refs], axis=0)
    values = jnp.concatenate([turned_block(ref[:, LANES:]) for ref in kv_refs], axis=1)
    outs = []
    for which in range(2):
        query = stack_heads(query_ref[...], which)
        scores = jnp.where(seen, dot_nt(keys, query), masked_score)
        peak = jnp.max(scores, axis=0, keepdims=True)
        weight = jnp.exp(scores - peak)
        total = jnp.sum(weight, axis=0, keepdims=True)
        outs.append(dot_nn(values, weight.astype(low)) / total)
        log_ref[0, which : which + 1, :] = peak + jnp.log(total)
    first = lane_of(outs[0].shape, 0, 0)
    both = jnp.where(first, outs[0], outs[1]).T
    for g in range(GROUPS):
        piece = both[g * tokens : (g + 1) * tokens, :]
        out_ref[:, g * LANES : (g + 1) * LANES] = piece
        out_low_ref[:, g * LANES : (g + 1) * LANES] = piece.astype(low)


def attend(query, key_pos, query_pos, kv_parts, order):
    tokens = query.shape[0]
    count = len(kv_parts)
    seq_len = tokens * count
    pairs = pl.BlockSpec((tokens, PAIR_WIDTH), lambda p: (0, p))
    return call(
        functools.partial(attend_body, count),
        (PAIRS,),
        [
            pairs,
            pl.BlockSpec((seq_len, 1), lambda p: (0, 0)),
            pl.BlockSpec((1, tokens), lambda p: (0, 0)),
        ]
        + [pl.BlockSpec((tokens, 2 * LANES), lambda p: (0, p))] * count,
        [pairs, pairs, pl.BlockSpec((1, 2, GROUPS * tokens), lambda p: (p, 0, 0))],
        [
            jax.ShapeDtypeStruct((tokens, QUERY_WIDTH), wide),
            jax.ShapeDtypeStruct((tokens, QUERY_WIDTH), low),
            jax.ShapeDtypeStruct((PAIRS, 2, GROUPS * tokens), wide),
        ],
    )(query, key_pos, query_pos, *kv_parts, order)


def attend_back_body(count, own_ref, query_ref, grad_ref, out_ref, log_ref, key_pos_ref, query_pos_ref,
                     scale_ref, cos_ref, sin_ref, *refs):
    kv_refs, (grad_query_ref, grad_kv_ref) = refs[:count], refs[count:]
    tokens = query_ref.shape[0]
    grads = grad_ref[...]
    product = jnp.concatenate(
        [
            (grads[:, g * LANES : (g + 1) * LANES].astype(wide)
             * out_ref[:, g * LANES : (g + 1) * LANES]).T
            for g in range(GROUPS)
        ],
        axis=1,
    )
    first = lane_of(product.shape, 0, 0)
    delta = [
        jnp.sum(jnp.where(first, product, 0.0), axis=0, keepdims=True),
        jnp.sum(jnp.where(first, 0.0, product), axis=0, keepdims=True),
    ]
    seen = allowed_pairs(key_pos_ref[...], query_pos_ref[...])
    keys = jnp.concatenate([ref[:, :LANES] for ref in kv_refs], axis=0)
    values = jnp.concatenate([ref[:, LANES:] for ref in kv_refs], axis=0)
    keys_turned = jnp.concatenate([turned_block(ref[:, :LANES]) for ref in kv_refs], axis=1)
    grad_key, grad_value, grad_query = None, None, []
    for which in range(2):
        query = stack_heads(query_ref[...], which)
        head = stack_heads(grads, which)
        scores = jnp.where(seen, dot_nt(keys, query), masked_score)
        probs = jnp.exp(scores - log_ref[0, which : which + 1, :])
        grad_probs = dot_nt(values, head)
        grad_scores = (probs * (grad_probs - delta[which])).astype(low)
        part_value = dot_nn(probs.astype(low), head)
        part_key = dot_nn(grad_scores, query)
        grad_query.append(dot_nn(keys_turned, grad_scores))
        grad_value = part_value if grad_value is None else grad_value + part_value
        grad_key = part_key if grad_key is None else grad_key + part_key
    scale, cosine, sine = scale_ref[...], cos_ref[...], sin_ref[...]
    for k in range(count):
        rows = slice(k * tokens, (k + 1) * tokens)
        grad_kv_ref[own_ref[0] ^ k, :, :LANES] = grad_key[rows, :].astype(low)
        grad_kv_ref[own_ref[0] ^ k, :, LANES:] = grad_value[rows, :].astype(low)
    first = lane_of(grad_query[0].shape, 0, 0)
    both = (jnp.where(first, grad_query[0], grad_query[1]) * HEAD_DIM**-0.5).T
    for g in range(GROUPS):
        piece = both[g * tokens : (g + 1) * tokens, :]
        back = turn(piece, cosine, -sine) * scale
        grad_query_ref[:, g * LANES : (g + 1) * LANES] = back.astype(low)


def attend_back(
    own, query, grads, out, logs, key_pos, query_pos, scale, cosine, sine, kv_parts, order
):
    tokens = query.shape[0]
    count = len(kv_parts)
    seq_len = tokens * count
    pairs = pl.BlockSpec((tokens, PAIR_WIDTH), lambda p: (0, p))
    whole = lambda shape: pl.BlockSpec(shape, lambda p: (0, 0))
    part = pl.BlockSpec((tokens, 2 * LANES), lambda p: (0, p))
    return call(
        functools.partial(attend_back_body, count),
        (PAIRS,),
        [
            SCALAR,
            pairs,
            pairs,
            pairs,
            pl.BlockSpec((1, 2, GROUPS * tokens), lambda p: (p, 0, 0)),
            whole((seq_len, 1)),
            whole((1, tokens)),
            whole((tokens, 1)),
            whole((tokens, LANES)),
            whole((tokens, LANES)),
        ]
        + [part] * count,
        [pairs, pl.BlockSpec((count, tokens, 2 * LANES), lambda p: (0, 0, p))],
        [
            jax.ShapeDtypeStruct((tokens, QUERY_WIDTH), low),
            jax.ShapeDtypeStruct((count, tokens, 2 * KV_WIDTH), low),
        ],
    )(own, query, grads, out, logs, key_pos, query_pos, scale, cosine, sine, *kv_parts, order)


def hidden_body(count, first, own_ref, grads_ref, gate_ref, weight_ref, *refs):
    part_refs, (hidden_ref, back_ref, rows_ref) = refs[:count], refs[count:]
    expert, place = pl.program_id(0), pl.program_id(1)
    block = grads_ref.shape[0]
    tokens = part_refs[0].shape[0]

    @pl.when((expert == 0) & (place == 0))
    def _():
        for k, part_ref in enumerate(part_refs):
            start = pl.multiple_of((own_ref[0] ^ k) * tokens, tokens)
            rows_ref[pl.ds(start, tokens), :] = part_ref[...]

    rows = rows_ref[pl.ds(pl.multiple_of(place * block, block), block), :]
    grads = grads_ref[...]
    lane = lax.broadcasted_iota(jnp.int32, gate_ref.shape, 1)
    weight = jnp.sum(
        jnp.where(lane == expert + first, gate_ref[...], 0.0), axis=1, keepdims=True
    )
    step = 256
    for h in range(0, FF, step):
        gate = dot_nn(rows, weight_ref[0, :, h : h + step])
        up = dot_nn(rows, weight_ref[0, :, FF + h : FF + h + step])
        grad_hidden = dot_nn(grads, weight_ref[0, :, 2 * FF + h : 2 * FF + h + step]) * weight
        sigmoid = 1.0 / (1.0 + jnp.exp(-gate))
        active = gate * sigmoid
        hidden_ref[0, :, h : h + step] = (active * up * weight).astype(low)
        slope = sigmoid + active * (1.0 - sigmoid)
        back_ref[0, :, h : h + step] = (grad_hidden * up * slope).astype(low)
        back_ref[0, :, FF + h : FF + h + step] = (grad_hidden * active).astype(low)


def expert_hidden(own, parts, grads, gates, first, weights, order):
    tokens, width = grads.shape
    experts = weights.shape[0]
    block = min(tokens, 1024)
    part_rows = parts[0].shape[0]
    return call(
        functools.partial(hidden_body, len(parts), first),
        (experts, tokens // block),
        [
            SCALAR,
            pl.BlockSpec((block, width), lambda e, t: (t, 0)),
            pl.BlockSpec((block, gates.shape[1]), lambda e, t: (t, 0)),
            pl.BlockSpec((1, width, 3 * FF), lambda e, t: (e, 0, 0)),
        ]
        + [
            pl.BlockSpec((part_rows, width), lambda e, t: (0, 0), pipeline_mode=pl.Buffered(1))
        ]
        * len(parts),
        [
            pl.BlockSpec((1, block, FF), lambda e, t: (e, t, 0)),
            pl.BlockSpec((1, block, 2 * FF), lambda e, t: (e, t, 0)),
        ],
        [
            jax.ShapeDtypeStruct((experts, tokens, FF), low),
            jax.ShapeDtypeStruct((experts, tokens, 2 * FF), low),
        ],
        scratch=[pltpu.VMEM((tokens, width), low)],
    )(own, grads, gates, weights, *parts, order)


def turn_body(count, own_ref, *refs):
    part_refs, out_ref = refs[:count], refs[count]
    tokens = part_refs[0].shape[0]
    for k, part_ref in enumerate(part_refs):
        start = pl.multiple_of((own_ref[0] ^ k) * tokens, tokens)
        out_ref[:, pl.ds(start, tokens)] = turned_block(part_ref[...])


def turn_rows(own, parts, order):
    count = len(parts)
    if count == 1:
        count = parts[0].shape[0] // 256
    width = parts[0].shape[1]
    tokens = parts[0].shape[0] if len(parts) > 1 else 256
    specs = [
        pl.BlockSpec((tokens, width), (lambda i, k=k: (k, 0)) if len(parts) == 1 else (lambda i: (0, 0)))
        for k in range(count)
    ]
    return call(
        functools.partial(turn_body, count),
        (1,),
        [SCALAR, *specs],
        pl.BlockSpec((width, count * tokens), lambda i: (0, 0)),
        jax.ShapeDtypeStruct((width, count * tokens), low),
    )(own, *(parts * count if len(parts) == 1 else parts), order)


def weight_grad_body(sizes, rows_ref, grads_ref, *refs):
    count = len(sizes)
    back_refs, hidden_refs, out_ref = refs[:count], refs[count : 2 * count], refs[2 * count]
    step = pl.program_id(0)
    start = 0
    for back_ref, hidden_ref, size in zip(back_refs, hidden_refs, sizes):

        @pl.when((step >= start) & (step < start + size))
        def _():
            out_ref[0, :, : 2 * FF] = dot_nn(rows_ref[...], back_ref[0]).astype(low)
            out_ref[0, :, 2 * FF :] = dot_nn(grads_ref[...], hidden_ref[0]).astype(low)

        start += size


def expert_weight_grads(rows_turned, grads_turned, parts, order):
    width, tokens = rows_turned.shape
    sizes = [last - first for _, _, first, last in parts]
    firsts = [first for _, _, first, _ in parts]
    starts = [sum(sizes[:i]) for i in range(len(sizes))]
    block = width // 2
    place = lambda e, first, start, size: first + jnp.clip(e - start, 0, size - 1)

    def specs(depth):
        return [
            pl.BlockSpec((1, tokens, depth), lambda e, m, f=f, s=s, n=n: (place(e, f, s, n), 0, 0))
            for f, s, n in zip(firsts, starts, sizes)
        ]

    return call(
        functools.partial(weight_grad_body, sizes),
        (sum(sizes), width // block),
        [
            pl.BlockSpec((block, tokens), lambda e, m: (m, 0)),
            pl.BlockSpec((block, tokens), lambda e, m: (m, 0)),
            *specs(2 * FF),
            *specs(FF),
        ],
        pl.BlockSpec((1, block, 3 * FF), lambda e, m: (e, m, 0)),
        jax.ShapeDtypeStruct((sum(sizes), width, 3 * FF), low),
    )(
        rows_turned,
        grads_turned,
        *[back for _, back, _, _ in parts],
        *[hidden for hidden, _, _, _ in parts],
        order,
    )


def combine_body(sizes, own_ref, *refs):
    count = len(sizes)
    part_refs, weight_refs = refs[:count], refs[count : 2 * count]
    out_refs, total_ref = refs[2 * count : -1], refs[-1]
    step = pl.program_id(0)

    @pl.when(step == 0)
    def _():
        total_ref[...] = jnp.zeros_like(total_ref)

    start = 0
    for part_ref, weight_ref, size in zip(part_refs, weight_refs, sizes):

        @pl.when((step >= start) & (step < start + size))
        def _():
            total_ref[...] += dot_nt(part_ref[0], weight_ref[0])

        start += size

    @pl.when(step == start - 1)
    def _():
        tokens = out_refs[0].shape[0]
        for k, out_ref in enumerate(out_refs):
            place = pl.multiple_of((own_ref[0] ^ k) * tokens, tokens)
            out_ref[...] = total_ref[pl.ds(place, tokens), :].astype(low)


def combine(own, owners, parts, weights, column, order):
    tokens, depth = parts[0].shape[1:]
    width = weights[0].shape[1]
    sizes = [w.shape[0] for w in weights]
    starts = [sum(sizes[:i]) for i in range(len(sizes))]
    place = lambda e, start, size: jnp.clip(e - start, 0, size - 1)
    part_specs = [
        pl.BlockSpec((1, tokens, depth), lambda e, s=s, n=n: (place(e, s, n), 0, 0))
        for s, n in zip(starts, sizes)
    ]
    weight_specs = [
        pl.BlockSpec((1, width, depth), lambda e, s=s, n=n: (place(e, s, n), 0, column))
        for s, n in zip(starts, sizes)
    ]
    return call(
        functools.partial(combine_body, sizes),
        (sum(sizes),),
        [SCALAR] + part_specs + weight_specs,
        [pl.BlockSpec((tokens // owners, width), lambda e: (0, 0))] * owners,
        [jax.ShapeDtypeStruct((tokens // owners, width), low)] * owners,
        scratch=[pltpu.VMEM((tokens, width), wide)],
    )(own, *parts, *weights, order)


def norm_back_body(count, scale_ref, gain_ref, middle_ref, cotangent_ref, weight_ref, *refs):
    part_refs = refs[:count]
    middle_grad_ref, turned_ref, attended_ref, gain_grad_ref, proj_ref = refs[count:]

    @pl.when(pl.program_id(0) == 0)
    def _():
        grad = functools.reduce(jnp.add, [ref[...].astype(wide) for ref in part_refs])
        scale = scale_ref[...]
        unit = middle_ref[...] * scale
        gain = jnp.sum((grad * unit).T, axis=1, keepdims=True)
        gain_grad_ref[...] = jnp.broadcast_to(gain, gain_grad_ref.shape).astype(low)
        grad = grad * gain_ref[...]
        mean = jnp.mean(grad * unit, axis=1, keepdims=True)
        grad = cotangent_ref[...].astype(wide) + scale * (grad - unit * mean)
        middle_grad_ref[...] = grad
        proj_ref[...] = grad.astype(low)
        turned_ref[...] = grad.T.astype(low)

    attended_ref[...] = dot_nn(proj_ref[...], weight_ref[...]).astype(low)


def norm_back_two(parts, middle, scale, gain, cotangent, output_pack, order):
    tokens, width = middle.shape
    block = 512
    whole = lambda shape: pl.BlockSpec(shape, lambda j: (0, 0))
    return call(
        functools.partial(norm_back_body, len(parts)),
        (QUERY_WIDTH // block,),
        [
            whole((tokens, 1)),
            whole((1, width)),
            whole((tokens, width)),
            whole((tokens, width)),
            pl.BlockSpec((width, block), lambda j: (0, j)),
        ]
        + [whole((tokens, width))] * len(parts),
        [
            whole((tokens, width)),
            whole((width, tokens)),
            pl.BlockSpec((tokens, block), lambda j: (0, j)),
            whole((width, LANES)),
        ],
        [
            jax.ShapeDtypeStruct((tokens, width), wide),
            jax.ShapeDtypeStruct((width, tokens), low),
            jax.ShapeDtypeStruct((tokens, QUERY_WIDTH), low),
            jax.ShapeDtypeStruct((width, LANES), low),
        ],
        scratch=[pltpu.VMEM((tokens, width), low)],
    )(scale, gain, middle, cotangent, output_pack, *parts, order)


def outer_body(rows, first, place_ref, input_ref, proj_ref, gain_ref, query_ref, attended_ref,
               out_ref, picked_ref):
    out_ref[:, :QUERY_WIDTH] = dot_nn(input_ref[...], query_ref[...]).astype(low)
    if rows:
        for i in range(out_ref.shape[0] // rows):
            start = pl.multiple_of(place_ref[first + i] * rows, rows)
            part = slice(i * rows, (i + 1) * rows)
            picked_ref[part, :] = proj_ref[pl.ds(start, rows), :]
            out_ref[part, 2 * QUERY_WIDTH :] = gain_ref[pl.ds(start, rows), :]
    else:
        picked_ref[...] = proj_ref[...]
        out_ref[:, 2 * QUERY_WIDTH :] = gain_ref[...]
    out_ref[:, QUERY_WIDTH : 2 * QUERY_WIDTH] = dot_nn(picked_ref[...], attended_ref[...]).astype(low)


def outer_grads(half, cores, place, input_turned, proj_turned, gain_turned, grad_query, attended, order):
    width, tokens = input_turned.shape
    rows = width // cores
    slice_rows = width // place.shape[0]
    part = lambda columns: pl.BlockSpec((rows, columns), lambda i: (half, 0))
    inside = slice_rows % 16 == 0
    every = lambda columns: pl.BlockSpec((width, columns), lambda i: (0, 0))
    if not inside:
        pick = lambda array: jnp.take(
            array.reshape(place.shape[0], slice_rows, -1), place, axis=0, mode="clip"
        ).reshape(array.shape)
        proj_turned, gain_turned = pick(proj_turned), pick(gain_turned)
        every = part
    whole = pl.BlockSpec((tokens, QUERY_WIDTH), lambda i: (0, 0))
    columns = 2 * QUERY_WIDTH + LANES
    return call(
        functools.partial(outer_body, slice_rows if inside else 0, half * (place.shape[0] // cores)),
        (1,),
        [SCALAR, part(tokens), every(tokens), every(LANES), whole, whole],
        pl.BlockSpec((rows, columns), lambda i: (0, 0)),
        jax.ShapeDtypeStruct((rows, columns), low),
        scratch=[pltpu.VMEM((rows, tokens), low)],
    )(place, input_turned, proj_turned, gain_turned, grad_query, attended, order)


def kv_body(parts_ref, scale_ref, cos_ref, sin_ref, input_ref, grad_ref, *out_refs):
    total = jnp.sum(parts_ref[...].astype(wide), axis=0)
    cosine, sine, scale = cos_ref[...], sin_ref[...], scale_ref[...]
    for i in range(2 * PAIRS):
        group = total[:, i * LANES : (i + 1) * LANES]
        group = turn(group, cosine, -sine) if i % 2 == 0 else group
        grad_ref[:, i * LANES : (i + 1) * LANES] = (group * scale).astype(low)
    grads = grad_ref[...]
    rows = out_refs[0].shape[0]
    for k, out_ref in enumerate(out_refs):
        out_ref[...] = dot_nn(input_ref[k * rows : (k + 1) * rows, :], grads).astype(low)


def kv_grads(cores, parts, scale, cosine, sine, input_turned, order):
    tokens, columns = parts.shape[1:]
    width = input_turned.shape[0]
    shapes = [(tokens, columns)] + [(width // cores, columns)] * cores
    whole = lambda shape: pl.BlockSpec(shape, lambda i: (0,) * len(shape))
    return call(
        kv_body,
        (1,),
        [
            whole(parts.shape),
            whole((tokens, 1)),
            whole((tokens, LANES)),
            whole((tokens, LANES)),
            whole((width, tokens)),
        ],
        [whole(shape) for shape in shapes],
        [jax.ShapeDtypeStruct(shape, low) for shape in shapes],
    )(parts, scale, cosine, sine, input_turned, order)


def input_body(count, rows, place_ref, query_ref, kv_ref, scale_ref, input_ref, middle_ref, *refs):
    weight_refs, (out_ref, turned_ref) = refs[:count], refs[count:]
    weights = jnp.concatenate([ref[...] for ref in weight_refs], axis=0)
    part = dot_nt(weights[:, :QUERY_WIDTH], query_ref[...])
    part += dot_nt(weights[:, QUERY_WIDTH:], kv_ref[...])
    for i in range(part.shape[0] // rows):
        start = pl.multiple_of(place_ref[i] * rows, rows)
        turned_ref[pl.ds(start, rows), :] = part[i * rows : (i + 1) * rows, :]
    grad = turned_ref[...].T
    unit = input_ref[...].astype(wide) * scale_ref[...]
    mean = jnp.mean(grad * unit, axis=1, keepdims=True)
    out_ref[...] = (middle_ref[...] + grad - unit * mean).astype(low)


def input_grads(place, grad_query, grad_kv, scale, rows, grad_middle, weights, order):
    tokens, width = rows.shape
    whole = lambda array: pl.BlockSpec(array.shape, lambda i: (0, 0))
    operands = [grad_query, grad_kv, scale, rows, grad_middle, *weights]
    return call(
        functools.partial(input_body, len(weights), width // place.shape[0]),
        (1,),
        [SCALAR] + [whole(operand) for operand in operands],
        pl.BlockSpec((tokens, width), lambda i: (0, 0)),
        jax.ShapeDtypeStruct((tokens, width), low),
        scratch=[pltpu.VMEM((width, tokens), wide)],
    )(place, *operands, order)


def adam_body(held, grad_ref, *refs):
    expand, contract, refs = refs[:3], refs[3:6], refs[6 + held :]
    grads = grad_ref[0].astype(wide)
    split = expand[0].shape[2]
    for arrays, grad, rate, out_refs in (
        (expand, grads[:, :split], rate_expand, refs[:3]),
        (contract, grads[:, split:], rate_contract, refs[3:]),
    ):
        results = adamw(*[array[0] for array in arrays], grad, rate, decay_rate)
        for out_ref, result in zip(out_refs, results):
            out_ref[0] = result


def adam_experts(first, grads, arrays, held, order):
    count = grads.shape[0]
    held = held or []
    block = lambda array: pl.BlockSpec((1, *array.shape[1:]), lambda e: (first + e, 0, 0))
    return call(
        functools.partial(adam_body, len(held)),
        (count,),
        [pl.BlockSpec((1, *grads.shape[1:]), lambda e: (e, 0, 0))]
        + [block(array) for array in arrays]
        + [pl.BlockSpec(memory_space=pl.ANY)] * len(held),
        [block(array) for array in arrays],
        [jax.ShapeDtypeStruct(array.shape, wide) for array in arrays],
        aliases={1 + len(arrays) + i: i for i in range(len(held))},
    )(grads, *arrays, *held, order)


def adam_joined_body(count, query_mat_ref, key_mat_ref, gain_ref, *refs):
    grads, kv = [
        functools.reduce(jnp.add, [ref[...].astype(wide) for ref in part])
        for part in (refs[:count], refs[count : 2 * count])
    ]
    refs = refs[2 * count :]
    joined, output, gains, outs = refs[:3], refs[3:6], refs[6:9], refs[9:]
    back = lambda grad, mat: lax.dot_general(
        grad, mat, (((1,), (1,)), ((), ())), precision=lax.Precision.HIGHEST, preferred_element_type=wide
    )
    query_mat, key_mat = query_mat_ref[...], key_mat_ref[...]
    pairs = lambda start: [
        back(grads[:, start + p * PAIR_WIDTH : start + (p + 1) * PAIR_WIDTH], query_mat)
        for p in range(PAIRS)
    ]
    keys = [back(kv[:, 2 * p * LANES : (2 * p + 1) * LANES], key_mat) for p in range(PAIRS)]
    values = [back(kv[:, (2 * p + 1) * LANES : (2 * p + 2) * LANES], key_mat) for p in range(PAIRS)]
    unit_grad = jnp.concatenate([*pairs(0), *keys, *values], axis=1)
    low_weight = joined[0][...].astype(low).astype(wide)
    gain_one = jnp.sum(low_weight * unit_grad, axis=1, keepdims=True)
    gain_two = grads[:, 2 * QUERY_WIDTH : 2 * QUERY_WIDTH + 1]
    output_grad = jnp.concatenate(pairs(QUERY_WIDTH), axis=1)
    joined_grad = gain_ref[...] * unit_grad
    gains_grad = jnp.concatenate([gain_one, gain_two], axis=1)
    for arrays, grad, rate, decay, out_refs in (
        (joined, joined_grad, rate_joined, decay_rate, outs[:3]),
        (output, output_grad, rate_output, decay_rate, outs[3:6]),
        (gains, gains_grad, rate_gains, 0.0, outs[6:]),
    ):
        results = adamw(*[array[...] for array in arrays], grad, rate, decay)
        for out_ref, result in zip(out_refs, results):
            out_ref[...] = result


def adam_joined(gain, query_parts, kv_parts, arrays, order):
    query_mat, key_mat = order_matrix(GROUPS).astype(wide), order_matrix(1).astype(wide)
    operands = [query_mat, key_mat, gain, *query_parts, *kv_parts, *arrays]
    whole = lambda array: pl.BlockSpec(array.shape, lambda i: (0, 0))
    return call(
        functools.partial(adam_joined_body, len(query_parts)),
        (1,),
        [whole(operand) for operand in operands],
        [whole(array) for array in arrays],
        [jax.ShapeDtypeStruct(array.shape, wide) for array in arrays],
    )(*operands, order)


def body(
    layer_input,
    cotangent,
    block_order,
    routes,
    route_gates,
    joined_weight,
    joined_first,
    joined_second,
    output_weight,
    output_first,
    output_second,
    norm_gains,
    gains_first,
    gains_second,
    expand_weight,
    expand_first,
    expand_second,
    contract_weight,
    contract_first,
    contract_second,
):
    experts_dev = expand_weight.shape[0]
    owners = lax.axis_size("expert")
    contexts = lax.axis_size("context")
    cores = lax.axis_size("dp")
    experts = experts_dev * owners
    tokens = layer_input.shape[1]
    width = layer_input.shape[2]
    half_block = tokens // 2
    slice_rows = joined_weight.shape[0]
    own_expert = lax.axis_index("expert")
    own_context = lax.axis_index("context")
    own_core = lax.axis_index("dp")

    gain_rows = norm_gains.astype(low).astype(wide).T
    joined_low = joined_weight.astype(low)
    joined_shard = reorder_columns((gain_rows[:, :1] * joined_low.astype(wide)).astype(low)).astype(low)
    query_mat = order_matrix(GROUPS)
    output_shard = jnp.einsum(
        "pod,on->dpn",
        output_weight.astype(low).reshape(PAIRS, PAIR_WIDTH, slice_rows),
        query_mat,
        preferred_element_type=wide,
    ).reshape(slice_rows, QUERY_WIDTH).astype(low)
    gain_column = jnp.broadcast_to(gain_rows[:, 1:].astype(low), (slice_rows, LANES))
    columns = joined_shard.shape[1]
    shard = jnp.concatenate([joined_shard, output_shard, gain_column], axis=1)

    bounds = [0, experts_dev // 2, experts_dev]
    chunks = list(zip(bounds[:-1], bounds[1:]))
    expert_low = [
        jnp.concatenate(
            [
                expand_weight[a:b].astype(low),
                jnp.swapaxes(contract_weight[a:b].astype(low), 1, 2),
            ],
            axis=2,
        )
        for a, b in chunks
    ]
    line, *expert_low = lax.optimization_barrier(
        (jnp.concatenate(spread(shard, "context"), axis=0), *expert_low)
    )
    joined_mine = spread(line[:, :columns], "expert")
    gather_expert = lambda part: lax.all_gather(part, ("context", "dp"), axis=1, tiled=True)
    expert_full = [gather_expert(expert_low[0])]

    ar = lambda n: jnp.arange(n, dtype=jnp.int32)
    to_relative = (
        ((own_expert ^ ar(owners))[None, :, None] * contexts + (own_context ^ ar(contexts))[None, None, :])
        * cores
        + (own_core ^ ar(cores))[:, None, None]
    ).reshape(-1)
    to_absolute = (
        (own_core ^ ar(cores))[None, None, :] * owners + (own_expert ^ ar(owners))[:, None, None]
    ) * contexts + (own_context ^ ar(contexts))[None, :, None]
    to_absolute = to_absolute.reshape(-1)
    slices = owners * contexts * cores

    def pick_rows(rows, index):
        return jnp.take(
            rows.reshape(slices, slice_rows, -1), index, axis=0, mode="clip", unique_indices=True
        ).reshape(rows.shape)

    hits = routes[0][:, :, None] == ar(experts)[None, None, :]
    gate_table = jnp.sum(jnp.where(hits, route_gates[0][:, :, None], 0.0), axis=1)
    gate_table = gate_table.reshape(tokens, owners, experts_dev)
    gate_sent = [
        lax.dynamic_index_in_dim(gate_table, own_expert ^ k, axis=1, keepdims=False)
        for k in range(owners)
    ]
    own = own_expert.reshape(1)
    zero = jnp.zeros((1,), jnp.int32)

    order = block_order[0]
    offsets = ar(half_block)

    def places_of(index):
        mine = lax.dynamic_slice_in_dim(order, 2 * index, 2)
        return (mine[:, None] * half_block + offsets[None, :]).reshape(-1)

    query_pos = places_of(own_context)
    key_pos = jnp.concatenate([places_of(own_context ^ k) for k in range(contexts)])
    half = HEAD_DIM // 2
    freq = jnp.exp(ar(half).astype(wide) * (2.0 / HEAD_DIM) * -math.log(10000.0))
    angle = query_pos.astype(wide)[:, None] * freq[None, :]
    cosine = jnp.tile(jnp.cos(angle), (1, 4))
    sine = jnp.sin(angle)
    sine = jnp.concatenate([-sine, -sine, sine, sine], axis=1)

    low_input = layer_input[0]
    resid = low_input.astype(wide)
    scale_one = lax.rsqrt(jnp.mean(resid * resid, axis=-1, keepdims=True) + norm_eps)
    unit_one = resid * scale_one
    input_turned = pick_rows(low_input.T, to_relative)
    input_relative = input_turned.T
    gate_sent = all_after(gate_sent, line)
    gate_parts = [gate_sent[0]] + [swap(gate_sent[k], "expert", k) for k in range(1, owners)]
    joined_mine = [joined_mine[0]] + all_after(
        joined_mine[1:], cosine, sine, scale_one, input_relative, *gate_sent
    )
    joined_parts = joined_mine + [swap(part, "dp", 1) for part in joined_mine]
    query, kv = project(input_relative, scale_one, cosine, sine, joined_parts, token())
    kv_parts = spread(kv, "context")
    output_mine = share(after(line[:, columns:], kv), "expert")
    gates = in_order(all_after(gate_parts, kv), own_expert)
    output_parts = [output_mine, swap(output_mine, "dp", 1)]
    out_grads = share(after(cotangent[0], output_mine), "expert").reshape(-1, width)
    output_place = (
        (own_core ^ ar(cores))[None, None, :] * owners + ar(owners)[:, None, None]
    ) * contexts + (own_context ^ ar(contexts))[None, :, None]
    output_pack = pick_rows(
        jnp.concatenate([part.reshape(-1, output_mine.shape[-1]) for part in output_parts], axis=0),
        output_place.reshape(-1),
    )
    output_turned = output_pack[:, :QUERY_WIDTH]
    gain_two = output_pack[:, QUERY_WIDTH].astype(wide)[None, :]
    out_grads_turned = turn_rows(zero, [out_grads], token(output_pack))
    kv_parts = all_after(kv_parts, output_pack, out_grads_turned, gates)
    kv_parts, later = lax.optimization_barrier((kv_parts, expert_low[1:]))
    expert_full += [gather_expert(part) for part in later]
    attended_wide, attended, logs = attend(
        query, key_pos[:, None], query_pos[None, :], kv_parts, token()
    )
    middle = resid + dot_nt(attended, output_turned)
    scale_two = lax.rsqrt(jnp.mean(middle * middle, axis=-1, keepdims=True) + norm_eps)
    unit_two = middle * scale_two
    normed_two = (unit_two * gain_two).astype(low)

    row_parts = spread(normed_two, "expert")
    def grads_of(hidden, back, *others):
        return expert_weight_grads(
            rows_turned, out_grads_turned, [(hidden, back, 0, back.shape[0])], token(*others)
        )

    def to_owners(grads):
        return lax.psum_scatter(grads, ("context", "dp"), scatter_dimension=1, tiled=True)

    def to_tokens(parts):
        return [parts[0]] + [swap(parts[k], "expert", k) for k in range(1, owners)]

    cut = bounds[1]
    first_unit = expert_hidden(
        own, row_parts, out_grads, gates, 0, expert_full[0], token()
    )
    rows_turned = turn_rows(own, row_parts, token(first_unit[0]))
    first_grads = grads_of(*first_unit)
    second_unit = expert_hidden(
        own, row_parts, out_grads, gates, cut, expert_full[1], token(first_grads)
    )
    backs = [first_unit[1], second_unit[1]]
    grad_sent = combine(own, owners, backs, expert_full, 0, token())
    first_sum = to_owners(first_grads)
    grad_parts = to_tokens(grad_sent)
    second_grads = grads_of(*second_unit, *grad_sent)
    mixture_sent = combine(
        own, owners, [first_unit[0], second_unit[0]], expert_full, 2, token(second_grads)
    )
    mixture_parts = to_tokens(mixture_sent)

    grad_middle, proj_turned, grad_attended, gain_turned = norm_back_two(
        grad_parts, middle, scale_two, gain_two, cotangent[0], output_pack, token(*mixture_sent)
    )
    grad_query, grad_kv = attend_back(
        own_context.reshape(1), query, grad_attended, attended_wide, logs, key_pos[:, None], query_pos[None, :],
        scale_one, cosine, sine, kv_parts, token(grad_attended, first_sum),
    )
    expert_grads = [first_sum, to_owners(after(second_grads, first_sum, grad_attended))]
    grad_kv_parts = trade(grad_kv, "context")

    def outer(half, *others):
        return outer_grads(
            half, cores, to_relative, input_turned, proj_turned, gain_turned, grad_query, attended,
            token(*others),
        )

    mixture = functools.reduce(
        jnp.add, [part.astype(wide) for part in all_after(mixture_parts, grad_query)]
    )
    output = (middle + mixture).astype(low)
    other = outer(1, output)
    query_sum = OwnerSum(outer(0, other), other, owners, contexts)
    latest = query_sum.spread_experts(query_sum.own)
    latest = query_sum.spread_contexts(*latest)
    own_grad_kv, *kv_parts_sent = kv_grads(
        cores, grad_kv_parts, scale_one, cosine, sine, input_turned, token(*latest)
    )
    kv_sum = OwnerSum(*kv_parts_sent, owners, contexts)
    latest = kv_sum.spread_experts(own_grad_kv)
    if slice_rows % 16 == 0:
        grad_input = input_grads(
            to_relative, grad_query, own_grad_kv, scale_one, low_input, grad_middle, joined_parts,
            token(*latest),
        )
    else:
        grad_joined = jnp.concatenate([grad_query, own_grad_kv], axis=1)
        scaled_grad = jnp.concatenate([dot_nt(part, grad_joined) for part in joined_parts], axis=0)
        scaled_grad = pick_rows(scaled_grad, to_absolute).T
        grad_input = (
            grad_middle
            + scaled_grad
            - unit_one * jnp.mean(scaled_grad * unit_one, axis=-1, keepdims=True)
        ).astype(low)

    latest = kv_sum.spread_contexts(grad_input)
    contract_arrays = [contract_weight, contract_first, contract_second]
    arrays = [expand_weight, expand_first, expand_second]
    arrays += [jnp.swapaxes(array, 1, 2) for array in contract_arrays]
    expert_new = adam_experts(0, expert_grads[0], arrays, None, token(*latest))
    expert_new = adam_experts(cut, expert_grads[1], arrays, expert_new, token())
    expand_new = expert_new[:3]
    contract_new = [jnp.swapaxes(array, 1, 2) for array in expert_new[3:]]
    turned = [output_weight, output_first, output_second, norm_gains, gains_first, gains_second]
    joined_new = adam_joined(
        gain_rows[:, :1],
        query_sum.parts,
        kv_sum.parts,
        [joined_weight, joined_first, joined_second] + [array.T for array in turned],
        token(expand_new[0]),
    )
    output_new = [array.T for array in joined_new[3:6]]
    gains_new = [array.T for array in joined_new[6:]]
    joined_new = joined_new[:3]
    return (
        output.reshape(1, tokens, width),
        grad_input.reshape(1, tokens, width),
        *joined_new,
        *output_new,
        *gains_new,
        *expand_new,
        *contract_new,
    )


def solution(mesh):
    rows = P(("expert", "dp"), "context", None)
    joined = P(("expert", "context", "dp"), None)
    column = P(None, ("expert", "context", "dp"))
    expand = P("expert", ("context", "dp"), None)
    contract = P("expert", None, ("context", "dp"))
    placed = (
        (rows, rows, P(("expert", "dp"), None), rows, rows)
        + (joined,) * 3
        + (column,) * 6
        + (expand,) * 3
        + (contract,) * 3
    )
    return jax.shard_map(
        body,
        mesh=mesh,
        in_specs=placed,
        out_specs=(rows, rows) + placed[5:],
        check_vma=False,
    )
```

```python
import functools
import math

import jax
import jax.numpy as jnp
import numpy as np
from jax import lax
from jax.experimental import pallas as pl
from jax.experimental.pallas import tpu as pltpu
from jax.sharding import PartitionSpec as P

HEADS = 24
KV_HEADS = 8
HEAD_DIM = 64
FF = 512
TOP = 8
STEP = 10
GROUPS = HEADS // KV_HEADS
PAIRS = KV_HEADS // 2
QUERY_WIDTH = HEADS * HEAD_DIM
KV_WIDTH = KV_HEADS * HEAD_DIM
PAIR_WIDTH = 2 * GROUPS * HEAD_DIM
LANES = 128
VMEM_BYTES = 60 * 1024 * 1024
TOKEN = (8, 128)
SCALAR = pl.BlockSpec(memory_space=pltpu.SMEM)

norm_eps = 1e-06
beta_one = 0.9
beta_two = 0.95
adam_eps = 1e-08
decay_rate = 0.1
rate_joined = 0.08
rate_output = 0.6
rate_gains = 0.6
rate_expand = 0.08
rate_contract = 0.5
masked_score = -1e30

low = jnp.bfloat16
wide = jnp.float32


def adamw(weight, first, second, grad, rate, decay):
    first_new = beta_one * first + (1.0 - beta_one) * grad
    second_new = beta_two * second + (1.0 - beta_two) * grad * grad
    first_hat = first_new / (1.0 - beta_one**STEP)
    second_hat = second_new / (1.0 - beta_two**STEP)
    weight_new = weight - rate * (first_hat / (jnp.sqrt(second_hat) + adam_eps) + decay * weight)
    return (weight_new, first_new, second_new)


def dot_nn(left, right):
    return lax.dot_general(left, right, (((1,), (0,)), ((), ())), preferred_element_type=wide)


def dot_nt(left, right):
    return lax.dot_general(left, right, (((1,), (1,)), ((), ())), preferred_element_type=wide)


def pair_order(groups):
    half = HEAD_DIM // 2
    old = np.arange(2 * groups * HEAD_DIM).reshape(2, groups, 2, half)
    return old.transpose(1, 2, 0, 3).reshape(-1)


def order_matrix(groups):
    order = pair_order(groups)
    size = order.shape[0]
    return jnp.asarray(np.arange(size)[:, None] == order[None, :], dtype=low)


def reorder_columns(rows, back=False):
    count = rows.shape[0]
    query_mat = order_matrix(GROUPS)
    key_mat = order_matrix(1)
    kv = rows[:, QUERY_WIDTH:]
    if back:
        query_mat = query_mat.T
        key_mat = key_mat.T
        kv = jnp.swapaxes(kv.reshape(count, PAIRS, 2, LANES), 1, 2)
    else:
        kv = jnp.swapaxes(kv.reshape(count, 2, PAIRS, LANES), 1, 2)
    exact = lax.Precision.HIGHEST if rows.dtype == wide else None
    query = jnp.einsum(
        "rpo,on->rpn",
        rows[:, :QUERY_WIDTH].reshape(count, PAIRS, PAIR_WIDTH),
        query_mat.astype(rows.dtype),
        precision=exact,
        preferred_element_type=wide,
    ).reshape(count, QUERY_WIDTH)
    others = jnp.einsum(
        "rpo,on->rpn",
        kv.reshape(count, 2 * PAIRS, LANES),
        key_mat.astype(rows.dtype),
        precision=exact,
        preferred_element_type=wide,
    ).reshape(count, 2 * KV_WIDTH)
    return jnp.concatenate([query, others], axis=1)


def swap(block, axis, step):
    count = lax.axis_size(axis)
    return lax.ppermute(block, axis, [(i, i ^ step) for i in range(count)])


def spread(block, axis):
    return [block] + [swap(block, axis, k) for k in range(1, lax.axis_size(axis))]


def after(value, *others):
    return lax.optimization_barrier((value, *others))[0]


def all_after(values, *others):
    count = len(values)
    return list(lax.optimization_barrier((*values, *others))[:count])


def share(block, axis):
    return trade(jnp.broadcast_to(block[None], (lax.axis_size(axis), *block.shape)), axis)


def trade(blocks, axis):
    return lax.all_to_all(blocks, axis, split_axis=0, concat_axis=0, tiled=True)


def in_order(parts, own):
    rows = parts[0].shape[0]
    joined = jnp.zeros((len(parts) * rows, *parts[0].shape[1:]), parts[0].dtype)
    for k, part in enumerate(parts):
        joined = lax.dynamic_update_slice_in_dim(joined, part, (own ^ k) * rows, 0)
    return joined


def call(body, grid, in_specs, out_specs, out_shape, scratch=(), aliases=None):
    order = pl.BlockSpec(TOKEN, lambda *_: (0, 0))

    def ordered(*refs):
        place = len(in_specs)
        body(*refs[:place], *refs[place + 1 :])

    return pl.pallas_call(
        ordered,
        grid=grid,
        in_specs=[*in_specs, order],
        out_specs=out_specs,
        out_shape=out_shape,
        scratch_shapes=list(scratch),
        input_output_aliases=aliases or {},
        compiler_params=pltpu.CompilerParams(vmem_limit_bytes=VMEM_BYTES),
        cost_estimate=pl.CostEstimate(flops=1, bytes_accessed=1, transcendentals=0),
    )


def token(*others):
    return lax.optimization_barrier((jnp.zeros(TOKEN, wide), *others))[0]


def halves_body(own_ref, came_ref, *out_refs):
    total = own_ref[...].astype(wide) + came_ref[...].astype(wide)
    rows = out_refs[0].shape[0]
    for k, out_ref in enumerate(out_refs):
        out_ref[...] = total[k * rows : (k + 1) * rows, :].astype(low)


def add_halves(own, came, parts, order):
    rows, columns = own.shape
    block = max(b for b in (128, 256, 512, 640) if columns % b == 0)
    spec = pl.BlockSpec((rows, block), lambda j: (0, j))
    out = pl.BlockSpec((rows // parts, block), lambda j: (0, j))
    return call(
        halves_body,
        (columns // block,),
        [spec, spec],
        [out] * parts,
        [jax.ShapeDtypeStruct((rows // parts, columns), low)] * parts,
    )(own, came, order)


def parts_body(count, *refs):
    part_refs, out_refs = refs[:count], refs[count:]
    total = functools.reduce(jnp.add, [ref[...].astype(wide) for ref in part_refs])
    rows = out_refs[0].shape[0]
    for k, out_ref in enumerate(out_refs):
        out_ref[...] = total[k * rows : (k + 1) * rows, :].astype(out_ref.dtype)


def add_parts(parts, cuts, order):
    rows, columns = parts[0].shape
    block = max(b for b in (128, 256, 512, 640) if columns % b == 0)
    spec = pl.BlockSpec((rows, block), lambda j: (0, j))
    out = pl.BlockSpec((rows // cuts, block), lambda j: (0, j))
    shape = (rows // cuts, columns)
    return call(
        functools.partial(parts_body, len(parts)),
        (columns // block,),
        [spec] * len(parts),
        [out] * cuts,
        [jax.ShapeDtypeStruct(shape, wide)] + [jax.ShapeDtypeStruct(shape, low)] * (cuts - 1),
    )(*parts, order)


class OwnerSum:
    def __init__(self, own, other, owners, contexts):
        self.own = own
        self.came = swap(other, "dp", 1)
        self.owners, self.contexts = owners, contexts

    def spread_experts(self, *others):
        if self.own.shape[0] // self.owners // self.contexts % 16 == 0:
            both = add_halves(self.own, self.came, self.owners, token(*others))
        else:
            came = after(self.came, *others)
            total = (self.own.astype(wide) + came.astype(wide)).astype(low)
            both = list(total.reshape(self.owners, -1, total.shape[1]))
        self.parts = [both[0]] + [swap(both[k], "expert", k) for k in range(1, len(both))]
        return both

    def spread_contexts(self, *others):
        if self.parts[0].shape[0] // self.contexts % 16 == 0:
            total = add_parts(self.parts, self.contexts, token(*others))
        else:
            parts = all_after(self.parts, *others)
            total = functools.reduce(jnp.add, [part.astype(wide) for part in parts])
            total = total.reshape(self.contexts, -1, total.shape[1])
            total = [total[0]] + [part.astype(low) for part in total[1:]]
        self.parts = [total[0]] + [swap(part, "context", k) for k, part in enumerate(total) if k]
        return total[1:]


def turn(vals, cosine, sine):
    return vals * cosine + pltpu.roll(vals, LANES // 2, 1) * sine


def project_body(count, rows_ref, scale_ref, cos_ref, sin_ref, *refs):
    weight_refs, (query_ref, kv_ref, weight_ref) = refs[:count], refs[count:]
    step = pl.program_id(0)
    depth = weight_refs[0].shape[0]
    for k in range(count):
        weight_ref[k * depth : (k + 1) * depth, :] = weight_refs[k][...]
    total = dot_nn(rows_ref[...], weight_ref[...]) * scale_ref[...]
    block = total.shape[1]
    query_steps = QUERY_WIDTH // block
    cosine, sine = cos_ref[...], sin_ref[...]
    groups = [total[:, i * LANES : (i + 1) * LANES] for i in range(block // LANES)]

    @pl.when(step < query_steps)
    def _():
        for i, group in enumerate(groups):
            turned = turn(group, cosine, sine) * HEAD_DIM**-0.5
            query_ref[:, i * LANES : (i + 1) * LANES] = turned.astype(low)

    @pl.when(step >= query_steps)
    def _():
        for i, group in enumerate(groups):
            kept = turn(group, cosine, sine) if i % 2 == 0 else group
            kv_ref[:, i * LANES : (i + 1) * LANES] = kept.astype(low)


def project(rows, scale, cosine, sine, weights, order):
    tokens, width = rows.shape
    columns = QUERY_WIDTH + 2 * KV_WIDTH
    block = 512
    query_steps = QUERY_WIDTH // block
    depth = weights[0].shape[0]
    whole = lambda shape: pl.BlockSpec(shape, lambda j: (0, 0))
    return call(
        functools.partial(project_body, len(weights)),
        (columns // block,),
        [whole((tokens, width)), whole((tokens, 1)), whole((tokens, LANES)), whole((tokens, LANES))]
        + [pl.BlockSpec((depth, block), lambda j: (0, j))] * len(weights),
        [
            pl.BlockSpec((tokens, block), lambda j: (0, jnp.minimum(j, query_steps - 1))),
            pl.BlockSpec((tokens, block), lambda j: (0, jnp.maximum(j - query_steps, 0))),
        ],
        [
            jax.ShapeDtypeStruct((tokens, QUERY_WIDTH), low),
            jax.ShapeDtypeStruct((tokens, 2 * KV_WIDTH), low),
        ],
        scratch=[pltpu.VMEM((width, block), low)],
    )(rows, scale, cosine, sine, *weights, order)


def lane_of(shape, axis, which):
    place = lax.broadcasted_iota(jnp.int32, shape, axis)
    return ((place // (HEAD_DIM // 2)) % 2) == which


def stack_heads(block, which):
    keep = lane_of((block.shape[0], LANES), 1, which)
    return jnp.concatenate(
        [
            jnp.where(keep, block[:, g * LANES : (g + 1) * LANES], jnp.zeros((), block.dtype))
            for g in range(GROUPS)
        ],
        axis=0,
    )


def allowed_pairs(key_pos, query_pos):
    seen = key_pos <= query_pos
    return jnp.concatenate([seen] * GROUPS, axis=1)


def turned_block(block):
    return block.astype(wide).T.astype(low)


def attend_body(count, query_ref, key_pos_ref, query_pos_ref, *refs):
    kv_refs, (out_ref, out_low_ref, log_ref) = refs[:count], refs[count:]
    tokens = query_ref.shape[0]
    seen = allowed_pairs(key_pos_ref[...], query_pos_ref[...])
    keys = jnp.concatenate([ref[:, :LANES] for ref in kv_refs], axis=0)
    values = jnp.concatenate([turned_block(ref[:, LANES:]) for ref in kv_refs], axis=1)
    outs = []
    for which in range(2):
        query = stack_heads(query_ref[...], which)
        scores = jnp.where(seen, dot_nt(keys, query), masked_score)
        peak = jnp.max(scores, axis=0, keepdims=True)
        weight = jnp.exp(scores - peak)
        total = jnp.sum(weight, axis=0, keepdims=True)
        outs.append(dot_nn(values, weight.astype(low)) / total)
        log_ref[0, which : which + 1, :] = peak + jnp.log(total)
    first = lane_of(outs[0].shape, 0, 0)
    both = jnp.where(first, outs[0], outs[1]).T
    for g in range(GROUPS):
        piece = both[g * tokens : (g + 1) * tokens, :]
        out_ref[:, g * LANES : (g + 1) * LANES] = piece
        out_low_ref[:, g * LANES : (g + 1) * LANES] = piece.astype(low)


def attend(query, key_pos, query_pos, kv_parts, order):
    tokens = query.shape[0]
    count = len(kv_parts)
    seq_len = tokens * count
    pairs = pl.BlockSpec((tokens, PAIR_WIDTH), lambda p: (0, p))
    return call(
        functools.partial(attend_body, count),
        (PAIRS,),
        [
            pairs,
            pl.BlockSpec((seq_len, 1), lambda p: (0, 0)),
            pl.BlockSpec((1, tokens), lambda p: (0, 0)),
        ]
        + [pl.BlockSpec((tokens, 2 * LANES), lambda p: (0, p))] * count,
        [pairs, pairs, pl.BlockSpec((1, 2, GROUPS * tokens), lambda p: (p, 0, 0))],
        [
            jax.ShapeDtypeStruct((tokens, QUERY_WIDTH), wide),
            jax.ShapeDtypeStruct((tokens, QUERY_WIDTH), low),
            jax.ShapeDtypeStruct((PAIRS, 2, GROUPS * tokens), wide),
        ],
    )(query, key_pos, query_pos, *kv_parts, order)


def attend_back_body(count, own_ref, query_ref, grad_ref, out_ref, log_ref, key_pos_ref, query_pos_ref,
                     scale_ref, cos_ref, sin_ref, *refs):
    kv_refs, (grad_query_ref, grad_kv_ref) = refs[:count], refs[count:]
    tokens = query_ref.shape[0]
    grads = grad_ref[...]
    product = jnp.concatenate(
        [
            (grads[:, g * LANES : (g + 1) * LANES].astype(wide)
             * out_ref[:, g * LANES : (g + 1) * LANES]).T
            for g in range(GROUPS)
        ],
        axis=1,
    )
    first = lane_of(product.shape, 0, 0)
    delta = [
        jnp.sum(jnp.where(first, product, 0.0), axis=0, keepdims=True),
        jnp.sum(jnp.where(first, 0.0, product), axis=0, keepdims=True),
    ]
    seen = allowed_pairs(key_pos_ref[...], query_pos_ref[...])
    keys = jnp.concatenate([ref[:, :LANES] for ref in kv_refs], axis=0)
    values = jnp.concatenate([ref[:, LANES:] for ref in kv_refs], axis=0)
    keys_turned = jnp.concatenate([turned_block(ref[:, :LANES]) for ref in kv_refs], axis=1)
    grad_key, grad_value, grad_query = None, None, []
    for which in range(2):
        query = stack_heads(query_ref[...], which)
        head = stack_heads(grads, which)
        scores = jnp.where(seen, dot_nt(keys, query), masked_score)
        probs = jnp.exp(scores - log_ref[0, which : which + 1, :])
        grad_probs = dot_nt(values, head)
        grad_scores = (probs * (grad_probs - delta[which])).astype(low)
        part_value = dot_nn(probs.astype(low), head)
        part_key = dot_nn(grad_scores, query)
        grad_query.append(dot_nn(keys_turned, grad_scores))
        grad_value = part_value if grad_value is None else grad_value + part_value
        grad_key = part_key if grad_key is None else grad_key + part_key
    scale, cosine, sine = scale_ref[...], cos_ref[...], sin_ref[...]
    for k in range(count):
        rows = slice(k * tokens, (k + 1) * tokens)
        grad_kv_ref[own_ref[0] ^ k, :, :LANES] = grad_key[rows, :].astype(low)
        grad_kv_ref[own_ref[0] ^ k, :, LANES:] = grad_value[rows, :].astype(low)
    first = lane_of(grad_query[0].shape, 0, 0)
    both = (jnp.where(first, grad_query[0], grad_query[1]) * HEAD_DIM**-0.5).T
    for g in range(GROUPS):
        piece = both[g * tokens : (g + 1) * tokens, :]
        back = turn(piece, cosine, -sine) * scale
        grad_query_ref[:, g * LANES : (g + 1) * LANES] = back.astype(low)


def attend_back(
    own, query, grads, out, logs, key_pos, query_pos, scale, cosine, sine, kv_parts, order
):
    tokens = query.shape[0]
    count = len(kv_parts)
    seq_len = tokens * count
    pairs = pl.BlockSpec((tokens, PAIR_WIDTH), lambda p: (0, p))
    whole = lambda shape: pl.BlockSpec(shape, lambda p: (0, 0))
    part = pl.BlockSpec((tokens, 2 * LANES), lambda p: (0, p))
    return call(
        functools.partial(attend_back_body, count),
        (PAIRS,),
        [
            SCALAR,
            pairs,
            pairs,
            pairs,
            pl.BlockSpec((1, 2, GROUPS * tokens), lambda p: (p, 0, 0)),
            whole((seq_len, 1)),
            whole((1, tokens)),
            whole((tokens, 1)),
            whole((tokens, LANES)),
            whole((tokens, LANES)),
        ]
        + [part] * count,
        [pairs, pl.BlockSpec((count, tokens, 2 * LANES), lambda p: (0, 0, p))],
        [
            jax.ShapeDtypeStruct((tokens, QUERY_WIDTH), low),
            jax.ShapeDtypeStruct((count, tokens, 2 * KV_WIDTH), low),
        ],
    )(own, query, grads, out, logs, key_pos, query_pos, scale, cosine, sine, *kv_parts, order)


def hidden_body(count, first, own_ref, grads_ref, gate_ref, weight_ref, *refs):
    part_refs, (hidden_ref, back_ref, rows_ref) = refs[:count], refs[count:]
    expert, place = pl.program_id(0), pl.program_id(1)
    block = grads_ref.shape[0]
    tokens = part_refs[0].shape[0]

    @pl.when((expert == 0) & (place == 0))
    def _():
        for k, part_ref in enumerate(part_refs):
            start = pl.multiple_of((own_ref[0] ^ k) * tokens, tokens)
            rows_ref[pl.ds(start, tokens), :] = part_ref[...]

    rows = rows_ref[pl.ds(pl.multiple_of(place * block, block), block), :]
    grads = grads_ref[...]
    lane = lax.broadcasted_iota(jnp.int32, gate_ref.shape, 1) % (LANES // 2)
    weight = jnp.sum(
        jnp.where(lane == expert + first, gate_ref[...].astype(wide), 0.0), axis=1, keepdims=True
    )
    step = 256
    for h in range(0, FF, step):
        gate = dot_nn(rows, weight_ref[0, :, h : h + step])
        up = dot_nn(rows, weight_ref[0, :, FF + h : FF + h + step])
        grad_hidden = dot_nn(grads, weight_ref[0, :, 2 * FF + h : 2 * FF + h + step]) * weight
        sigmoid = 1.0 / (1.0 + jnp.exp(-gate))
        active = gate * sigmoid
        hidden_ref[0, :, h : h + step] = (active * up * weight).astype(low)
        slope = sigmoid + active * (1.0 - sigmoid)
        back_ref[0, :, h : h + step] = (grad_hidden * up * slope).astype(low)
        back_ref[0, :, FF + h : FF + h + step] = (grad_hidden * active).astype(low)


def expert_hidden(own, parts, grads, first, weights, order):
    tokens = grads.shape[0]
    width = parts[0].shape[1]
    experts = weights.shape[0]
    block = min(tokens, 1024)
    part_rows = parts[0].shape[0]
    return call(
        functools.partial(hidden_body, len(parts), first),
        (experts, tokens // block),
        [
            SCALAR,
            pl.BlockSpec((block, width), lambda e, t: (t, 0)),
            pl.BlockSpec((block, LANES), lambda e, t: (t, width // LANES)),
            pl.BlockSpec((1, width, 3 * FF), lambda e, t: (e, 0, 0)),
        ]
        + [
            pl.BlockSpec((part_rows, width), lambda e, t: (0, 0), pipeline_mode=pl.Buffered(1))
        ]
        * len(parts),
        [
            pl.BlockSpec((1, block, FF), lambda e, t: (e, t, 0)),
            pl.BlockSpec((1, block, 2 * FF), lambda e, t: (e, t, 0)),
        ],
        [
            jax.ShapeDtypeStruct((experts, tokens, FF), low),
            jax.ShapeDtypeStruct((experts, tokens, 2 * FF), low),
        ],
        scratch=[pltpu.VMEM((tokens, width), low)],
    )(own, grads, grads, weights, *parts, order)


def turn_body(count, slices, own_ref, place_ref, *refs):
    part_refs, (out_ref, placed_ref) = refs[:count], refs[count:]
    width, tokens = out_ref.shape[0], part_refs[0].shape[0]
    size = width // slices
    for k, part_ref in enumerate(part_refs):
        turned = turned_block(part_ref[...])
        column = pl.multiple_of((own_ref[0] ^ k) * tokens, tokens)
        out_ref[:, pl.ds(column, tokens)] = turned
        for i in range(slices):
            start = pl.multiple_of(place_ref[i] * size, size)
            placed_ref[pl.ds(start, size), pl.ds(column, tokens)] = turned[i * size : (i + 1) * size, :]


def turn_rows(own, place, parts, tokens, width, count, order):
    specs = [
        pl.BlockSpec((tokens, width), (lambda i, k=k: (k, 0)) if len(parts) == 1 else (lambda i: (0, 0)))
        for k in range(count)
    ]
    out = pl.BlockSpec((width, count * tokens), lambda i: (0, 0), pipeline_mode=pl.Buffered(1))
    return call(
        functools.partial(turn_body, count, place.shape[0]),
        (1,),
        [SCALAR, SCALAR, *specs],
        [out, out],
        [jax.ShapeDtypeStruct((width, count * tokens), low)] * 2,
    )(own, place, *(parts * count if len(parts) == 1 else parts), order)


def weight_grad_body(rows_ref, grads_ref, back_ref, hidden_ref, *out_refs):
    from_rows = dot_nn(rows_ref[...], back_ref[0]).astype(low)
    from_grads = dot_nn(grads_ref[...], hidden_ref[0]).astype(low)
    for half, out_ref in enumerate(out_refs):

        @pl.when((len(out_refs) == 1) | (pl.program_id(1) == half))
        def _():
            out_ref[0, :, : 2 * FF] = from_rows
            out_ref[0, :, 2 * FF :] = from_grads


def expert_weight_grads(rows_turned, grads_turned, hidden, back, halves, order):
    width, tokens = rows_turned.shape
    experts = back.shape[0]
    block = width // 2
    if halves:
        out_specs = [pl.BlockSpec((1, block, 3 * FF), lambda e, m: (e, 0, 0))] * 2
        out_shape = [jax.ShapeDtypeStruct((experts, block, 3 * FF), low)] * 2
    else:
        out_specs = [pl.BlockSpec((1, block, 3 * FF), lambda e, m: (e, m, 0))]
        out_shape = [jax.ShapeDtypeStruct((experts, width, 3 * FF), low)]
    return call(
        weight_grad_body,
        (experts, 2),
        [
            pl.BlockSpec((block, tokens), lambda e, m: (m, 0)),
            pl.BlockSpec((block, tokens), lambda e, m: (m, 0)),
            pl.BlockSpec((1, tokens, 2 * FF), lambda e, m: (e, 0, 0)),
            pl.BlockSpec((1, tokens, FF), lambda e, m: (e, 0, 0)),
        ],
        out_specs,
        out_shape,
    )(rows_turned, grads_turned, back, hidden, order)


def slices_body(plan, *refs):
    count = max(index for terms in plan for index, _ in terms) + 1
    arrays, outs = refs[:count], refs[count:]
    for terms, out_ref in zip(plan, outs):
        size = out_ref.shape[1]
        out_ref[0] = functools.reduce(
            jnp.add, [arrays[i][0, start : start + size, :].astype(wide) for i, start in terms]
        ).astype(low)


def add_slices(arrays, plan, sizes, order):
    experts, _, columns = arrays[0].shape
    spec = lambda rows: pl.BlockSpec((1, rows, columns), lambda e: (e, 0, 0))
    return call(
        functools.partial(slices_body, plan),
        (experts,),
        [spec(array.shape[1]) for array in arrays],
        [spec(size) for size in sizes],
        [jax.ShapeDtypeStruct((experts, size, columns), low) for size in sizes],
    )(*arrays, order)


class LineSum:
    def __init__(self, own, other):
        self.own = own
        self.came = swap(other, "dp", 1)
        self.size = own.shape[1] // 4

    def inward(self, *others):
        size = self.size
        self.first, self.last = add_slices(
            [self.own, self.came],
            [[(0, 0), (1, 0)], [(0, 3 * size), (1, 3 * size)]],
            [3 * size, size],
            token(*others),
        )
        self.from_end = lax.ppermute(self.first, "context", [(0, 1), (3, 2)])
        return self.last

    def across(self, *others):
        size = self.size
        plan = [[(0, 0), (1, 0)], [(0, size), (1, size)]]
        self.kept, sent = add_slices(
            [self.first, self.from_end], plan, [size, 2 * size], token(*others)
        )
        self.from_inner = lax.ppermute(sent, "context", [(1, 2), (2, 1)])
        return sent

    def outward(self, *others):
        size = self.size
        self.kept, sent = add_slices(
            [self.kept, self.last, self.from_inner],
            [[(0, 0), (2, 0)], [(1, 0), (2, size)]],
            [size, size],
            token(*others),
        )
        self.to_end = lax.ppermute(sent, "context", [(1, 0), (2, 3)])
        return sent

    def finish(self, *others):
        return [self.kept, self.last, self.to_end]


def combine_body(sizes, own_ref, *refs):
    count = len(sizes)
    part_refs, weight_refs = refs[:count], refs[count : 2 * count]
    out_refs, total_ref = refs[2 * count : -1], refs[-1]
    step = pl.program_id(0)

    @pl.when(step == 0)
    def _():
        total_ref[...] = jnp.zeros_like(total_ref)

    start = 0
    for part_ref, weight_ref, size in zip(part_refs, weight_refs, sizes):

        @pl.when((step >= start) & (step < start + size))
        def _():
            total_ref[...] += dot_nt(part_ref[0], weight_ref[0])

        start += size

    @pl.when(step == start - 1)
    def _():
        tokens = out_refs[0].shape[0]
        for k, out_ref in enumerate(out_refs):
            place = pl.multiple_of((own_ref[0] ^ k) * tokens, tokens) if len(out_refs) > 1 else 0
            out_ref[...] = total_ref[pl.ds(place, tokens), :].astype(low)


def combine(own, owners, parts, weights, column, order):
    tokens, depth = parts[0].shape[1:]
    width = weights[0].shape[1]
    sizes = [w.shape[0] for w in weights]
    starts = [sum(sizes[:i]) for i in range(len(sizes))]
    place = lambda e, start, size: jnp.clip(e - start, 0, size - 1)
    part_specs = [
        pl.BlockSpec((1, tokens, depth), lambda e, s=s, n=n: (place(e, s, n), 0, 0))
        for s, n in zip(starts, sizes)
    ]
    weight_specs = [
        pl.BlockSpec((1, width, depth), lambda e, s=s, n=n: (place(e, s, n), 0, column))
        for s, n in zip(starts, sizes)
    ]
    return call(
        functools.partial(combine_body, sizes),
        (sum(sizes),),
        [SCALAR] + part_specs + weight_specs,
        [pl.BlockSpec((tokens // owners, width), lambda e: (0, 0))] * owners,
        [jax.ShapeDtypeStruct((tokens // owners, width), low)] * owners,
        scratch=[pltpu.VMEM((tokens, width), wide)],
    )(own, *parts, *weights, order)


def norm_back_body(count, scale_ref, gain_ref, middle_ref, cotangent_ref, weight_ref, *refs):
    part_refs = refs[:count]
    middle_grad_ref, turned_ref, attended_ref, gain_grad_ref, proj_ref = refs[count:]

    @pl.when(pl.program_id(0) == 0)
    def _():
        grad = functools.reduce(jnp.add, [ref[...].astype(wide) for ref in part_refs])
        scale = scale_ref[...]
        unit = middle_ref[...] * scale
        gain = jnp.sum((grad * unit).T, axis=1, keepdims=True)
        gain_grad_ref[...] = jnp.broadcast_to(gain, gain_grad_ref.shape).astype(low)
        grad = grad * gain_ref[...]
        mean = jnp.mean(grad * unit, axis=1, keepdims=True)
        grad = cotangent_ref[...].astype(wide) + scale * (grad - unit * mean)
        middle_grad_ref[...] = grad
        proj_ref[...] = grad.astype(low)
        turned_ref[...] = grad.T.astype(low)

    attended_ref[...] = dot_nn(proj_ref[...], weight_ref[...]).astype(low)


def norm_back_two(parts, middle, scale, gain, cotangent, output_pack, order):
    tokens, width = middle.shape
    block = 512
    whole = lambda shape: pl.BlockSpec(shape, lambda j: (0, 0))
    return call(
        functools.partial(norm_back_body, len(parts)),
        (QUERY_WIDTH // block,),
        [
            whole((tokens, 1)),
            whole((1, width)),
            whole((tokens, width)),
            whole((tokens, width)),
            pl.BlockSpec((width, block), lambda j: (0, j)),
        ]
        + [whole((tokens, width))] * len(parts),
        [
            whole((tokens, width)),
            whole((width, tokens)),
            pl.BlockSpec((tokens, block), lambda j: (0, j)),
            whole((width, LANES)),
        ],
        [
            jax.ShapeDtypeStruct((tokens, width), wide),
            jax.ShapeDtypeStruct((width, tokens), low),
            jax.ShapeDtypeStruct((tokens, QUERY_WIDTH), low),
            jax.ShapeDtypeStruct((width, LANES), low),
        ],
        scratch=[pltpu.VMEM((tokens, width), low)],
    )(scale, gain, middle, cotangent, output_pack, *parts, order)


def outer_body(rows, first, place_ref, input_ref, proj_ref, gain_ref, query_ref, attended_ref,
               out_ref, picked_ref):
    out_ref[:, :QUERY_WIDTH] = dot_nn(input_ref[...], query_ref[...]).astype(low)
    if rows:
        for i in range(out_ref.shape[0] // rows):
            start = pl.multiple_of(place_ref[first + i] * rows, rows)
            part = slice(i * rows, (i + 1) * rows)
            picked_ref[part, :] = proj_ref[pl.ds(start, rows), :]
            out_ref[part, 2 * QUERY_WIDTH :] = gain_ref[pl.ds(start, rows), :]
    else:
        picked_ref[...] = proj_ref[...]
        out_ref[:, 2 * QUERY_WIDTH :] = gain_ref[...]
    out_ref[:, QUERY_WIDTH : 2 * QUERY_WIDTH] = dot_nn(picked_ref[...], attended_ref[...]).astype(low)


def outer_grads(half, cores, place, input_turned, proj_turned, gain_turned, grad_query, attended, order):
    width, tokens = input_turned.shape
    rows = width // cores
    slice_rows = width // place.shape[0]
    part = lambda columns: pl.BlockSpec((rows, columns), lambda i: (half, 0))
    inside = slice_rows % 16 == 0
    every = lambda columns: pl.BlockSpec((width, columns), lambda i: (0, 0))
    if not inside:
        pick = lambda array: jnp.take(
            array.reshape(place.shape[0], slice_rows, -1), place, axis=0, mode="clip"
        ).reshape(array.shape)
        proj_turned, gain_turned = pick(proj_turned), pick(gain_turned)
        every = part
    whole = pl.BlockSpec((tokens, QUERY_WIDTH), lambda i: (0, 0))
    columns = 2 * QUERY_WIDTH + LANES
    return call(
        functools.partial(outer_body, slice_rows if inside else 0, half * (place.shape[0] // cores)),
        (1,),
        [SCALAR, part(tokens), every(tokens), every(LANES), whole, whole],
        pl.BlockSpec((rows, columns), lambda i: (0, 0)),
        jax.ShapeDtypeStruct((rows, columns), low),
        scratch=[pltpu.VMEM((rows, tokens), low)],
    )(place, input_turned, proj_turned, gain_turned, grad_query, attended, order)


def kv_body(parts_ref, scale_ref, cos_ref, sin_ref, input_ref, grad_ref, *out_refs):
    total = jnp.sum(parts_ref[...].astype(wide), axis=0)
    cosine, sine, scale = cos_ref[...], sin_ref[...], scale_ref[...]
    for i in range(2 * PAIRS):
        group = total[:, i * LANES : (i + 1) * LANES]
        group = turn(group, cosine, -sine) if i % 2 == 0 else group
        grad_ref[:, i * LANES : (i + 1) * LANES] = (group * scale).astype(low)
    grads = grad_ref[...]
    rows = out_refs[0].shape[0]
    for k, out_ref in enumerate(out_refs):
        out_ref[...] = dot_nn(input_ref[k * rows : (k + 1) * rows, :], grads).astype(low)


def kv_grads(cores, parts, scale, cosine, sine, input_turned, order):
    tokens, columns = parts.shape[1:]
    width = input_turned.shape[0]
    shapes = [(tokens, columns)] + [(width // cores, columns)] * cores
    whole = lambda shape: pl.BlockSpec(shape, lambda i: (0,) * len(shape))
    return call(
        kv_body,
        (1,),
        [
            whole(parts.shape),
            whole((tokens, 1)),
            whole((tokens, LANES)),
            whole((tokens, LANES)),
            whole((width, tokens)),
        ],
        [whole(shape) for shape in shapes],
        [jax.ShapeDtypeStruct(shape, low) for shape in shapes],
    )(parts, scale, cosine, sine, input_turned, order)


def input_body(count, rows, place_ref, query_ref, kv_ref, scale_ref, input_ref, middle_ref, *refs):
    weight_refs, (out_ref, turned_ref) = refs[:count], refs[count:]
    weights = jnp.concatenate([ref[...] for ref in weight_refs], axis=0)
    part = dot_nt(weights[:, :QUERY_WIDTH], query_ref[...])
    part += dot_nt(weights[:, QUERY_WIDTH:], kv_ref[...])
    for i in range(part.shape[0] // rows):
        start = pl.multiple_of(place_ref[i] * rows, rows)
        turned_ref[pl.ds(start, rows), :] = part[i * rows : (i + 1) * rows, :]
    grad = turned_ref[...].T
    unit = input_ref[...].astype(wide) * scale_ref[...]
    mean = jnp.mean(grad * unit, axis=1, keepdims=True)
    out_ref[...] = (middle_ref[...] + grad - unit * mean).astype(low)


def input_grads(place, grad_query, grad_kv, scale, rows, grad_middle, weights, order):
    tokens, width = rows.shape
    whole = lambda array: pl.BlockSpec(array.shape, lambda i: (0, 0))
    operands = [grad_query, grad_kv, scale, rows, grad_middle, *weights]
    return call(
        functools.partial(input_body, len(weights), width // place.shape[0]),
        (1,),
        [SCALAR] + [whole(operand) for operand in operands],
        pl.BlockSpec((tokens, width), lambda i: (0, 0)),
        jax.ShapeDtypeStruct((tokens, width), low),
        scratch=[pltpu.VMEM((width, tokens), wide)],
    )(place, *operands, order)


def adam_body(count, held, inner_ref, *refs):
    grads, refs = [ref[0].astype(wide) for ref in refs[:count]], refs[count:]
    expand, contract, refs = refs[:3], refs[3:6], refs[6 + held :]
    if count == 1:
        grads = grads[0]
    else:
        grads = jnp.where(inner_ref[0] == 1, grads[0], grads[1] + grads[2])
    split = expand[0].shape[2]
    for arrays, grad, rate, out_refs in (
        (expand, grads[:, :split], rate_expand, refs[:3]),
        (contract, grads[:, split:], rate_contract, refs[3:]),
    ):
        results = adamw(*[array[0] for array in arrays], grad, rate, decay_rate)
        for out_ref, result in zip(out_refs, results):
            out_ref[0] = result


def adam_experts(first, inner, grads, arrays, held, order):
    count = grads[0].shape[0]
    held = held or []
    block = lambda array: pl.BlockSpec((1, *array.shape[1:]), lambda e: (first + e, 0, 0))
    return call(
        functools.partial(adam_body, len(grads), len(held)),
        (count,),
        [SCALAR]
        + [pl.BlockSpec((1, *grad.shape[1:]), lambda e: (e, 0, 0)) for grad in grads]
        + [block(array) for array in arrays]
        + [pl.BlockSpec(memory_space=pl.ANY)] * len(held),
        [block(array) for array in arrays],
        [jax.ShapeDtypeStruct(array.shape, wide) for array in arrays],
        aliases={1 + len(grads) + len(arrays) + i: i for i in range(len(held))},
    )(inner, *grads, *arrays, *held, order)


def adam_joined_body(count, query_mat_ref, key_mat_ref, gain_ref, *refs):
    grads, kv = [
        functools.reduce(jnp.add, [ref[...].astype(wide) for ref in part])
        for part in (refs[:count], refs[count : 2 * count])
    ]
    refs = refs[2 * count :]
    joined, output, gains, outs = refs[:3], refs[3:6], refs[6:9], refs[9:]
    back = lambda grad, mat: lax.dot_general(
        grad, mat, (((1,), (1,)), ((), ())), precision=lax.Precision.HIGHEST, preferred_element_type=wide
    )
    query_mat, key_mat = query_mat_ref[...], key_mat_ref[...]
    pairs = lambda start: [
        back(grads[:, start + p * PAIR_WIDTH : start + (p + 1) * PAIR_WIDTH], query_mat)
        for p in range(PAIRS)
    ]
    keys = [back(kv[:, 2 * p * LANES : (2 * p + 1) * LANES], key_mat) for p in range(PAIRS)]
    values = [back(kv[:, (2 * p + 1) * LANES : (2 * p + 2) * LANES], key_mat) for p in range(PAIRS)]
    unit_grad = jnp.concatenate([*pairs(0), *keys, *values], axis=1)
    low_weight = joined[0][...].astype(low).astype(wide)
    gain_one = jnp.sum(low_weight * unit_grad, axis=1, keepdims=True)
    gain_two = grads[:, 2 * QUERY_WIDTH : 2 * QUERY_WIDTH + 1]
    output_grad = jnp.concatenate(pairs(QUERY_WIDTH), axis=1)
    joined_grad = gain_ref[...] * unit_grad
    gains_grad = jnp.concatenate([gain_one, gain_two], axis=1)
    for arrays, grad, rate, decay, out_refs in (
        (joined, joined_grad, rate_joined, decay_rate, outs[:3]),
        (output, output_grad, rate_output, decay_rate, outs[3:6]),
        (gains, gains_grad, rate_gains, 0.0, outs[6:]),
    ):
        results = adamw(*[array[...] for array in arrays], grad, rate, decay)
        for out_ref, result in zip(out_refs, results):
            out_ref[...] = result


def adam_joined(gain, query_parts, kv_parts, arrays, order):
    query_mat, key_mat = order_matrix(GROUPS).astype(wide), order_matrix(1).astype(wide)
    operands = [query_mat, key_mat, gain, *query_parts, *kv_parts, *arrays]
    whole = lambda array: pl.BlockSpec(array.shape, lambda i: (0, 0))
    return call(
        functools.partial(adam_joined_body, len(query_parts)),
        (1,),
        [whole(operand) for operand in operands],
        [whole(array) for array in arrays],
        [jax.ShapeDtypeStruct(array.shape, wide) for array in arrays],
    )(*operands, order)


def body(
    layer_input,
    cotangent,
    block_order,
    routes,
    route_gates,
    joined_weight,
    joined_first,
    joined_second,
    output_weight,
    output_first,
    output_second,
    norm_gains,
    gains_first,
    gains_second,
    expand_weight,
    expand_first,
    expand_second,
    contract_weight,
    contract_first,
    contract_second,
):
    experts_dev = expand_weight.shape[0]
    owners = lax.axis_size("expert")
    contexts = lax.axis_size("context")
    cores = lax.axis_size("dp")
    experts = experts_dev * owners
    tokens = layer_input.shape[1]
    width = layer_input.shape[2]
    half_block = tokens // 2
    slice_rows = joined_weight.shape[0]
    own_expert = lax.axis_index("expert")
    own_context = lax.axis_index("context")
    own_core = lax.axis_index("dp")

    gain_rows = norm_gains.astype(low).astype(wide).T
    joined_low = joined_weight.astype(low)
    joined_shard = reorder_columns((gain_rows[:, :1] * joined_low.astype(wide)).astype(low)).astype(low)
    query_mat = order_matrix(GROUPS)
    output_shard = jnp.einsum(
        "pod,on->dpn",
        output_weight.astype(low).reshape(PAIRS, PAIR_WIDTH, slice_rows),
        query_mat,
        preferred_element_type=wide,
    ).reshape(slice_rows, QUERY_WIDTH).astype(low)
    gain_column = jnp.broadcast_to(gain_rows[:, 1:].astype(low), (slice_rows, LANES))
    columns = joined_shard.shape[1]
    shard = jnp.concatenate([joined_shard, output_shard, gain_column], axis=1)

    bounds = [0, experts_dev // 2, experts_dev]
    chunks = list(zip(bounds[:-1], bounds[1:]))
    expert_low = [
        jnp.concatenate(
            [
                expand_weight[a:b].astype(low),
                jnp.swapaxes(contract_weight[a:b].astype(low), 1, 2),
            ],
            axis=2,
        )
        for a, b in chunks
    ]
    line, *expert_low = lax.optimization_barrier(
        (jnp.concatenate(spread(shard, "context"), axis=0), *expert_low)
    )
    joined_mine = spread(line[:, :columns], "expert")
    gather_expert = lambda part: lax.all_gather(part, ("context", "dp"), axis=1, tiled=True)
    expert_full = [gather_expert(expert_low[0])]

    ar = lambda n: jnp.arange(n, dtype=jnp.int32)
    to_relative = (
        ((own_expert ^ ar(owners))[None, :, None] * contexts + (own_context ^ ar(contexts))[None, None, :])
        * cores
        + (own_core ^ ar(cores))[:, None, None]
    ).reshape(-1)
    to_absolute = (
        (own_core ^ ar(cores))[None, None, :] * owners + (own_expert ^ ar(owners))[:, None, None]
    ) * contexts + (own_context ^ ar(contexts))[None, :, None]
    to_absolute = to_absolute.reshape(-1)
    slices = owners * contexts * cores

    def pick_rows(rows, index):
        return jnp.take(
            rows.reshape(slices, slice_rows, -1), index, axis=0, mode="clip", unique_indices=True
        ).reshape(rows.shape)

    hits = routes[0][:, :, None] == ar(experts)[None, None, :]
    gate_table = jnp.sum(jnp.where(hits, route_gates[0][:, :, None], 0.0), axis=1)
    gate_table = gate_table.reshape(tokens, owners, experts_dev)
    high = lax.reduce_precision(gate_table, 8, 7)
    terms = jnp.stack([high, gate_table - high], axis=2)
    terms = jnp.pad(terms, ((0, 0), (0, 0), (0, 0), (0, LANES // 2 - experts_dev)))
    terms = terms.reshape(tokens, owners, LANES).transpose(1, 0, 2).astype(low)
    grads_sent = jnp.concatenate(
        [jnp.broadcast_to(cotangent, (owners, tokens, width)), terms], axis=2
    )
    own = own_expert.reshape(1)
    zero = jnp.zeros((1,), jnp.int32)
    on_line = contexts == 4 and cores == 2
    inner = ((own_context == 1) | (own_context == 2)).astype(jnp.int32).reshape(1)
    if on_line:
        along = jnp.where(
            own_context < 2, jnp.array([3, 0, 1, 2], jnp.int32), jnp.array([2, 1, 0, 3], jnp.int32)
        )
        line_place = (along[:, None] + (own_core ^ ar(cores))[None, :] * contexts).reshape(-1)
    else:
        line_place = ar(contexts * cores)

    order = block_order[0]
    offsets = ar(half_block)

    def places_of(index):
        mine = lax.dynamic_slice_in_dim(order, 2 * index, 2)
        return (mine[:, None] * half_block + offsets[None, :]).reshape(-1)

    query_pos = places_of(own_context)
    key_pos = jnp.concatenate([places_of(own_context ^ k) for k in range(contexts)])
    half = HEAD_DIM // 2
    freq = jnp.exp(ar(half).astype(wide) * (2.0 / HEAD_DIM) * -math.log(10000.0))
    angle = query_pos.astype(wide)[:, None] * freq[None, :]
    cosine = jnp.tile(jnp.cos(angle), (1, 4))
    sine = jnp.sin(angle)
    sine = jnp.concatenate([-sine, -sine, sine, sine], axis=1)

    low_input = layer_input[0]
    resid = low_input.astype(wide)
    scale_one = lax.rsqrt(jnp.mean(resid * resid, axis=-1, keepdims=True) + norm_eps)
    unit_one = resid * scale_one
    input_turned = pick_rows(low_input.T, to_relative)
    input_relative = input_turned.T
    first, *others, grads_sent = lax.optimization_barrier(
        (*joined_mine, grads_sent, cosine, sine, scale_one, input_relative)
    )[: owners + 1]
    joined_mine = [first, *others]
    joined_parts = joined_mine + [swap(part, "dp", 1) for part in joined_mine]
    output_mine = share(after(line[:, columns:], *joined_mine), "expert")
    query, kv = project(input_relative, scale_one, cosine, sine, joined_parts, token())
    kv_parts = spread(kv, "context")
    output_mine = after(output_mine, kv)
    output_parts = [output_mine, swap(output_mine, "dp", 1)]
    out_grads = trade(after(grads_sent, output_mine), "expert").reshape(owners * tokens, -1)
    output_place = (
        (own_core ^ ar(cores))[None, None, :] * owners + ar(owners)[:, None, None]
    ) * contexts + (own_context ^ ar(contexts))[None, :, None]
    output_pack = pick_rows(
        jnp.concatenate([part.reshape(-1, output_mine.shape[-1]) for part in output_parts], axis=0),
        output_place.reshape(-1),
    )
    output_turned = output_pack[:, :QUERY_WIDTH]
    gain_two = output_pack[:, QUERY_WIDTH].astype(wide)[None, :]
    out_grads_turned = turn_rows(
        zero, line_place, [out_grads], tokens, width, owners, token(output_pack)
    )
    kv_parts = all_after(kv_parts, output_pack, *out_grads_turned)
    kv_parts, later = lax.optimization_barrier((kv_parts, expert_low[1:]))
    expert_full += [gather_expert(part) for part in later]
    attended_wide, attended, logs = attend(
        query, key_pos[:, None], query_pos[None, :], kv_parts, token()
    )
    middle = resid + dot_nt(attended, output_turned)
    scale_two = lax.rsqrt(jnp.mean(middle * middle, axis=-1, keepdims=True) + norm_eps)
    unit_two = middle * scale_two
    normed_two = (unit_two * gain_two).astype(low)

    row_parts = spread(normed_two, "expert")
    def grads_of(unit, on_line, *others):
        return expert_weight_grads(
            rows_turned[on_line], out_grads_turned[on_line], *unit, on_line, token(*others)
        )

    def to_owners(grads):
        return lax.psum_scatter(grads, ("context", "dp"), scatter_dimension=1, tiled=True)

    def to_tokens(parts):
        return [parts[0]] + [swap(parts[k], "expert", k) for k in range(1, owners)]

    cut = bounds[1]
    first_unit = expert_hidden(
        own, row_parts, out_grads, 0, expert_full[0], token()
    )
    rows_turned = turn_rows(
        own, line_place, row_parts, tokens, width, owners, token(first_unit[0])
    )
    first_grads = grads_of(first_unit, on_line)
    if on_line:
        line_sum = LineSum(*first_grads)
        latest = line_sum.inward()
    else:
        first_sum = to_owners(first_grads[0])
        latest = first_grads[0]
    second_unit = expert_hidden(own, row_parts, out_grads, cut, expert_full[1], token(latest))
    backs = [first_unit[1], second_unit[1]]
    grad_sent = combine(own, owners, backs, expert_full, 0, token())
    grad_parts = to_tokens(grad_sent)
    second_grads = grads_of(second_unit, False, *grad_sent)[0]
    latest = line_sum.across(second_grads) if on_line else second_grads
    mixture_sent = combine(
        own, owners, [first_unit[0], second_unit[0]], expert_full, 2, token(latest)
    )
    *mixture_sent, second_grads, grad_parts = lax.optimization_barrier(
        (*mixture_sent, second_grads, grad_parts)
    )
    second_sum = to_owners(second_grads)
    mixture_parts = to_tokens(mixture_sent)

    grad_middle, proj_turned, grad_attended, gain_turned = norm_back_two(
        grad_parts, middle, scale_two, gain_two, cotangent[0], output_pack, token(*mixture_sent)
    )
    grad_query, grad_kv = attend_back(
        own_context.reshape(1), query, grad_attended, attended_wide, logs, key_pos[:, None],
        query_pos[None, :], scale_one, cosine, sine, kv_parts, token(grad_attended),
    )
    grad_kv_parts = trade(grad_kv, "context")

    def outer(half, *others):
        return outer_grads(
            half, cores, to_relative, input_turned, proj_turned, gain_turned, grad_query, attended,
            token(*others),
        )

    mixture = functools.reduce(
        jnp.add, [part.astype(wide) for part in all_after(mixture_parts, grad_query)]
    )
    output = (middle + mixture).astype(low)
    other = outer(1, output)
    query_sum = OwnerSum(outer(0, other), other, owners, contexts)
    latest = query_sum.spread_experts(query_sum.own)
    if on_line:
        latest = [line_sum.outward(*latest)]
    latest = query_sum.spread_contexts(*latest)
    own_grad_kv, *kv_parts_sent = kv_grads(
        cores, grad_kv_parts, scale_one, cosine, sine, input_turned, token(*latest)
    )
    kv_sum = OwnerSum(*kv_parts_sent, owners, contexts)
    latest = kv_sum.spread_experts(own_grad_kv)
    if slice_rows % 16 == 0:
        grad_input = input_grads(
            to_relative, grad_query, own_grad_kv, scale_one, low_input, grad_middle, joined_parts,
            token(*latest),
        )
    else:
        grad_joined = jnp.concatenate([grad_query, own_grad_kv], axis=1)
        scaled_grad = jnp.concatenate([dot_nt(part, grad_joined) for part in joined_parts], axis=0)
        scaled_grad = pick_rows(scaled_grad, to_absolute).T
        grad_input = (
            grad_middle
            + scaled_grad
            - unit_one * jnp.mean(scaled_grad * unit_one, axis=-1, keepdims=True)
        ).astype(low)

    latest = kv_sum.spread_contexts(grad_input)
    contract_arrays = [contract_weight, contract_first, contract_second]
    arrays = [expand_weight, expand_first, expand_second]
    arrays += [jnp.swapaxes(array, 1, 2) for array in contract_arrays]
    first_sum = line_sum.finish() if on_line else [first_sum]
    expert_new = adam_experts(0, inner, first_sum, arrays, None, token(*latest))
    expert_new = adam_experts(cut, inner, [second_sum], arrays, expert_new, token())
    expand_new = expert_new[:3]
    contract_new = [jnp.swapaxes(array, 1, 2) for array in expert_new[3:]]
    turned = [output_weight, output_first, output_second, norm_gains, gains_first, gains_second]
    joined_new = adam_joined(
        gain_rows[:, :1],
        query_sum.parts,
        kv_sum.parts,
        [joined_weight, joined_first, joined_second] + [array.T for array in turned],
        token(expand_new[0]),
    )
    output_new = [array.T for array in joined_new[3:6]]
    gains_new = [array.T for array in joined_new[6:]]
    joined_new = joined_new[:3]
    return (
        output.reshape(1, tokens, width),
        grad_input.reshape(1, tokens, width),
        *joined_new,
        *output_new,
        *gains_new,
        *expand_new,
        *contract_new,
    )


def solution(mesh):
    rows = P(("expert", "dp"), "context", None)
    joined = P(("expert", "context", "dp"), None)
    column = P(None, ("expert", "context", "dp"))
    expand = P("expert", ("context", "dp"), None)
    contract = P("expert", None, ("context", "dp"))
    placed = (
        (rows, rows, P(("expert", "dp"), None), rows, rows)
        + (joined,) * 3
        + (column,) * 6
        + (expand,) * 3
        + (contract,) * 3
    )
    return jax.shard_map(
        body,
        mesh=mesh,
        in_specs=placed,
        out_specs=(rows, rows) + placed[5:],
        check_vma=False,
    )
```

```python
import functools
import math

import jax
import jax.numpy as jnp
import numpy as np
from jax import lax
from jax.experimental import pallas as pl
from jax.experimental.pallas import tpu as pltpu
from jax.sharding import PartitionSpec as P

HEADS = 24
KV_HEADS = 8
HEAD_DIM = 64
FF = 512
TOP = 8
STEP = 10
GROUPS = HEADS // KV_HEADS
PAIRS = KV_HEADS // 2
QUERY_WIDTH = HEADS * HEAD_DIM
KV_WIDTH = KV_HEADS * HEAD_DIM
PAIR_WIDTH = 2 * GROUPS * HEAD_DIM
LANES = 128
VMEM_BYTES = 60 * 1024 * 1024
TOKEN = (8, 128)
SCALAR = pl.BlockSpec(memory_space=pltpu.SMEM)

norm_eps = 1e-06
beta_one = 0.9
beta_two = 0.95
adam_eps = 1e-08
decay_rate = 0.1
rate_joined = 0.08
rate_output = 0.6
rate_gains = 0.6
rate_expand = 0.08
rate_contract = 0.5
masked_score = -1e30

low = jnp.bfloat16
wide = jnp.float32


def adamw(weight, first, second, grad, rate, decay):
    first_new = beta_one * first + (1.0 - beta_one) * grad
    second_new = beta_two * second + (1.0 - beta_two) * grad * grad
    first_hat = first_new / (1.0 - beta_one**STEP)
    second_hat = second_new / (1.0 - beta_two**STEP)
    weight_new = weight - rate * (first_hat / (jnp.sqrt(second_hat) + adam_eps) + decay * weight)
    return (weight_new, first_new, second_new)


def dot_nn(left, right):
    return lax.dot_general(left, right, (((1,), (0,)), ((), ())), preferred_element_type=wide)


def dot_nt(left, right):
    return lax.dot_general(left, right, (((1,), (1,)), ((), ())), preferred_element_type=wide)


def pair_order(groups):
    half = HEAD_DIM // 2
    old = np.arange(2 * groups * HEAD_DIM).reshape(2, groups, 2, half)
    return old.transpose(1, 2, 0, 3).reshape(-1)


def order_matrix(groups):
    order = pair_order(groups)
    size = order.shape[0]
    return jnp.asarray(np.arange(size)[:, None] == order[None, :], dtype=low)


def reorder_columns(rows, back=False):
    count = rows.shape[0]
    query_mat = order_matrix(GROUPS)
    key_mat = order_matrix(1)
    kv = rows[:, QUERY_WIDTH:]
    if back:
        query_mat = query_mat.T
        key_mat = key_mat.T
        kv = jnp.swapaxes(kv.reshape(count, PAIRS, 2, LANES), 1, 2)
    else:
        kv = jnp.swapaxes(kv.reshape(count, 2, PAIRS, LANES), 1, 2)
    exact = lax.Precision.HIGHEST if rows.dtype == wide else None
    query = jnp.einsum(
        "rpo,on->rpn",
        rows[:, :QUERY_WIDTH].reshape(count, PAIRS, PAIR_WIDTH),
        query_mat.astype(rows.dtype),
        precision=exact,
        preferred_element_type=wide,
    ).reshape(count, QUERY_WIDTH)
    others = jnp.einsum(
        "rpo,on->rpn",
        kv.reshape(count, 2 * PAIRS, LANES),
        key_mat.astype(rows.dtype),
        precision=exact,
        preferred_element_type=wide,
    ).reshape(count, 2 * KV_WIDTH)
    return jnp.concatenate([query, others], axis=1)


def swap(block, axis, step):
    count = lax.axis_size(axis)
    return lax.ppermute(block, axis, [(i, i ^ step) for i in range(count)])


def spread(block, axis):
    return [block] + [swap(block, axis, k) for k in range(1, lax.axis_size(axis))]


def after(value, *others):
    return lax.optimization_barrier((value, *others))[0]


def all_after(values, *others):
    count = len(values)
    return list(lax.optimization_barrier((*values, *others))[:count])


def share(block, axis):
    return trade(jnp.broadcast_to(block[None], (lax.axis_size(axis), *block.shape)), axis)


def trade(blocks, axis):
    return lax.all_to_all(blocks, axis, split_axis=0, concat_axis=0, tiled=True)


def in_order(parts, own):
    rows = parts[0].shape[0]
    joined = jnp.zeros((len(parts) * rows, *parts[0].shape[1:]), parts[0].dtype)
    for k, part in enumerate(parts):
        joined = lax.dynamic_update_slice_in_dim(joined, part, (own ^ k) * rows, 0)
    return joined


def call(body, grid, in_specs, out_specs, out_shape, scratch=(), aliases=None):
    order = pl.BlockSpec(TOKEN, lambda *_: (0, 0))

    def ordered(*refs):
        place = len(in_specs)
        body(*refs[:place], *refs[place + 1 :])

    return pl.pallas_call(
        ordered,
        grid=grid,
        in_specs=[*in_specs, order],
        out_specs=out_specs,
        out_shape=out_shape,
        scratch_shapes=list(scratch),
        input_output_aliases=aliases or {},
        compiler_params=pltpu.CompilerParams(vmem_limit_bytes=VMEM_BYTES),
        cost_estimate=pl.CostEstimate(flops=1, bytes_accessed=1, transcendentals=0),
    )


def token(*others):
    return lax.optimization_barrier((jnp.zeros(TOKEN, wide), *others))[0]


def halves_body(own_ref, came_ref, *out_refs):
    total = own_ref[...].astype(wide) + came_ref[...].astype(wide)
    rows = out_refs[0].shape[0]
    for k, out_ref in enumerate(out_refs):
        out_ref[...] = total[k * rows : (k + 1) * rows, :].astype(low)


def add_halves(own, came, parts, order):
    rows, columns = own.shape
    block = max(b for b in (128, 256, 512, 640) if columns % b == 0)
    spec = pl.BlockSpec((rows, block), lambda j: (0, j))
    out = pl.BlockSpec((rows // parts, block), lambda j: (0, j))
    return call(
        halves_body,
        (columns // block,),
        [spec, spec],
        [out] * parts,
        [jax.ShapeDtypeStruct((rows // parts, columns), low)] * parts,
    )(own, came, order)


def parts_body(count, *refs):
    part_refs, out_refs = refs[:count], refs[count:]
    total = functools.reduce(jnp.add, [ref[...].astype(wide) for ref in part_refs])
    rows = out_refs[0].shape[0]
    for k, out_ref in enumerate(out_refs):
        out_ref[...] = total[k * rows : (k + 1) * rows, :].astype(out_ref.dtype)


def add_parts(parts, cuts, order):
    rows, columns = parts[0].shape
    block = max(b for b in (128, 256, 512, 640) if columns % b == 0)
    spec = pl.BlockSpec((rows, block), lambda j: (0, j))
    out = pl.BlockSpec((rows // cuts, block), lambda j: (0, j))
    shape = (rows // cuts, columns)
    return call(
        functools.partial(parts_body, len(parts)),
        (columns // block,),
        [spec] * len(parts),
        [out] * cuts,
        [jax.ShapeDtypeStruct(shape, wide)] + [jax.ShapeDtypeStruct(shape, low)] * (cuts - 1),
    )(*parts, order)


class OwnerSum:
    def __init__(self, own, other, owners, contexts):
        self.own = own
        self.came = swap(other, "dp", 1)
        self.owners, self.contexts = owners, contexts

    def spread_experts(self, *others):
        if self.own.shape[0] // self.owners // self.contexts % 16 == 0:
            both = add_halves(self.own, self.came, self.owners, token(*others))
        else:
            came = after(self.came, *others)
            total = (self.own.astype(wide) + came.astype(wide)).astype(low)
            both = list(total.reshape(self.owners, -1, total.shape[1]))
        self.parts = [both[0]] + [swap(both[k], "expert", k) for k in range(1, len(both))]
        return both

    def spread_contexts(self, *others):
        if self.parts[0].shape[0] // self.contexts % 16 == 0:
            total = add_parts(self.parts, self.contexts, token(*others))
        else:
            parts = all_after(self.parts, *others)
            total = functools.reduce(jnp.add, [part.astype(wide) for part in parts])
            total = total.reshape(self.contexts, -1, total.shape[1])
            total = [total[0]] + [part.astype(low) for part in total[1:]]
        self.parts = [total[0]] + [swap(part, "context", k) for k, part in enumerate(total) if k]
        return total[1:]


def turn(vals, cosine, sine):
    return vals * cosine + pltpu.roll(vals, LANES // 2, 1) * sine


def project_body(count, rows_ref, scale_ref, cos_ref, sin_ref, *refs):
    weight_refs, (query_ref, kv_ref, weight_ref) = refs[:count], refs[count:]
    step = pl.program_id(0)
    depth = weight_refs[0].shape[0]
    for k in range(count):
        weight_ref[k * depth : (k + 1) * depth, :] = weight_refs[k][...]
    total = dot_nn(rows_ref[...], weight_ref[...]) * scale_ref[...]
    block = total.shape[1]
    query_steps = QUERY_WIDTH // block
    cosine, sine = cos_ref[...], sin_ref[...]
    groups = [total[:, i * LANES : (i + 1) * LANES] for i in range(block // LANES)]

    @pl.when(step < query_steps)
    def _():
        for i, group in enumerate(groups):
            turned = turn(group, cosine, sine) * HEAD_DIM**-0.5
            query_ref[:, i * LANES : (i + 1) * LANES] = turned.astype(low)

    @pl.when(step >= query_steps)
    def _():
        for i, group in enumerate(groups):
            kept = turn(group, cosine, sine) if i % 2 == 0 else group
            kv_ref[:, i * LANES : (i + 1) * LANES] = kept.astype(low)


def project(rows, scale, cosine, sine, weights, order):
    tokens, width = rows.shape
    columns = QUERY_WIDTH + 2 * KV_WIDTH
    block = 512
    query_steps = QUERY_WIDTH // block
    depth = weights[0].shape[0]
    whole = lambda shape: pl.BlockSpec(shape, lambda j: (0, 0))
    return call(
        functools.partial(project_body, len(weights)),
        (columns // block,),
        [whole((tokens, width)), whole((tokens, 1)), whole((tokens, LANES)), whole((tokens, LANES))]
        + [pl.BlockSpec((depth, block), lambda j: (0, j))] * len(weights),
        [
            pl.BlockSpec((tokens, block), lambda j: (0, jnp.minimum(j, query_steps - 1))),
            pl.BlockSpec((tokens, block), lambda j: (0, jnp.maximum(j - query_steps, 0))),
        ],
        [
            jax.ShapeDtypeStruct((tokens, QUERY_WIDTH), low),
            jax.ShapeDtypeStruct((tokens, 2 * KV_WIDTH), low),
        ],
        scratch=[pltpu.VMEM((width, block), low)],
    )(rows, scale, cosine, sine, *weights, order)


def lane_of(shape, axis, which):
    place = lax.broadcasted_iota(jnp.int32, shape, axis)
    return ((place // (HEAD_DIM // 2)) % 2) == which


def stack_heads(block, which):
    keep = lane_of((block.shape[0], LANES), 1, which)
    return jnp.concatenate(
        [
            jnp.where(keep, block[:, g * LANES : (g + 1) * LANES], jnp.zeros((), block.dtype))
            for g in range(GROUPS)
        ],
        axis=0,
    )


def allowed_pairs(key_pos, query_pos):
    seen = key_pos <= query_pos
    return jnp.concatenate([seen] * GROUPS, axis=1)


def turned_block(block):
    return block.astype(wide).T.astype(low)


def attend_body(count, query_ref, key_pos_ref, query_pos_ref, *refs):
    kv_refs, (out_ref, out_low_ref, log_ref) = refs[:count], refs[count:]
    tokens = query_ref.shape[0]
    seen = allowed_pairs(key_pos_ref[...], query_pos_ref[...])
    keys = jnp.concatenate([ref[:, :LANES] for ref in kv_refs], axis=0)
    values = jnp.concatenate([turned_block(ref[:, LANES:]) for ref in kv_refs], axis=1)
    outs = []
    for which in range(2):
        query = stack_heads(query_ref[...], which)
        scores = jnp.where(seen, dot_nt(keys, query), masked_score)
        peak = jnp.max(scores, axis=0, keepdims=True)
        weight = jnp.exp(scores - peak)
        total = jnp.sum(weight, axis=0, keepdims=True)
        outs.append(dot_nn(values, weight.astype(low)) / total)
        log_ref[0, which : which + 1, :] = peak + jnp.log(total)
    first = lane_of(outs[0].shape, 0, 0)
    both = jnp.where(first, outs[0], outs[1]).T
    for g in range(GROUPS):
        piece = both[g * tokens : (g + 1) * tokens, :]
        out_ref[:, g * LANES : (g + 1) * LANES] = piece
        out_low_ref[:, g * LANES : (g + 1) * LANES] = piece.astype(low)


def attend(query, key_pos, query_pos, kv_parts, order):
    tokens = query.shape[0]
    count = len(kv_parts)
    seq_len = tokens * count
    pairs = pl.BlockSpec((tokens, PAIR_WIDTH), lambda p: (0, p))
    return call(
        functools.partial(attend_body, count),
        (PAIRS,),
        [
            pairs,
            pl.BlockSpec((seq_len, 1), lambda p: (0, 0)),
            pl.BlockSpec((1, tokens), lambda p: (0, 0)),
        ]
        + [pl.BlockSpec((tokens, 2 * LANES), lambda p: (0, p))] * count,
        [pairs, pairs, pl.BlockSpec((1, 2, GROUPS * tokens), lambda p: (p, 0, 0))],
        [
            jax.ShapeDtypeStruct((tokens, QUERY_WIDTH), wide),
            jax.ShapeDtypeStruct((tokens, QUERY_WIDTH), low),
            jax.ShapeDtypeStruct((PAIRS, 2, GROUPS * tokens), wide),
        ],
    )(query, key_pos, query_pos, *kv_parts, order)


def attend_back_body(count, own_ref, query_ref, grad_ref, out_ref, log_ref, key_pos_ref, query_pos_ref,
                     scale_ref, cos_ref, sin_ref, *refs):
    kv_refs, (grad_query_ref, grad_kv_ref) = refs[:count], refs[count:]
    tokens = query_ref.shape[0]
    grads = grad_ref[...]
    product = jnp.concatenate(
        [
            (grads[:, g * LANES : (g + 1) * LANES].astype(wide)
             * out_ref[:, g * LANES : (g + 1) * LANES]).T
            for g in range(GROUPS)
        ],
        axis=1,
    )
    first = lane_of(product.shape, 0, 0)
    delta = [
        jnp.sum(jnp.where(first, product, 0.0), axis=0, keepdims=True),
        jnp.sum(jnp.where(first, 0.0, product), axis=0, keepdims=True),
    ]
    seen = allowed_pairs(key_pos_ref[...], query_pos_ref[...])
    keys = jnp.concatenate([ref[:, :LANES] for ref in kv_refs], axis=0)
    values = jnp.concatenate([ref[:, LANES:] for ref in kv_refs], axis=0)
    keys_turned = jnp.concatenate([turned_block(ref[:, :LANES]) for ref in kv_refs], axis=1)
    grad_key, grad_value, grad_query = None, None, []
    for which in range(2):
        query = stack_heads(query_ref[...], which)
        head = stack_heads(grads, which)
        scores = jnp.where(seen, dot_nt(keys, query), masked_score)
        probs = jnp.exp(scores - log_ref[0, which : which + 1, :])
        grad_probs = dot_nt(values, head)
        grad_scores = (probs * (grad_probs - delta[which])).astype(low)
        part_value = dot_nn(probs.astype(low), head)
        part_key = dot_nn(grad_scores, query)
        grad_query.append(dot_nn(keys_turned, grad_scores))
        grad_value = part_value if grad_value is None else grad_value + part_value
        grad_key = part_key if grad_key is None else grad_key + part_key
    scale, cosine, sine = scale_ref[...], cos_ref[...], sin_ref[...]
    for k in range(count):
        rows = slice(k * tokens, (k + 1) * tokens)
        grad_kv_ref[own_ref[0] ^ k, :, :LANES] = grad_key[rows, :].astype(low)
        grad_kv_ref[own_ref[0] ^ k, :, LANES:] = grad_value[rows, :].astype(low)
    first = lane_of(grad_query[0].shape, 0, 0)
    both = (jnp.where(first, grad_query[0], grad_query[1]) * HEAD_DIM**-0.5).T
    for g in range(GROUPS):
        piece = both[g * tokens : (g + 1) * tokens, :]
        back = turn(piece, cosine, -sine) * scale
        grad_query_ref[:, g * LANES : (g + 1) * LANES] = back.astype(low)


def attend_back(
    own, query, grads, out, logs, key_pos, query_pos, scale, cosine, sine, kv_parts, order
):
    tokens = query.shape[0]
    count = len(kv_parts)
    seq_len = tokens * count
    pairs = pl.BlockSpec((tokens, PAIR_WIDTH), lambda p: (0, p))
    whole = lambda shape: pl.BlockSpec(shape, lambda p: (0, 0))
    part = pl.BlockSpec((tokens, 2 * LANES), lambda p: (0, p))
    return call(
        functools.partial(attend_back_body, count),
        (PAIRS,),
        [
            SCALAR,
            pairs,
            pairs,
            pairs,
            pl.BlockSpec((1, 2, GROUPS * tokens), lambda p: (p, 0, 0)),
            whole((seq_len, 1)),
            whole((1, tokens)),
            whole((tokens, 1)),
            whole((tokens, LANES)),
            whole((tokens, LANES)),
        ]
        + [part] * count,
        [pairs, pl.BlockSpec((count, tokens, 2 * LANES), lambda p: (0, 0, p))],
        [
            jax.ShapeDtypeStruct((tokens, QUERY_WIDTH), low),
            jax.ShapeDtypeStruct((count, tokens, 2 * KV_WIDTH), low),
        ],
    )(own, query, grads, out, logs, key_pos, query_pos, scale, cosine, sine, *kv_parts, order)


def hidden_body(count, first, own_ref, grads_ref, gate_ref, weight_ref, *refs):
    part_refs, (hidden_ref, back_ref, rows_ref) = refs[:count], refs[count:]
    expert, place = pl.program_id(0), pl.program_id(1)
    block = grads_ref.shape[0]
    tokens = part_refs[0].shape[0]

    @pl.when((expert == 0) & (place == 0))
    def _():
        for k, part_ref in enumerate(part_refs):
            start = pl.multiple_of((own_ref[0] ^ k) * tokens, tokens)
            rows_ref[pl.ds(start, tokens), :] = part_ref[...]

    rows = rows_ref[pl.ds(pl.multiple_of(place * block, block), block), :]
    grads = grads_ref[...]
    lane = lax.broadcasted_iota(jnp.int32, gate_ref.shape, 1) % (LANES // 2)
    weight = jnp.sum(
        jnp.where(lane == expert + first, gate_ref[...].astype(wide), 0.0), axis=1, keepdims=True
    )
    step = 256
    for h in range(0, FF, step):
        gate = dot_nn(rows, weight_ref[0, :, h : h + step])
        up = dot_nn(rows, weight_ref[0, :, FF + h : FF + h + step])
        grad_hidden = dot_nn(grads, weight_ref[0, :, 2 * FF + h : 2 * FF + h + step]) * weight
        sigmoid = 1.0 / (1.0 + jnp.exp(-gate))
        active = gate * sigmoid
        hidden_ref[0, :, h : h + step] = (active * up * weight).astype(low)
        slope = sigmoid + active * (1.0 - sigmoid)
        back_ref[0, :, h : h + step] = (grad_hidden * up * slope).astype(low)
        back_ref[0, :, FF + h : FF + h + step] = (grad_hidden * active).astype(low)


def expert_hidden(own, parts, grads, first, weights, order):
    tokens = grads.shape[0]
    width = parts[0].shape[1]
    experts = weights.shape[0]
    block = min(tokens, 1024)
    part_rows = parts[0].shape[0]
    return call(
        functools.partial(hidden_body, len(parts), first),
        (experts, tokens // block),
        [
            SCALAR,
            pl.BlockSpec((block, width), lambda e, t: (t, 0)),
            pl.BlockSpec((block, LANES), lambda e, t: (t, width // LANES)),
            pl.BlockSpec((1, width, 3 * FF), lambda e, t: (e, 0, 0)),
        ]
        + [
            pl.BlockSpec((part_rows, width), lambda e, t: (0, 0), pipeline_mode=pl.Buffered(1))
        ]
        * len(parts),
        [
            pl.BlockSpec((1, block, FF), lambda e, t: (e, t, 0)),
            pl.BlockSpec((1, block, 2 * FF), lambda e, t: (e, t, 0)),
        ],
        [
            jax.ShapeDtypeStruct((experts, tokens, FF), low),
            jax.ShapeDtypeStruct((experts, tokens, 2 * FF), low),
        ],
        scratch=[pltpu.VMEM((tokens, width), low)],
    )(own, grads, grads, weights, *parts, order)


def turn_body(count, slices, own_ref, place_ref, *refs):
    part_refs, (out_ref, placed_ref) = refs[:count], refs[count:]
    width, tokens = out_ref.shape[0], part_refs[0].shape[0]
    size = width // slices
    for k, part_ref in enumerate(part_refs):
        turned = turned_block(part_ref[...])
        column = pl.multiple_of((own_ref[0] ^ k) * tokens, tokens)
        out_ref[:, pl.ds(column, tokens)] = turned
        for i in range(slices):
            start = pl.multiple_of(place_ref[i] * size, size)
            placed_ref[pl.ds(start, size), pl.ds(column, tokens)] = turned[i * size : (i + 1) * size, :]


def turn_rows(own, place, parts, tokens, width, count, order):
    specs = [
        pl.BlockSpec((tokens, width), (lambda i, k=k: (k, 0)) if len(parts) == 1 else (lambda i: (0, 0)))
        for k in range(count)
    ]
    out = pl.BlockSpec((width, count * tokens), lambda i: (0, 0), pipeline_mode=pl.Buffered(1))
    return call(
        functools.partial(turn_body, count, place.shape[0]),
        (1,),
        [SCALAR, SCALAR, *specs],
        [out, out],
        [jax.ShapeDtypeStruct((width, count * tokens), low)] * 2,
    )(own, place, *(parts * count if len(parts) == 1 else parts), order)


def weight_grad_body(rows_ref, grads_ref, back_ref, hidden_ref, *out_refs):
    from_rows = dot_nn(rows_ref[...], back_ref[0]).astype(low)
    from_grads = dot_nn(grads_ref[...], hidden_ref[0]).astype(low)
    for half, out_ref in enumerate(out_refs):

        @pl.when((len(out_refs) == 1) | (pl.program_id(1) == half))
        def _():
            out_ref[0, :, : 2 * FF] = from_rows
            out_ref[0, :, 2 * FF :] = from_grads


def expert_weight_grads(rows_turned, grads_turned, hidden, back, halves, order):
    width, tokens = rows_turned.shape
    experts = back.shape[0]
    block = width // 2
    if halves:
        out_specs = [pl.BlockSpec((1, block, 3 * FF), lambda e, m: (e, 0, 0))] * 2
        out_shape = [jax.ShapeDtypeStruct((experts, block, 3 * FF), low)] * 2
    else:
        out_specs = [pl.BlockSpec((1, block, 3 * FF), lambda e, m: (e, m, 0))]
        out_shape = [jax.ShapeDtypeStruct((experts, width, 3 * FF), low)]
    return call(
        weight_grad_body,
        (experts, 2),
        [
            pl.BlockSpec((block, tokens), lambda e, m: (m, 0)),
            pl.BlockSpec((block, tokens), lambda e, m: (m, 0)),
            pl.BlockSpec((1, tokens, 2 * FF), lambda e, m: (e, 0, 0)),
            pl.BlockSpec((1, tokens, FF), lambda e, m: (e, 0, 0)),
        ],
        out_specs,
        out_shape,
    )(rows_turned, grads_turned, back, hidden, order)


def slices_body(plan, *refs):
    count = max(index for terms in plan for index, _ in terms) + 1
    arrays, outs = refs[:count], refs[count:]
    for terms, out_ref in zip(plan, outs):
        size = out_ref.shape[1]
        out_ref[0] = functools.reduce(
            jnp.add, [arrays[i][0, start : start + size, :].astype(wide) for i, start in terms]
        ).astype(low)


def add_slices(arrays, plan, sizes, order):
    experts, _, columns = arrays[0].shape
    spec = lambda rows: pl.BlockSpec((1, rows, columns), lambda e: (e, 0, 0))
    return call(
        functools.partial(slices_body, plan),
        (experts,),
        [spec(array.shape[1]) for array in arrays],
        [spec(size) for size in sizes],
        [jax.ShapeDtypeStruct((experts, size, columns), low) for size in sizes],
    )(*arrays, order)


class LineSum:
    def __init__(self, own, other):
        self.own = own
        self.came = swap(other, "dp", 1)
        self.size = own.shape[1] // 4

    def inward(self, *others):
        size = self.size
        self.first, self.last = add_slices(
            [self.own, self.came],
            [[(0, 0), (1, 0)], [(0, 3 * size), (1, 3 * size)]],
            [3 * size, size],
            token(*others),
        )
        self.from_end = lax.ppermute(self.first, "context", [(0, 1), (3, 2)])
        return self.last

    def across(self, *others):
        size = self.size
        plan = [[(0, 0), (1, 0)], [(0, size), (1, size)]]
        self.kept, sent = add_slices(
            [self.first, self.from_end], plan, [size, 2 * size], token(*others)
        )
        self.from_inner = lax.ppermute(sent, "context", [(1, 2), (2, 1)])
        return sent

    def outward(self, *others):
        size = self.size
        self.kept, sent = add_slices(
            [self.kept, self.last, self.from_inner],
            [[(0, 0), (2, 0)], [(1, 0), (2, size)]],
            [size, size],
            token(*others),
        )
        self.to_end = lax.ppermute(sent, "context", [(1, 0), (2, 3)])
        return sent

    def finish(self, *others):
        return [self.kept, self.last, self.to_end]


def combine_body(sizes, own_ref, *refs):
    count = len(sizes)
    part_refs, weight_refs = refs[:count], refs[count : 2 * count]
    out_refs, total_ref = refs[2 * count : -1], refs[-1]
    step = pl.program_id(0)

    @pl.when(step == 0)
    def _():
        total_ref[...] = jnp.zeros_like(total_ref)

    start = 0
    for part_ref, weight_ref, size in zip(part_refs, weight_refs, sizes):

        @pl.when((step >= start) & (step < start + size))
        def _():
            total_ref[...] += dot_nt(part_ref[0], weight_ref[0])

        start += size

    @pl.when(step == start - 1)
    def _():
        tokens = out_refs[0].shape[0]
        for k, out_ref in enumerate(out_refs):
            place = pl.multiple_of((own_ref[0] ^ k) * tokens, tokens) if len(out_refs) > 1 else 0
            out_ref[...] = total_ref[pl.ds(place, tokens), :].astype(low)


def combine(own, owners, parts, weights, column, order):
    tokens, depth = parts[0].shape[1:]
    width = weights[0].shape[1]
    sizes = [w.shape[0] for w in weights]
    starts = [sum(sizes[:i]) for i in range(len(sizes))]
    place = lambda e, start, size: jnp.clip(e - start, 0, size - 1)
    part_specs = [
        pl.BlockSpec((1, tokens, depth), lambda e, s=s, n=n: (place(e, s, n), 0, 0))
        for s, n in zip(starts, sizes)
    ]
    weight_specs = [
        pl.BlockSpec((1, width, depth), lambda e, s=s, n=n: (place(e, s, n), 0, column))
        for s, n in zip(starts, sizes)
    ]
    return call(
        functools.partial(combine_body, sizes),
        (sum(sizes),),
        [SCALAR] + part_specs + weight_specs,
        [pl.BlockSpec((tokens // owners, width), lambda e: (0, 0))] * owners,
        [jax.ShapeDtypeStruct((tokens // owners, width), low)] * owners,
        scratch=[pltpu.VMEM((tokens, width), wide)],
    )(own, *parts, *weights, order)


def norm_back_body(count, scale_ref, gain_ref, middle_ref, cotangent_ref, weight_ref, *refs):
    part_refs = refs[:count]
    middle_grad_ref, turned_ref, attended_ref, gain_grad_ref, proj_ref = refs[count:]

    @pl.when(pl.program_id(0) == 0)
    def _():
        grad = functools.reduce(jnp.add, [ref[...].astype(wide) for ref in part_refs])
        scale = scale_ref[...]
        unit = middle_ref[...] * scale
        gain = jnp.sum((grad * unit).T, axis=1, keepdims=True)
        gain_grad_ref[...] = jnp.broadcast_to(gain, gain_grad_ref.shape).astype(low)
        grad = grad * gain_ref[...]
        mean = jnp.mean(grad * unit, axis=1, keepdims=True)
        grad = cotangent_ref[...].astype(wide) + scale * (grad - unit * mean)
        middle_grad_ref[...] = grad
        proj_ref[...] = grad.astype(low)
        turned_ref[...] = grad.T.astype(low)

    attended_ref[...] = dot_nn(proj_ref[...], weight_ref[...]).astype(low)


def norm_back_two(parts, middle, scale, gain, cotangent, output_pack, order):
    tokens, width = middle.shape
    block = 512
    whole = lambda shape: pl.BlockSpec(shape, lambda j: (0, 0))
    return call(
        functools.partial(norm_back_body, len(parts)),
        (QUERY_WIDTH // block,),
        [
            whole((tokens, 1)),
            whole((1, width)),
            whole((tokens, width)),
            whole((tokens, width)),
            pl.BlockSpec((width, block), lambda j: (0, j)),
        ]
        + [whole((tokens, width))] * len(parts),
        [
            whole((tokens, width)),
            whole((width, tokens)),
            pl.BlockSpec((tokens, block), lambda j: (0, j)),
            whole((width, LANES)),
        ],
        [
            jax.ShapeDtypeStruct((tokens, width), wide),
            jax.ShapeDtypeStruct((width, tokens), low),
            jax.ShapeDtypeStruct((tokens, QUERY_WIDTH), low),
            jax.ShapeDtypeStruct((width, LANES), low),
        ],
        scratch=[pltpu.VMEM((tokens, width), low)],
    )(scale, gain, middle, cotangent, output_pack, *parts, order)


def outer_body(rows, first, place_ref, input_ref, proj_ref, gain_ref, query_ref, attended_ref,
               out_ref, picked_ref):
    out_ref[:, :QUERY_WIDTH] = dot_nn(input_ref[...], query_ref[...]).astype(low)
    if rows:
        for i in range(out_ref.shape[0] // rows):
            start = pl.multiple_of(place_ref[first + i] * rows, rows)
            part = slice(i * rows, (i + 1) * rows)
            picked_ref[part, :] = proj_ref[pl.ds(start, rows), :]
            out_ref[part, 2 * QUERY_WIDTH :] = gain_ref[pl.ds(start, rows), :]
    else:
        picked_ref[...] = proj_ref[...]
        out_ref[:, 2 * QUERY_WIDTH :] = gain_ref[...]
    out_ref[:, QUERY_WIDTH : 2 * QUERY_WIDTH] = dot_nn(picked_ref[...], attended_ref[...]).astype(low)


def outer_grads(half, cores, place, input_turned, proj_turned, gain_turned, grad_query, attended, order):
    width, tokens = input_turned.shape
    rows = width // cores
    slice_rows = width // place.shape[0]
    part = lambda columns: pl.BlockSpec((rows, columns), lambda i: (half, 0))
    inside = slice_rows % 16 == 0
    every = lambda columns: pl.BlockSpec((width, columns), lambda i: (0, 0))
    if not inside:
        pick = lambda array: jnp.take(
            array.reshape(place.shape[0], slice_rows, -1), place, axis=0, mode="clip"
        ).reshape(array.shape)
        proj_turned, gain_turned = pick(proj_turned), pick(gain_turned)
        every = part
    whole = pl.BlockSpec((tokens, QUERY_WIDTH), lambda i: (0, 0))
    columns = 2 * QUERY_WIDTH + LANES
    return call(
        functools.partial(outer_body, slice_rows if inside else 0, half * (place.shape[0] // cores)),
        (1,),
        [SCALAR, part(tokens), every(tokens), every(LANES), whole, whole],
        pl.BlockSpec((rows, columns), lambda i: (0, 0)),
        jax.ShapeDtypeStruct((rows, columns), low),
        scratch=[pltpu.VMEM((rows, tokens), low)],
    )(place, input_turned, proj_turned, gain_turned, grad_query, attended, order)


def kv_body(parts_ref, scale_ref, cos_ref, sin_ref, input_ref, grad_ref, *out_refs):
    total = jnp.sum(parts_ref[...].astype(wide), axis=0)
    cosine, sine, scale = cos_ref[...], sin_ref[...], scale_ref[...]
    for i in range(2 * PAIRS):
        group = total[:, i * LANES : (i + 1) * LANES]
        group = turn(group, cosine, -sine) if i % 2 == 0 else group
        grad_ref[:, i * LANES : (i + 1) * LANES] = (group * scale).astype(low)
    grads = grad_ref[...]
    rows = out_refs[0].shape[0]
    for k, out_ref in enumerate(out_refs):
        out_ref[...] = dot_nn(input_ref[k * rows : (k + 1) * rows, :], grads).astype(low)


def kv_grads(cores, parts, scale, cosine, sine, input_turned, order):
    tokens, columns = parts.shape[1:]
    width = input_turned.shape[0]
    shapes = [(tokens, columns)] + [(width // cores, columns)] * cores
    whole = lambda shape: pl.BlockSpec(shape, lambda i: (0,) * len(shape))
    return call(
        kv_body,
        (1,),
        [
            whole(parts.shape),
            whole((tokens, 1)),
            whole((tokens, LANES)),
            whole((tokens, LANES)),
            whole((width, tokens)),
        ],
        [whole(shape) for shape in shapes],
        [jax.ShapeDtypeStruct(shape, low) for shape in shapes],
    )(parts, scale, cosine, sine, input_turned, order)


def input_body(count, rows, place_ref, query_ref, kv_ref, scale_ref, input_ref, middle_ref, *refs):
    weight_refs, (out_ref, turned_ref) = refs[:count], refs[count:]
    weights = jnp.concatenate([ref[...] for ref in weight_refs], axis=0)
    part = dot_nt(weights[:, :QUERY_WIDTH], query_ref[...])
    part += dot_nt(weights[:, QUERY_WIDTH:], kv_ref[...])
    for i in range(part.shape[0] // rows):
        start = pl.multiple_of(place_ref[i] * rows, rows)
        turned_ref[pl.ds(start, rows), :] = part[i * rows : (i + 1) * rows, :]
    grad = turned_ref[...].T
    unit = input_ref[...].astype(wide) * scale_ref[...]
    mean = jnp.mean(grad * unit, axis=1, keepdims=True)
    out_ref[...] = (middle_ref[...] + grad - unit * mean).astype(low)


def input_grads(place, grad_query, grad_kv, scale, rows, grad_middle, weights, order):
    tokens, width = rows.shape
    whole = lambda array: pl.BlockSpec(array.shape, lambda i: (0, 0))
    operands = [grad_query, grad_kv, scale, rows, grad_middle, *weights]
    return call(
        functools.partial(input_body, len(weights), width // place.shape[0]),
        (1,),
        [SCALAR] + [whole(operand) for operand in operands],
        pl.BlockSpec((tokens, width), lambda i: (0, 0)),
        jax.ShapeDtypeStruct((tokens, width), low),
        scratch=[pltpu.VMEM((width, tokens), wide)],
    )(place, *operands, order)


def adam_body(count, held, inner_ref, *refs):
    grads, refs = [ref[0].astype(wide) for ref in refs[:count]], refs[count:]
    expand, contract, refs = refs[:3], refs[3:6], refs[6 + held :]
    if count == 1:
        grads = grads[0]
    else:
        grads = jnp.where(inner_ref[0] == 1, grads[0], grads[1] + grads[2])
    split = expand[0].shape[2]
    for arrays, grad, rate, out_refs in (
        (expand, grads[:, :split], rate_expand, refs[:3]),
        (contract, grads[:, split:], rate_contract, refs[3:]),
    ):
        results = adamw(*[array[0] for array in arrays], grad, rate, decay_rate)
        for out_ref, result in zip(out_refs, results):
            out_ref[0] = result


def adam_experts(first, inner, grads, arrays, held, order):
    count = grads[0].shape[0]
    held = held or []
    block = lambda array: pl.BlockSpec((1, *array.shape[1:]), lambda e: (first + e, 0, 0))
    return call(
        functools.partial(adam_body, len(grads), len(held)),
        (count,),
        [SCALAR]
        + [pl.BlockSpec((1, *grad.shape[1:]), lambda e: (e, 0, 0)) for grad in grads]
        + [block(array) for array in arrays]
        + [pl.BlockSpec(memory_space=pl.ANY)] * len(held),
        [block(array) for array in arrays],
        [jax.ShapeDtypeStruct(array.shape, wide) for array in arrays],
        aliases={1 + len(grads) + len(arrays) + i: i for i in range(len(held))},
    )(inner, *grads, *arrays, *held, order)


def adam_joined_body(count, query_mat_ref, key_mat_ref, gain_ref, *refs):
    grads, kv = [
        functools.reduce(jnp.add, [ref[...].astype(wide) for ref in part])
        for part in (refs[:count], refs[count : 2 * count])
    ]
    refs = refs[2 * count :]
    joined, output, gains, outs = refs[:3], refs[3:6], refs[6:9], refs[9:]
    back = lambda grad, mat: lax.dot_general(
        grad, mat, (((1,), (1,)), ((), ())), precision=lax.Precision.HIGHEST, preferred_element_type=wide
    )
    query_mat, key_mat = query_mat_ref[...], key_mat_ref[...]
    pairs = lambda start: [
        back(grads[:, start + p * PAIR_WIDTH : start + (p + 1) * PAIR_WIDTH], query_mat)
        for p in range(PAIRS)
    ]
    keys = [back(kv[:, 2 * p * LANES : (2 * p + 1) * LANES], key_mat) for p in range(PAIRS)]
    values = [back(kv[:, (2 * p + 1) * LANES : (2 * p + 2) * LANES], key_mat) for p in range(PAIRS)]
    unit_grad = jnp.concatenate([*pairs(0), *keys, *values], axis=1)
    low_weight = joined[0][...].astype(low).astype(wide)
    gain_one = jnp.sum(low_weight * unit_grad, axis=1, keepdims=True)
    gain_two = grads[:, 2 * QUERY_WIDTH : 2 * QUERY_WIDTH + 1]
    output_grad = jnp.concatenate(pairs(QUERY_WIDTH), axis=1)
    joined_grad = gain_ref[...] * unit_grad
    gains_grad = jnp.concatenate([gain_one, gain_two], axis=1)
    for arrays, grad, rate, decay, out_refs in (
        (joined, joined_grad, rate_joined, decay_rate, outs[:3]),
        (output, output_grad, rate_output, decay_rate, outs[3:6]),
        (gains, gains_grad, rate_gains, 0.0, outs[6:]),
    ):
        results = adamw(*[array[...] for array in arrays], grad, rate, decay)
        for out_ref, result in zip(out_refs, results):
            out_ref[...] = result


def adam_joined(gain, query_parts, kv_parts, arrays, order):
    query_mat, key_mat = order_matrix(GROUPS).astype(wide), order_matrix(1).astype(wide)
    operands = [query_mat, key_mat, gain, *query_parts, *kv_parts, *arrays]
    whole = lambda array: pl.BlockSpec(array.shape, lambda i: (0, 0))
    return call(
        functools.partial(adam_joined_body, len(query_parts)),
        (1,),
        [whole(operand) for operand in operands],
        [whole(array) for array in arrays],
        [jax.ShapeDtypeStruct(array.shape, wide) for array in arrays],
    )(*operands, order)


def body(
    layer_input,
    cotangent,
    block_order,
    routes,
    route_gates,
    joined_weight,
    joined_first,
    joined_second,
    output_weight,
    output_first,
    output_second,
    norm_gains,
    gains_first,
    gains_second,
    expand_weight,
    expand_first,
    expand_second,
    contract_weight,
    contract_first,
    contract_second,
):
    experts_dev = expand_weight.shape[0]
    owners = lax.axis_size("expert")
    contexts = lax.axis_size("context")
    cores = lax.axis_size("dp")
    experts = experts_dev * owners
    tokens = layer_input.shape[1]
    width = layer_input.shape[2]
    half_block = tokens // 2
    slice_rows = joined_weight.shape[0]
    own_expert = lax.axis_index("expert")
    own_context = lax.axis_index("context")
    own_core = lax.axis_index("dp")

    gain_rows = norm_gains.astype(low).astype(wide).T
    joined_low = joined_weight.astype(low)
    joined_shard = reorder_columns((gain_rows[:, :1] * joined_low.astype(wide)).astype(low)).astype(low)
    query_mat = order_matrix(GROUPS)
    output_shard = jnp.einsum(
        "pod,on->dpn",
        output_weight.astype(low).reshape(PAIRS, PAIR_WIDTH, slice_rows),
        query_mat,
        preferred_element_type=wide,
    ).reshape(slice_rows, QUERY_WIDTH).astype(low)
    gain_column = jnp.broadcast_to(gain_rows[:, 1:].astype(low), (slice_rows, LANES))
    columns = joined_shard.shape[1]
    shard = jnp.concatenate([joined_shard, output_shard, gain_column], axis=1)

    on_line = contexts == 4 and cores == 2
    bounds = [0, 2, 4, experts_dev] if on_line else [0, 2, experts_dev]
    chunks = list(zip(bounds[:-1], bounds[1:]))
    expert_low = [
        jnp.concatenate(
            [
                expand_weight[a:b].astype(low),
                jnp.swapaxes(contract_weight[a:b].astype(low), 1, 2),
            ],
            axis=2,
        )
        for a, b in chunks
    ]
    line, *expert_low = lax.optimization_barrier(
        (jnp.concatenate(spread(shard, "context"), axis=0), *expert_low)
    )
    joined_mine = spread(line[:, :columns], "expert")
    gather_expert = lambda part: lax.all_gather(part, ("context", "dp"), axis=1, tiled=True)
    expert_full = [gather_expert(expert_low[0])]

    ar = lambda n: jnp.arange(n, dtype=jnp.int32)
    to_relative = (
        ((own_expert ^ ar(owners))[None, :, None] * contexts + (own_context ^ ar(contexts))[None, None, :])
        * cores
        + (own_core ^ ar(cores))[:, None, None]
    ).reshape(-1)
    to_absolute = (
        (own_core ^ ar(cores))[None, None, :] * owners + (own_expert ^ ar(owners))[:, None, None]
    ) * contexts + (own_context ^ ar(contexts))[None, :, None]
    to_absolute = to_absolute.reshape(-1)
    slices = owners * contexts * cores

    def pick_rows(rows, index):
        return jnp.take(
            rows.reshape(slices, slice_rows, -1), index, axis=0, mode="clip", unique_indices=True
        ).reshape(rows.shape)

    hits = routes[0][:, :, None] == ar(experts)[None, None, :]
    gate_table = jnp.sum(jnp.where(hits, route_gates[0][:, :, None], 0.0), axis=1)
    gate_table = gate_table.reshape(tokens, owners, experts_dev)
    high = lax.reduce_precision(gate_table, 8, 7)
    terms = jnp.stack([high, gate_table - high], axis=2)
    terms = jnp.pad(terms, ((0, 0), (0, 0), (0, 0), (0, LANES // 2 - experts_dev)))
    terms = terms.reshape(tokens, owners, LANES).transpose(1, 0, 2).astype(low)
    grads_sent = jnp.concatenate(
        [jnp.broadcast_to(cotangent, (owners, tokens, width)), terms], axis=2
    )
    own = own_expert.reshape(1)
    zero = jnp.zeros((1,), jnp.int32)
    inner = ((own_context == 1) | (own_context == 2)).astype(jnp.int32).reshape(1)
    if on_line:
        along = jnp.where(
            own_context < 2, jnp.array([3, 0, 1, 2], jnp.int32), jnp.array([2, 1, 0, 3], jnp.int32)
        )
        line_place = (along[:, None] + (own_core ^ ar(cores))[None, :] * contexts).reshape(-1)
    else:
        line_place = ar(contexts * cores)

    order = block_order[0]
    offsets = ar(half_block)

    def places_of(index):
        mine = lax.dynamic_slice_in_dim(order, 2 * index, 2)
        return (mine[:, None] * half_block + offsets[None, :]).reshape(-1)

    query_pos = places_of(own_context)
    key_pos = jnp.concatenate([places_of(own_context ^ k) for k in range(contexts)])
    half = HEAD_DIM // 2
    freq = jnp.exp(ar(half).astype(wide) * (2.0 / HEAD_DIM) * -math.log(10000.0))
    angle = query_pos.astype(wide)[:, None] * freq[None, :]
    cosine = jnp.tile(jnp.cos(angle), (1, 4))
    sine = jnp.sin(angle)
    sine = jnp.concatenate([-sine, -sine, sine, sine], axis=1)

    low_input = layer_input[0]
    resid = low_input.astype(wide)
    scale_one = lax.rsqrt(jnp.mean(resid * resid, axis=-1, keepdims=True) + norm_eps)
    unit_one = resid * scale_one
    input_turned = pick_rows(low_input.T, to_relative)
    input_relative = input_turned.T
    first, *others, grads_sent = lax.optimization_barrier(
        (*joined_mine, grads_sent, cosine, sine, scale_one, input_relative)
    )[: owners + 1]
    joined_mine = [first, *others]
    joined_parts = joined_mine + [swap(part, "dp", 1) for part in joined_mine]
    output_mine = share(after(line[:, columns:], *joined_mine), "expert")
    query, kv = project(input_relative, scale_one, cosine, sine, joined_parts, token())
    kv_parts = spread(kv, "context")
    output_mine = after(output_mine, kv)
    output_parts = [output_mine, swap(output_mine, "dp", 1)]
    out_grads = trade(after(grads_sent, output_mine), "expert").reshape(owners * tokens, -1)
    output_place = (
        (own_core ^ ar(cores))[None, None, :] * owners + ar(owners)[:, None, None]
    ) * contexts + (own_context ^ ar(contexts))[None, :, None]
    output_pack = pick_rows(
        jnp.concatenate([part.reshape(-1, output_mine.shape[-1]) for part in output_parts], axis=0),
        output_place.reshape(-1),
    )
    output_turned = output_pack[:, :QUERY_WIDTH]
    gain_two = output_pack[:, QUERY_WIDTH].astype(wide)[None, :]
    out_grads_turned = turn_rows(
        zero, line_place, [out_grads], tokens, width, owners, token(output_pack)
    )
    kv_parts = all_after(kv_parts, output_pack, *out_grads_turned)
    kv_parts, later = lax.optimization_barrier((kv_parts, expert_low[1:]))
    expert_full += [gather_expert(part) for part in later]
    attended_wide, attended, logs = attend(
        query, key_pos[:, None], query_pos[None, :], kv_parts, token()
    )
    middle = resid + dot_nt(attended, output_turned)
    scale_two = lax.rsqrt(jnp.mean(middle * middle, axis=-1, keepdims=True) + norm_eps)
    unit_two = middle * scale_two
    normed_two = (unit_two * gain_two).astype(low)

    row_parts = spread(normed_two, "expert")
    def grads_of(unit, on_line, *others):
        return expert_weight_grads(
            rows_turned[on_line], out_grads_turned[on_line], *unit, on_line, token(*others)
        )

    def to_owners(grads):
        return lax.psum_scatter(grads, ("context", "dp"), scatter_dimension=1, tiled=True)

    def to_tokens(parts):
        return [parts[0]] + [swap(parts[k], "expert", k) for k in range(1, owners)]

    def forward_unit(unit, *others):
        return expert_hidden(
            own, row_parts, out_grads, bounds[unit], expert_full[unit], token(*others)
        )

    def combined(column, *others):
        parts = [unit[1 - column // 2] for unit in units]
        return combine(own, owners, parts, expert_full, column, token(*others))

    units = [forward_unit(0)]
    rows_turned = turn_rows(
        own, line_place, row_parts, tokens, width, owners, token(units[0][0])
    )
    if on_line:
        line_sum = LineSum(*grads_of(units[0], True))
        units.append(forward_unit(1, line_sum.own))
        latest = line_sum.inward(units[1][0])
        second_grads = grads_of(units[1], False, latest)[0]
        second_sum = to_owners(second_grads)
        units.append(forward_unit(2, second_grads))
        grad_sent = combined(0)
        grad_parts = to_tokens(grad_sent)
        mixture_sent = combined(2, *grad_sent)
        last_grads = grads_of(units[2], False, *mixture_sent)[0]
    else:
        first_grads = grads_of(units[0], False)[0]
        second_sum = to_owners(first_grads)
        units.append(forward_unit(1, first_grads))
        grad_sent = combined(0)
        grad_parts = to_tokens(grad_sent)
        last_grads = grads_of(units[1], False, *grad_sent)[0]
        mixture_sent = combined(2, last_grads)
    *mixture_sent, last_grads, grad_parts = lax.optimization_barrier(
        (*mixture_sent, last_grads, grad_parts)
    )
    last_sum = to_owners(last_grads)
    mixture_parts = to_tokens(mixture_sent)
    latest = line_sum.across(grad_parts[1]) if on_line else last_grads

    grad_middle, proj_turned, grad_attended, gain_turned = norm_back_two(
        grad_parts, middle, scale_two, gain_two, cotangent[0], output_pack, token(latest)
    )
    grad_query, grad_kv = attend_back(
        own_context.reshape(1), query, grad_attended, attended_wide, logs, key_pos[:, None],
        query_pos[None, :], scale_one, cosine, sine, kv_parts, token(grad_attended),
    )
    grad_kv_parts = trade(grad_kv, "context")

    def outer(half, *others):
        return outer_grads(
            half, cores, to_relative, input_turned, proj_turned, gain_turned, grad_query, attended,
            token(*others),
        )

    latest = line_sum.outward(grad_query) if on_line else grad_query
    mixture = functools.reduce(
        jnp.add, [part.astype(wide) for part in all_after(mixture_parts, latest)]
    )
    output = (middle + mixture).astype(low)
    other = outer(1, output, second_sum)
    query_sum = OwnerSum(outer(0, other), other, owners, contexts)
    latest = query_sum.spread_experts(query_sum.own)
    latest = query_sum.spread_contexts(*latest)
    own_grad_kv, *kv_parts_sent = kv_grads(
        cores, grad_kv_parts, scale_one, cosine, sine, input_turned, token(*latest)
    )
    kv_sum = OwnerSum(*kv_parts_sent, owners, contexts)
    latest = kv_sum.spread_experts(own_grad_kv)
    if slice_rows % 16 == 0:
        grad_input = input_grads(
            to_relative, grad_query, own_grad_kv, scale_one, low_input, grad_middle, joined_parts,
            token(*latest),
        )
    else:
        grad_joined = jnp.concatenate([grad_query, own_grad_kv], axis=1)
        scaled_grad = jnp.concatenate([dot_nt(part, grad_joined) for part in joined_parts], axis=0)
        scaled_grad = pick_rows(scaled_grad, to_absolute).T
        grad_input = (
            grad_middle
            + scaled_grad
            - unit_one * jnp.mean(scaled_grad * unit_one, axis=-1, keepdims=True)
        ).astype(low)

    latest = kv_sum.spread_contexts(grad_input)
    contract_arrays = [contract_weight, contract_first, contract_second]
    arrays = [expand_weight, expand_first, expand_second]
    arrays += [jnp.swapaxes(array, 1, 2) for array in contract_arrays]
    expert_grads = [[second_sum], [last_sum]]
    if on_line:
        expert_grads.insert(0, line_sum.finish())
    expert_new = None
    for first, grads in zip(bounds, expert_grads):
        expert_new = adam_experts(first, inner, grads, arrays, expert_new, token(*latest))
    expand_new = expert_new[:3]
    contract_new = [jnp.swapaxes(array, 1, 2) for array in expert_new[3:]]
    turned = [output_weight, output_first, output_second, norm_gains, gains_first, gains_second]
    joined_new = adam_joined(
        gain_rows[:, :1],
        query_sum.parts,
        kv_sum.parts,
        [joined_weight, joined_first, joined_second] + [array.T for array in turned],
        token(expand_new[0]),
    )
    output_new = [array.T for array in joined_new[3:6]]
    gains_new = [array.T for array in joined_new[6:]]
    joined_new = joined_new[:3]
    return (
        output.reshape(1, tokens, width),
        grad_input.reshape(1, tokens, width),
        *joined_new,
        *output_new,
        *gains_new,
        *expand_new,
        *contract_new,
    )


def solution(mesh):
    rows = P(("expert", "dp"), "context", None)
    joined = P(("expert", "context", "dp"), None)
    column = P(None, ("expert", "context", "dp"))
    expand = P("expert", ("context", "dp"), None)
    contract = P("expert", None, ("context", "dp"))
    placed = (
        (rows, rows, P(("expert", "dp"), None), rows, rows)
        + (joined,) * 3
        + (column,) * 6
        + (expand,) * 3
        + (contract,) * 3
    )
    return jax.shard_map(
        body,
        mesh=mesh,
        in_specs=placed,
        out_specs=(rows, rows) + placed[5:],
        check_vma=False,
    )
```
